32 devices in a mesh: row: 8 (over z, y), col: 4 (over x, core).
Axes of the slice: x: 2, y: 2, z: 4, core: 2. Of those that a mesh axis runs over, the one named last changes fastest.
Arguments:
- rhs: float32 [6, 8, 4, 1, 64, 128], P(None, 'row', 'col'), may hold values from -6 to 6
- diag_inv: float32 [6, 8, 4, 1, 128, 128], P(None, 'row', 'col'), as said below
- blocks: float32 [5, 8, 4, 32, 128, 128], P(None, 'row', 'col'), may hold values from -0.125 to 0.125
- blk_target: int32 [5, 8, 4, 32], P(None, 'row', 'col'), may hold values from 0 to 3
- blk_source: int32 [5, 8, 4, 32], P(None, 'row', 'col'), may hold values from 0 to 7
- blk_count: int32 [5, 8, 4], P(None, 'row', 'col'), may hold values from 8 to 32, as said below
Outputs:
- forward_solution: float32 [6, 8, 4, 1, 64, 128], P(None, 'row', 'col')
- solution: float32 [6, 8, 4, 1, 64, 128], P(None, 'row', 'col')
The draws below stay inside these ranges and needn't reach their ends.
Inputs may be any that keep to these rules, and one draw needn't show every extreme that they name: `blk_count`: every level has a device whose 32 slots are all live; most devices have from a quarter to two thirds of 32 live slots. `diag_inv`: each diagonal-block inverse has diagonal entries between 0.7 and 1.4.
All inputs are finite; a program needn't handle non-finite values.
Results may differ from the reference program's by a relative error of at most 0.0003.
Values sent between devices are 32-bit elements; how exact they have to be, the bound alone decides.
No kernel may reach another device: no remote copies, remote signals or barrier semaphores. Data moves between devices by JAX's collectives and lax.ppermute only.
A program may use at most 64 MiB of HBM per device.

```python
import jax
import jax.numpy as jnp
from jax import lax

BLK = 128
NRHS = 64
LEV = 6
SPL = 1
NBLK = 32
N_ROW = 8
N_COL = 4


def draw_diag_inv(key, part):
    array_shape = (LEV, N_ROW, N_COL, SPL, BLK, BLK)
    key_diag = jax.random.fold_in(key, 11)
    key_off = jax.random.fold_in(key, 12)
    logs = jax.random.uniform(key_diag, (LEV, N_ROW, N_COL, SPL, BLK, 1), jnp.float32, jnp.log(0.7), jnp.log(1.4))
    off = jax.random.normal(key_off, array_shape, jnp.float32) * (0.25 / BLK ** 0.5)
    eye = jnp.arange(BLK, dtype=jnp.int32)[:, None] == jnp.arange(BLK, dtype=jnp.int32)[None, :]
    return jnp.where(eye, jnp.exp(logs), off).astype(jnp.float32)


def draw_blk_count(key, part):
    array_shape = (LEV - 1, N_ROW, N_COL)
    base = jax.random.randint(jax.random.fold_in(key, 21), array_shape, NBLK // 4, 2 * NBLK // 3 + 1)
    heavy = jax.random.randint(jax.random.fold_in(key, 22), array_shape, 0, 16) == 0
    chosen = jax.random.randint(jax.random.fold_in(key, 23), (LEV - 1, 1, 1), 0, N_ROW * N_COL)
    position = jnp.arange(N_ROW * N_COL, dtype=jnp.int32).reshape(1, N_ROW, N_COL)
    forced = position == chosen
    return jnp.where(heavy | forced, NBLK, base).astype(jnp.int32)


def set_ends(entries, rng, smallest, top_value):
    longest = entries.shape.index(max(entries.shape))
    spots = []
    for shift in (0, 1):
        where = [jax.random.randint(jax.random.fold_in(rng, axis), (), 0, length) for axis, length in enumerate(entries.shape)]
        where[longest] = (where[longest] + shift) % entries.shape[longest]
        spots.append(tuple(where))
    return entries.at[spots[0]].set(smallest).at[spots[1]].set(top_value)


def block_levels(key, dims, cuts, smallest, largest):
    loudness, own = 1.0, jax.random.fold_in(key, 6)
    for axis_at, parts in cuts:
        steps = jnp.exp(jax.random.uniform(jax.random.fold_in(own, axis_at), (parts,), jnp.float32, smallest / len(cuts), largest / len(cuts)))
        loudness = loudness * jnp.repeat(steps, dims[axis_at] // parts).reshape([-1 if axis == axis_at else 1 for axis in range(len(dims))])
    return loudness


def bell_draw(own_key, dims, deviation, most, split=(), kind=jnp.bfloat16):
    loudness = block_levels(own_key, dims, split, -0.22, 0.18) if split else 1.0
    array = jax.random.normal(own_key, dims, jnp.float32) * deviation * loudness
    return jnp.minimum(jnp.maximum(array, -most), most).astype(kind)


def setup_inputs(seed: int = 0) -> dict:
    streams_of = jax.random.split(jax.random.key(seed), 7)
    return {
        "rhs": bell_draw(streams_of[0], (LEV, N_ROW, N_COL, SPL, NRHS, BLK), 1.0, 6.0, ((1, 8), (2, 4)), jnp.float32),
        "diag_inv": draw_diag_inv(jax.random.fold_in(streams_of[6], 71), 0),
        "blocks": bell_draw(streams_of[2], (LEV - 1, N_ROW, N_COL, NBLK, BLK, BLK), (16 * BLK) ** -0.5, 0.125, ((1, 8), (2, 4)), jnp.float32),
        "blk_target": set_ends(jax.random.randint(streams_of[3], (LEV - 1, N_ROW, N_COL, NBLK), 0, N_COL * SPL), jax.random.fold_in(streams_of[3], 1), 0, (N_COL * SPL) - 1).astype(jnp.int32),
        "blk_source": set_ends(jax.random.randint(streams_of[4], (LEV - 1, N_ROW, N_COL, NBLK), 0, N_ROW * SPL), jax.random.fold_in(streams_of[4], 1), 0, (N_ROW * SPL) - 1).astype(jnp.int32),
        "blk_count": draw_blk_count(jax.random.fold_in(streams_of[6], 71), 0),
    }


HIGH_PRECISION = lax.Precision.HIGHEST


def apply_rows(values, inverse):
    return jnp.einsum("xysrb,xysbc->xysrc", values, inverse, precision=HIGH_PRECISION)


def apply_cols(values, inverse):
    return jnp.einsum("xysrc,xysbc->xysrb", values, inverse, precision=HIGH_PRECISION)


def reference(rhs, diag_inv, blocks, blk_target, blk_source, blk_count):
    forward = [apply_rows(rhs[0], diag_inv[0])]
    for level in range(1, LEV):
        previous = forward[-1]
        blocks_l = blocks[level - 1]
        target_l = blk_target[level - 1]
        source_l = blk_source[level - 1]
        count_l = blk_count[level - 1]

        def per_row(row):
            weight_matrix = lax.dynamic_index_in_dim(blocks_l, row, 0, keepdims=False)
            target = lax.dynamic_index_in_dim(target_l, row, 0, keepdims=False)
            source = lax.dynamic_index_in_dim(source_l, row, 0, keepdims=False)
            entry_count = lax.dynamic_index_in_dim(count_l, row, 0, keepdims=False)
            columns = jnp.arange(N_COL, dtype=jnp.int32)[:, None] * jnp.ones_like(source)
            selected_blocks = previous[source // SPL, columns, source % SPL]
            product = jnp.einsum("ckrb,ckbe->ckre", selected_blocks, weight_matrix, precision=HIGH_PRECISION)
            active_flags = jnp.arange(NBLK, dtype=jnp.int32)[None, :] < entry_count[:, None]
            routing_table = ((target[:, :, None] == jnp.arange(N_COL * SPL, dtype=jnp.int32)[None, None, :]) & active_flags[:, :, None]).astype(previous.dtype)
            summed = jnp.einsum("ckt,ckre->tre", routing_table, product, precision=HIGH_PRECISION)
            return summed.reshape(N_COL, SPL, NRHS, BLK)

        summed = lax.map(per_row, jnp.arange(N_ROW, dtype=jnp.int32))
        forward.append(apply_rows(rhs[level] - summed, diag_inv[level]))
    backward = [None] * LEV
    backward[LEV - 1] = apply_cols(forward[LEV - 1], diag_inv[LEV - 1])
    for level in range(LEV - 2, -1, -1):
        upper = backward[level + 1]
        blocks_l = blocks[level]
        target_l = blk_target[level]
        source_l = blk_source[level]
        count_l = blk_count[level]

        def per_col(col):
            weight_matrix = lax.dynamic_index_in_dim(blocks_l, col, 1, keepdims=False)
            target = lax.dynamic_index_in_dim(target_l, col, 1, keepdims=False)
            source = lax.dynamic_index_in_dim(source_l, col, 1, keepdims=False)
            entry_count = lax.dynamic_index_in_dim(count_l, col, 1, keepdims=False)
            rows = jnp.arange(N_ROW, dtype=jnp.int32)[:, None] * jnp.ones_like(target)
            selected_blocks = upper[rows, target // SPL, target % SPL]
            product = jnp.einsum("qkre,qkbe->qkrb", selected_blocks, weight_matrix, precision=HIGH_PRECISION)
            active_flags = jnp.arange(NBLK, dtype=jnp.int32)[None, :] < entry_count[:, None]
            routing_table = ((source[:, :, None] == jnp.arange(N_ROW * SPL, dtype=jnp.int32)[None, None, :]) & active_flags[:, :, None]).astype(upper.dtype)
            summed = jnp.einsum("qkt,qkrb->trb", routing_table, product, precision=HIGH_PRECISION)
            return summed.reshape(N_ROW, SPL, NRHS, BLK)

        summed = jnp.swapaxes(lax.map(per_col, jnp.arange(N_COL, dtype=jnp.int32)), 0, 1)
        backward[level] = apply_cols(forward[level] - summed, diag_inv[level])
    return jnp.stack(forward), jnp.stack(backward)
```

```python
import functools

import jax
import jax.numpy as jnp
from jax import lax
from jax.experimental import pallas as pl
from jax.experimental.pallas import tpu as pltpu
from jax.sharding import PartitionSpec as P

HIGH_PRECISION = lax.Precision.HIGHEST
MIB = 1024 * 1024
VMEM = pltpu.MemorySpace.VMEM
SMEM = pltpu.MemorySpace.SMEM


def halves(value):
    high = value.astype(jnp.bfloat16)
    low = (value - high.astype(jnp.float32)).astype(jnp.bfloat16)
    return high, low


def product(left, right, transposed):
    contract = (((1,), (1 if transposed else 0,)), ((), ()))
    dot = functools.partial(
        lax.dot_general, dimension_numbers=contract, preferred_element_type=jnp.float32
    )
    return dot(left[0], right[0]) + (dot(left[0], right[1]) + dot(left[1], right[0]))


def gather_blocks_kernel(
    n_col, level, target_ref, source_ref, count_ref, place_ref, blocks_ref, high_ref, low_ref, total
):
    block = blocks_ref.shape[-1]
    total[...] = jnp.zeros_like(total)

    def add(slot, carry):
        below = source_ref[level, slot] ^ place_ref[0]
        above = target_ref[level, slot] ^ place_ref[1]
        pair = below * n_col + above
        total[pair] += blocks_ref[0, slot]
        return carry

    lax.fori_loop(0, count_ref[level], add, 0)
    for pair in range(total.shape[0]):
        rows = pl.ds(pair // n_col * block, block)
        lanes = pl.ds(pair % n_col * block, block)
        high, low = halves(total[pair])
        high_ref[rows, lanes] = high
        low_ref[rows, lanes] = low


def gather_blocks(level, target, source, count, place, blocks, n_row, n_col):
    slot_count, block = blocks.shape[1], blocks.shape[2]
    shape = (n_row * block, n_col * block)
    scalars = pl.BlockSpec(memory_space=SMEM)
    whole = pl.BlockSpec(shape, lambda i: (0, 0))
    return pl.pallas_call(
        functools.partial(gather_blocks_kernel, n_col, level),
        grid=(1,),
        out_shape=[jax.ShapeDtypeStruct(shape, jnp.bfloat16)] * 2,
        in_specs=[scalars] * 4
        + [pl.BlockSpec((1, slot_count, block, block), lambda i: (level, 0, 0, 0))],
        out_specs=[whole, whole],
        scratch_shapes=[pltpu.VMEM((n_row * n_col, block, block), jnp.float32)],
        compiler_params=pltpu.CompilerParams(vmem_limit_bytes=16 * MIB),
        cost_estimate=pl.CostEstimate(
            flops=2 * shape[0] * shape[1], bytes_accessed=8 * shape[0] * shape[1], transcendentals=0
        ),
        name=f"gather_blocks_{level}",
    )(target, source, count, place, blocks)


def couple_kernel(transposed, n_in, high_ref, low_ref, *refs):
    ins, outs = refs[:n_in], refs[n_in:]
    block = ins[0].shape[-1]
    joined = jnp.concatenate([ref[...] for ref in ins], axis=1)
    result = product(halves(joined), (high_ref[...], low_ref[...]), transposed)
    for place, ref in enumerate(outs):
        ref[...] = result[:, place * block : (place + 1) * block]


def couple(segments, high, low, transposed):
    n_out = high.shape[0 if transposed else 1] // segments[0].shape[1]
    n_in = len(segments)
    rows, block = segments[0].shape
    whole = pl.BlockSpec(memory_space=VMEM)
    return pl.pallas_call(
        functools.partial(couple_kernel, transposed, n_in),
        out_shape=[jax.ShapeDtypeStruct((rows, block), jnp.float32)] * n_out,
        in_specs=[whole] * (n_in + 2),
        out_specs=[whole] * n_out,
        compiler_params=pltpu.CompilerParams(vmem_limit_bytes=16 * MIB),
        cost_estimate=pl.CostEstimate(
            flops=6 * rows * high.size, bytes_accessed=4 * high.size, transcendentals=0
        ),
        name="couple_up" if not transposed else "couple_down",
    )(high, low, *segments)


def solve_kernel(transposed, right_ref, inverse_ref, *refs):
    parts, out_ref = refs[:-1], refs[-1]
    value = right_ref[...].reshape(out_ref.shape)
    if parts:
        summed = parts[0][...]
        for part in parts[1:]:
            summed += part[...]
        value -= summed
    inverse = inverse_ref[...].reshape(inverse_ref.shape[-2:])
    out_ref[...] = product(halves(value), halves(inverse), transposed)


def solve(right, inverse, level, parts, transposed):
    rows, block = right.shape[-2:]
    at_level = lambda shape: pl.BlockSpec((1,) + shape, lambda i: (level, 0, 0))
    plain = pl.BlockSpec((rows, block), lambda i: (0, 0))
    return pl.pallas_call(
        functools.partial(solve_kernel, transposed),
        grid=(1,),
        out_shape=jax.ShapeDtypeStruct((rows, block), jnp.float32),
        in_specs=[
            at_level((rows, block)) if right.ndim == 3 else plain,
            at_level((block, block)),
        ]
        + [plain] * len(parts),
        out_specs=plain,
        compiler_params=pltpu.CompilerParams(vmem_limit_bytes=8 * MIB),
        cost_estimate=pl.CostEstimate(
            flops=6 * rows * block * block, bytes_accessed=4 * block * block, transcendentals=0
        ),
        name="solve_up" if not transposed else "solve_down",
    )(right, inverse, *parts)


def spread(segment, axis):
    size = lax.axis_size(axis)
    return [segment] + [
        lax.ppermute(segment, axis, [(i, i ^ d) for i in range(size)]) for d in range(1, size)
    ]


def deliver(parts, axis):
    size = lax.axis_size(axis)
    return [parts[0]] + [
        lax.ppermute(parts[d], axis, [(i, i ^ d) for i in range(size)]) for d in range(1, size)
    ]


def direct_shards(rhs, diag_inv, blocks, blk_target, blk_source, blk_count):
    levels = rhs.shape[0]
    n_row, n_col = lax.axis_size("row"), lax.axis_size("col")
    right = rhs.reshape((levels,) + rhs.shape[-2:])
    inverse = diag_inv.reshape((levels,) + diag_inv.shape[-2:])
    weights = blocks.reshape((levels - 1,) + blocks.shape[-3:])
    target = blk_target.reshape(levels - 1, -1)
    source = blk_source.reshape(levels - 1, -1)
    count = blk_count.reshape(levels - 1)
    place = jnp.stack([lax.axis_index("row"), lax.axis_index("col")]).astype(jnp.int32)
    coupling = [
        gather_blocks(level, target, source, count, place, weights, n_row, n_col)
        for level in range(levels - 1)
    ]
    forward = [solve(right, inverse, 0, [], False)]
    for level in range(1, levels):
        partial = couple(spread(forward[-1], "row"), *coupling[level - 1], False)
        forward.append(solve(right, inverse, level, deliver(partial, "col"), False))
    backward = [None] * levels
    backward[-1] = solve(forward[-1], inverse, levels - 1, [], True)
    for level in range(levels - 2, -1, -1):
        partial = couple(spread(backward[level + 1], "col"), *coupling[level], True)
        backward[level] = solve(forward[level], inverse, level, deliver(partial, "row"), True)
    return (
        jnp.stack(forward).reshape(rhs.shape),
        jnp.stack(backward).reshape(rhs.shape),
    )


def fold_for(index, piece):
    entry_count = piece.shape[0]
    onehot = (index[:, None] == jnp.arange(entry_count, dtype=jnp.int32)[None, :]).astype(
        jnp.float32
    )
    return jnp.dot(
        onehot,
        piece.reshape(entry_count, -1),
        precision=HIGH_PRECISION,
        preferred_element_type=jnp.float32,
    )


def route_sum(index, entry_count, block_products, width):
    slot_count = block_products.shape[0]
    active_flags = jnp.arange(slot_count, dtype=jnp.int32) < entry_count
    routing_table = (
        (index[None, :] == jnp.arange(width, dtype=jnp.int32)[:, None]) & active_flags[None, :]
    ).astype(jnp.float32)
    return jnp.dot(
        routing_table,
        block_products.reshape(slot_count, -1),
        precision=HIGH_PRECISION,
        preferred_element_type=jnp.float32,
    )


def forward_level(previous, weight_matrix, target, source, entry_count):
    slot_count = weight_matrix.shape[0]
    slots, rhs_column_count, block_ordering = previous.shape
    selected_blocks = fold_for(source, lax.all_gather(previous, "row", axis=0, tiled=True))
    block_products = jnp.einsum(
        "ado,aon->adn",
        selected_blocks.reshape(slot_count, rhs_column_count, block_ordering),
        weight_matrix,
        precision=HIGH_PRECISION,
    )
    ncol = lax.axis_size("col")
    buckets = route_sum(target, entry_count, block_products, ncol * slots).reshape(
        ncol, slots, rhs_column_count, block_ordering
    )
    own = lax.psum_scatter(buckets, "col", scatter_dimension=0, tiled=True)[0]
    return own


def backward_level(upper, weight_matrix, target, source, entry_count):
    slot_count = weight_matrix.shape[0]
    slots, rhs_column_count, block_ordering = upper.shape
    selected_blocks = fold_for(target, lax.all_gather(upper, "col", axis=0, tiled=True))
    block_products = jnp.einsum(
        "mlv,mtv->mlt",
        selected_blocks.reshape(slot_count, rhs_column_count, block_ordering),
        weight_matrix,
        precision=HIGH_PRECISION,
    )
    nrow = lax.axis_size("row")
    buckets = route_sum(source, entry_count, block_products, nrow * slots).reshape(
        nrow, slots, rhs_column_count, block_ordering
    )
    own = lax.psum_scatter(buckets, "row", scatter_dimension=0, tiled=True)[0]
    return own


def shards(rhs, diag_inv, blocks, blk_target, blk_source, blk_count):
    levels = rhs.shape[0]
    right = rhs[:, 0, 0]
    inverse = diag_inv[:, 0, 0]
    weight_matrix = blocks[:, 0, 0]
    targets = blk_target[:, 0, 0]
    sources = blk_source[:, 0, 0]
    counts = blk_count[:, 0, 0]
    forward = [jnp.einsum("srb,sbc->src", right[0], inverse[0], precision=HIGH_PRECISION)]
    for level in range(1, levels):
        own = forward_level(
            forward[-1],
            weight_matrix[level - 1],
            targets[level - 1],
            sources[level - 1],
            counts[level - 1],
        )
        forward.append(
            jnp.einsum("srb,sbc->src", right[level] - own, inverse[level], precision=HIGH_PRECISION)
        )
    backward = [None] * levels
    backward[levels - 1] = jnp.einsum(
        "src,sbc->srb", forward[levels - 1], inverse[levels - 1], precision=HIGH_PRECISION
    )
    for level in range(levels - 2, -1, -1):
        own = backward_level(
            backward[level + 1], weight_matrix[level], targets[level], sources[level], counts[level]
        )
        backward[level] = jnp.einsum(
            "src,sbc->srb", forward[level] - own, inverse[level], precision=HIGH_PRECISION
        )
    forward_out = jnp.stack(forward)[:, None, None]
    backward_out = jnp.stack(backward)[:, None, None]
    return (forward_out, backward_out)


def solution(mesh):
    placed = (
        P(None, "row", "col", None, None, None),
        P(None, "row", "col", None, None, None),
        P(None, "row", "col", None, None, None),
        P(None, "row", "col", None),
        P(None, "row", "col", None),
        P(None, "row", "col"),
    )
    n_row, n_col = mesh.shape["row"], mesh.shape["col"]

    def local(rhs, diag_inv, blocks, blk_target, blk_source, blk_count):
        sizes = (n_row, n_col)
        dense = n_row * n_col <= blocks.shape[3] and rhs.shape[3] == 1
        even = all(size & (size - 1) == 0 for size in sizes)
        run = direct_shards if dense and even else shards
        return run(rhs, diag_inv, blocks, blk_target, blk_source, blk_count)

    return jax.shard_map(
        local,
        mesh=mesh,
        in_specs=placed,
        out_specs=(
            P(None, "row", "col", None, None, None),
            P(None, "row", "col", None, None, None),
        ),
        check_vma=False,
    )
```

```python
import functools

import jax
import jax.numpy as jnp
from jax import lax
from jax.experimental import pallas as pl
from jax.experimental.pallas import tpu as pltpu
from jax.sharding import PartitionSpec as P

HIGH_PRECISION = lax.Precision.HIGHEST
MIB = 1024 * 1024
VMEM = pltpu.MemorySpace.VMEM
SMEM = pltpu.MemorySpace.SMEM


def halves(value):
    high = value.astype(jnp.bfloat16)
    low = (value - high.astype(jnp.float32)).astype(jnp.bfloat16)
    return high, low


def product(left, right, transposed):
    contract = (((1,), (1 if transposed else 0,)), ((), ()))
    dot = functools.partial(
        lax.dot_general, dimension_numbers=contract, preferred_element_type=jnp.float32
    )
    return dot(left[0], right[0]) + (dot(left[0], right[1]) + dot(left[1], right[0]))


def gather_blocks_kernel(
    n_col, level, target_ref, source_ref, count_ref, place_ref, blocks_ref, high_ref, low_ref, total
):
    block = blocks_ref.shape[-1]
    total[...] = jnp.zeros_like(total)

    def add(slot, carry):
        below = source_ref[level, slot]
        above = target_ref[level, slot] ^ place_ref[1]
        pair = below * n_col + above
        total[pair] += blocks_ref[0, slot]
        return carry

    lax.fori_loop(0, count_ref[level], add, 0)
    for pair in range(total.shape[0]):
        rows = pl.ds(pair // n_col * block, block)
        lanes = pl.ds(pair % n_col * block, block)
        high, low = halves(total[pair])
        high_ref[rows, lanes] = high
        low_ref[rows, lanes] = low


def gather_blocks(level, target, source, count, place, blocks, n_row, n_col):
    slot_count, block = blocks.shape[1], blocks.shape[2]
    shape = (n_row * block, n_col * block)
    scalars = pl.BlockSpec(memory_space=SMEM)
    whole = pl.BlockSpec(shape, lambda i: (0, 0))
    return pl.pallas_call(
        functools.partial(gather_blocks_kernel, n_col, level),
        grid=(1,),
        out_shape=[jax.ShapeDtypeStruct(shape, jnp.bfloat16)] * 2,
        in_specs=[scalars] * 4
        + [pl.BlockSpec((1, slot_count, block, block), lambda i: (level, 0, 0, 0))],
        out_specs=[whole, whole],
        scratch_shapes=[pltpu.VMEM((n_row * n_col, block, block), jnp.float32)],
        compiler_params=pltpu.CompilerParams(vmem_limit_bytes=16 * MIB),
        cost_estimate=pl.CostEstimate(
            flops=2 * shape[0] * shape[1], bytes_accessed=8 * shape[0] * shape[1], transcendentals=0
        ),
        name=f"gather_blocks_{level}",
    )(target, source, count, place, blocks)


def couple_kernel(transposed, n_in, high_ref, low_ref, *refs):
    ins, outs = refs[:n_in], refs[n_in:]
    block = ins[0].shape[-1]
    if transposed:
        segments = [ref[...] for ref in ins]
    else:
        segments = [ins[0][place] for place in range(ins[0].shape[0])]
    joined = jnp.concatenate(segments, axis=1)
    result = product(halves(joined), (high_ref[...], low_ref[...]), transposed)
    for place in range(result.shape[1] // block):
        piece = result[:, place * block : (place + 1) * block]
        if transposed:
            outs[0][place] = piece
        else:
            outs[place][...] = piece


def couple(segments, high, low, transposed):
    n_in = len(segments)
    rows, block = segments[0].shape[-2:]
    n_out = high.shape[0 if transposed else 1] // block
    segment = jax.ShapeDtypeStruct((rows, block), jnp.float32)
    stacked = jax.ShapeDtypeStruct((n_out, rows, block), jnp.float32)
    out_shape = [stacked] if transposed else [segment] * n_out
    whole = pl.BlockSpec(memory_space=VMEM)
    return pl.pallas_call(
        functools.partial(couple_kernel, transposed, n_in),
        out_shape=out_shape,
        in_specs=[whole] * (n_in + 2),
        out_specs=[whole] * len(out_shape),
        compiler_params=pltpu.CompilerParams(vmem_limit_bytes=16 * MIB),
        cost_estimate=pl.CostEstimate(
            flops=6 * rows * high.size, bytes_accessed=4 * high.size, transcendentals=0
        ),
        name="couple_up" if not transposed else "couple_down",
    )(high, low, *segments)


def solve_kernel(transposed, n_parts, right_ref, inverse_ref, *refs):
    parts, outs = refs[:n_parts], refs[n_parts:]
    value = right_ref[...].reshape(outs[0].shape)
    pieces = []
    for part in parts:
        if len(part.shape) == 3:
            pieces += [part[place] for place in range(part.shape[0])]
        else:
            pieces.append(part[...])
    if pieces:
        summed = pieces[0]
        for piece in pieces[1:]:
            summed += piece
        value -= summed
    inverse = inverse_ref[...].reshape(inverse_ref.shape[-2:])
    result = product(halves(value), halves(inverse), transposed)
    outs[0][...] = result
    for copies in outs[1:]:
        for place in range(copies.shape[0]):
            copies[place] = result


def solve(right, inverse, level, parts, transposed, copies=0):
    rows, block = right.shape[-2:]
    at_level = lambda shape: pl.BlockSpec((1,) + shape, lambda i: (level, 0, 0))
    plain = pl.BlockSpec((rows, block), lambda i: (0, 0))
    spec_of = lambda part: pl.BlockSpec(part.shape, lambda i: (0,) * part.ndim)
    out_shape = [jax.ShapeDtypeStruct((rows, block), jnp.float32)]
    if copies:
        out_shape.append(jax.ShapeDtypeStruct((copies, rows, block), jnp.float32))
    return pl.pallas_call(
        functools.partial(solve_kernel, transposed, len(parts)),
        grid=(1,),
        out_shape=out_shape,
        in_specs=[
            at_level((rows, block)) if right.ndim == 3 else plain,
            at_level((block, block)),
        ]
        + [spec_of(part) for part in parts],
        out_specs=[spec_of(out) for out in out_shape],
        compiler_params=pltpu.CompilerParams(vmem_limit_bytes=8 * MIB),
        cost_estimate=pl.CostEstimate(
            flops=6 * rows * block * block, bytes_accessed=4 * block * block, transcendentals=0
        ),
        name="solve_up" if not transposed else "solve_down",
    )(right, inverse, *parts)


def spread(segment, axis):
    size = lax.axis_size(axis)
    return [segment] + [
        lax.ppermute(segment, axis, [(i, i ^ d) for i in range(size)]) for d in range(1, size)
    ]


def deliver(parts, axis):
    size = lax.axis_size(axis)
    return [parts[0]] + [
        lax.ppermute(parts[d], axis, [(i, i ^ d) for i in range(size)]) for d in range(1, size)
    ]


def direct_shards(rhs, diag_inv, blocks, blk_target, blk_source, blk_count):
    levels = rhs.shape[0]
    n_row, n_col = lax.axis_size("row"), lax.axis_size("col")
    right = rhs.reshape((levels,) + rhs.shape[-2:])
    inverse = diag_inv.reshape((levels,) + diag_inv.shape[-2:])
    weights = blocks.reshape((levels - 1,) + blocks.shape[-3:])
    target = blk_target.reshape(levels - 1, -1)
    source = blk_source.reshape(levels - 1, -1)
    count = blk_count.reshape(levels - 1)
    place = jnp.stack([lax.axis_index("row"), lax.axis_index("col")]).astype(jnp.int32)
    coupling = [
        gather_blocks(level, target, source, count, place, weights, n_row, n_col)
        for level in range(levels - 1)
    ]
    exchange = lambda stacked: lax.all_to_all(stacked, "row", 0, 0, tiled=True)
    first, copies = solve(right, inverse, 0, [], False, n_row)
    forward = [first]
    for level in range(1, levels):
        partial = couple([exchange(copies)], *coupling[level - 1], False)
        more = n_row if level < levels - 1 else 0
        solved = solve(right, inverse, level, deliver(partial, "col"), False, more)
        forward.append(solved[0])
        copies = solved[-1]
    backward = [None] * levels
    backward[-1] = solve(forward[-1], inverse, levels - 1, [], True)[0]
    for level in range(levels - 2, -1, -1):
        (partial,) = couple(spread(backward[level + 1], "col"), *coupling[level], True)
        backward[level] = solve(forward[level], inverse, level, [exchange(partial)], True)[0]
    return (
        jnp.stack(forward).reshape(rhs.shape),
        jnp.stack(backward).reshape(rhs.shape),
    )


def fold_for(index, piece):
    entry_count = piece.shape[0]
    onehot = (index[:, None] == jnp.arange(entry_count, dtype=jnp.int32)[None, :]).astype(
        jnp.float32
    )
    return jnp.dot(
        onehot,
        piece.reshape(entry_count, -1),
        precision=HIGH_PRECISION,
        preferred_element_type=jnp.float32,
    )


def route_sum(index, entry_count, block_products, width):
    slot_count = block_products.shape[0]
    active_flags = jnp.arange(slot_count, dtype=jnp.int32) < entry_count
    routing_table = (
        (index[None, :] == jnp.arange(width, dtype=jnp.int32)[:, None]) & active_flags[None, :]
    ).astype(jnp.float32)
    return jnp.dot(
        routing_table,
        block_products.reshape(slot_count, -1),
        precision=HIGH_PRECISION,
        preferred_element_type=jnp.float32,
    )


def forward_level(previous, weight_matrix, target, source, entry_count):
    slot_count = weight_matrix.shape[0]
    slots, rhs_column_count, block_ordering = previous.shape
    selected_blocks = fold_for(source, lax.all_gather(previous, "row", axis=0, tiled=True))
    block_products = jnp.einsum(
        "ado,aon->adn",
        selected_blocks.reshape(slot_count, rhs_column_count, block_ordering),
        weight_matrix,
        precision=HIGH_PRECISION,
    )
    ncol = lax.axis_size("col")
    buckets = route_sum(target, entry_count, block_products, ncol * slots).reshape(
        ncol, slots, rhs_column_count, block_ordering
    )
    own = lax.psum_scatter(buckets, "col", scatter_dimension=0, tiled=True)[0]
    return own


def backward_level(upper, weight_matrix, target, source, entry_count):
    slot_count = weight_matrix.shape[0]
    slots, rhs_column_count, block_ordering = upper.shape
    selected_blocks = fold_for(target, lax.all_gather(upper, "col", axis=0, tiled=True))
    block_products = jnp.einsum(
        "mlv,mtv->mlt",
        selected_blocks.reshape(slot_count, rhs_column_count, block_ordering),
        weight_matrix,
        precision=HIGH_PRECISION,
    )
    nrow = lax.axis_size("row")
    buckets = route_sum(source, entry_count, block_products, nrow * slots).reshape(
        nrow, slots, rhs_column_count, block_ordering
    )
    own = lax.psum_scatter(buckets, "row", scatter_dimension=0, tiled=True)[0]
    return own


def shards(rhs, diag_inv, blocks, blk_target, blk_source, blk_count):
    levels = rhs.shape[0]
    right = rhs[:, 0, 0]
    inverse = diag_inv[:, 0, 0]
    weight_matrix = blocks[:, 0, 0]
    targets = blk_target[:, 0, 0]
    sources = blk_source[:, 0, 0]
    counts = blk_count[:, 0, 0]
    forward = [jnp.einsum("srb,sbc->src", right[0], inverse[0], precision=HIGH_PRECISION)]
    for level in range(1, levels):
        own = forward_level(
            forward[-1],
            weight_matrix[level - 1],
            targets[level - 1],
            sources[level - 1],
            counts[level - 1],
        )
        forward.append(
            jnp.einsum("srb,sbc->src", right[level] - own, inverse[level], precision=HIGH_PRECISION)
        )
    backward = [None] * levels
    backward[levels - 1] = jnp.einsum(
        "src,sbc->srb", forward[levels - 1], inverse[levels - 1], precision=HIGH_PRECISION
    )
    for level in range(levels - 2, -1, -1):
        own = backward_level(
            backward[level + 1], weight_matrix[level], targets[level], sources[level], counts[level]
        )
        backward[level] = jnp.einsum(
            "src,sbc->srb", forward[level] - own, inverse[level], precision=HIGH_PRECISION
        )
    forward_out = jnp.stack(forward)[:, None, None]
    backward_out = jnp.stack(backward)[:, None, None]
    return (forward_out, backward_out)


def solution(mesh):
    placed = (
        P(None, "row", "col", None, None, None),
        P(None, "row", "col", None, None, None),
        P(None, "row", "col", None, None, None),
        P(None, "row", "col", None),
        P(None, "row", "col", None),
        P(None, "row", "col"),
    )
    n_row, n_col = mesh.shape["row"], mesh.shape["col"]

    def local(rhs, diag_inv, blocks, blk_target, blk_source, blk_count):
        sizes = (n_row, n_col)
        dense = n_row * n_col <= blocks.shape[3] and rhs.shape[3] == 1
        even = all(size & (size - 1) == 0 for size in sizes)
        run = direct_shards if dense and even else shards
        return run(rhs, diag_inv, blocks, blk_target, blk_source, blk_count)

    return jax.shard_map(
        local,
        mesh=mesh,
        in_specs=placed,
        out_specs=(
            P(None, "row", "col", None, None, None),
            P(None, "row", "col", None, None, None),
        ),
        check_vma=False,
    )
```

```python
import functools

import jax
import jax.numpy as jnp
from jax import lax
from jax.experimental import pallas as pl
from jax.experimental.pallas import tpu as pltpu
from jax.sharding import PartitionSpec as P

HIGH_PRECISION = lax.Precision.HIGHEST
MIB = 1024 * 1024
VMEM = pltpu.MemorySpace.VMEM
SMEM = pltpu.MemorySpace.SMEM


def halves(value):
    high = value.astype(jnp.bfloat16)
    low = (value - high.astype(jnp.float32)).astype(jnp.bfloat16)
    return high, low


def product(left, right, transposed):
    contract = (((1,), (1 if transposed else 0,)), ((), ()))
    dot = functools.partial(
        lax.dot_general, dimension_numbers=contract, preferred_element_type=jnp.float32
    )
    return dot(left[0], right[0]) + (dot(left[0], right[1]) + dot(left[1], right[0]))


def gather_blocks_kernel(
    n_col, level, target_ref, source_ref, count_ref, place_ref, blocks_ref, high_ref, low_ref, total
):
    block = blocks_ref.shape[-1]
    total[...] = jnp.zeros_like(total)

    def add(slot, carry):
        below = source_ref[level, slot] ^ place_ref[0]
        above = target_ref[level, slot] ^ place_ref[1]
        pair = below * n_col + above
        total[pair] += blocks_ref[0, slot]
        return carry

    lax.fori_loop(0, count_ref[level], add, 0)
    for pair in range(total.shape[0]):
        rows = pl.ds(pair // n_col * block, block)
        lanes = pl.ds(pair % n_col * block, block)
        high, low = halves(total[pair])
        high_ref[rows, lanes] = high
        low_ref[rows, lanes] = low


def gather_blocks(level, target, source, count, place, blocks, n_row, n_col):
    slot_count, block = blocks.shape[1], blocks.shape[2]
    shape = (n_row * block, n_col * block)
    scalars = pl.BlockSpec(memory_space=SMEM)
    whole = pl.BlockSpec(shape, lambda i: (0, 0))
    return pl.pallas_call(
        functools.partial(gather_blocks_kernel, n_col, level),
        grid=(1,),
        out_shape=[jax.ShapeDtypeStruct(shape, jnp.bfloat16)] * 2,
        in_specs=[scalars] * 4
        + [pl.BlockSpec((1, slot_count, block, block), lambda i: (level, 0, 0, 0))],
        out_specs=[whole, whole],
        scratch_shapes=[pltpu.VMEM((n_row * n_col, block, block), jnp.float32)],
        compiler_params=pltpu.CompilerParams(vmem_limit_bytes=16 * MIB),
        cost_estimate=pl.CostEstimate(
            flops=2 * shape[0] * shape[1], bytes_accessed=8 * shape[0] * shape[1], transcendentals=0
        ),
        name=f"gather_blocks_{level}",
    )(target, source, count, place, blocks)


def read(term, refs):
    number, place = term
    return refs[number][...] if place is None else refs[number][place]


def total_of(terms, refs):
    value = read(terms[0], refs)
    for term in terms[1:]:
        value += read(term, refs)
    return value


def write(ref, values):
    if len(ref.shape) == 2:
        ref[...] = values[0]
    else:
        for place, value in enumerate(values):
            ref[place] = value


class Operands:
    def __init__(self):
        self.arrays = []

    def term(self, piece):
        array, place = piece
        for number, known in enumerate(self.arrays):
            if known is array:
                return number, place
        self.arrays.append(array)
        return len(self.arrays) - 1, place


def message_shape(group, rows, block):
    shape = (rows, block) if len(group) == 1 else (len(group), rows, block)
    return jax.ShapeDtypeStruct(shape, jnp.float32)


def combine_kernel(sums, *refs):
    write(refs[-1], [total_of(terms, refs[:-1]) for terms in sums])


def combine(sums):
    if len(sums) == 1 and len(sums[0]) == 1 and sums[0][0][1] is None:
        return sums[0][0][0]
    operands = Operands()
    terms = [[operands.term(piece) for piece in pieces] for pieces in sums]
    rows, block = operands.arrays[0].shape[-2:]
    whole = pl.BlockSpec(memory_space=VMEM)
    return pl.pallas_call(
        functools.partial(combine_kernel, terms),
        out_shape=message_shape(sums, rows, block),
        in_specs=[whole] * len(operands.arrays),
        out_specs=whole,
        compiler_params=pltpu.CompilerParams(vmem_limit_bytes=4 * MIB),
        cost_estimate=pl.CostEstimate(
            flops=rows * block * len(sums), bytes_accessed=rows * block, transcendentals=0
        ),
        name="combine",
    )(*operands.arrays)


def couple_kernel(transposed, terms, groups, high_ref, low_ref, *refs):
    n_out = len(groups)
    ins, outs = refs[:-n_out], refs[-n_out:]
    block = ins[0].shape[-1]
    joined = jnp.concatenate([read(term, ins) for term in terms], axis=1)
    result = product(halves(joined), (high_ref[...], low_ref[...]), transposed)
    for group, ref in zip(groups, outs):
        write(ref, [result[:, place * block : (place + 1) * block] for place in group])


def couple(pieces, high, low, groups, transposed):
    operands = Operands()
    terms = [operands.term(pieces[partner]) for partner in range(len(pieces))]
    rows, block = operands.arrays[0].shape[-2:]
    whole = pl.BlockSpec(memory_space=VMEM)
    messages = pl.pallas_call(
        functools.partial(couple_kernel, transposed, terms, groups),
        out_shape=[message_shape(group, rows, block) for group in groups],
        in_specs=[whole] * (2 + len(operands.arrays)),
        out_specs=[whole] * len(groups),
        compiler_params=pltpu.CompilerParams(vmem_limit_bytes=16 * MIB),
        cost_estimate=pl.CostEstimate(
            flops=6 * rows * high.size, bytes_accessed=4 * high.size, transcendentals=0
        ),
        name="couple_up" if not transposed else "couple_down",
    )(high, low, *operands.arrays)
    return dict(zip(groups, messages))


def solve_kernel(transposed, terms, right_ref, inverse_ref, *refs):
    ins, out_ref = refs[:-1], refs[-1]
    value = right_ref[...].reshape(out_ref.shape)
    if terms:
        value -= total_of(terms, ins)
    inverse = inverse_ref[...].reshape(inverse_ref.shape[-2:])
    out_ref[...] = product(halves(value), halves(inverse), transposed)


def solve(right, inverse, level, pieces, transposed):
    rows, block = right.shape[-2:]
    operands = Operands()
    terms = [operands.term(piece) for piece in pieces]
    at_level = lambda shape: pl.BlockSpec((1,) + shape, lambda i: (level, 0, 0))
    spec_of = lambda part: pl.BlockSpec(part.shape, lambda i: (0,) * part.ndim)
    out_shape = jax.ShapeDtypeStruct((rows, block), jnp.float32)
    return pl.pallas_call(
        functools.partial(solve_kernel, transposed, terms),
        grid=(1,),
        out_shape=out_shape,
        in_specs=[
            at_level((rows, block)) if right.ndim == 3 else spec_of(right),
            at_level((block, block)),
        ]
        + [spec_of(part) for part in operands.arrays],
        out_specs=spec_of(out_shape),
        compiler_params=pltpu.CompilerParams(vmem_limit_bytes=8 * MIB),
        cost_estimate=pl.CostEstimate(
            flops=6 * rows * block * block, bytes_accessed=4 * block * block, transcendentals=0
        ),
        name="solve_up" if not transposed else "solve_down",
    )(right, inverse, *operands.arrays)


def depth_of(partner):
    return bin(partner).count("1")


def bits_of(size):
    return [1 << place for place in range(size.bit_length() - 1)]


def messages_of(held, bit):
    depths = sorted({depth_of(partner) for partner in held})
    return [
        tuple(partner | bit for partner in sorted(held) if depth_of(partner) == depth)
        for depth in depths
    ]


def exchange(message, axis, bit):
    size = lax.axis_size(axis)
    return lax.ppermute(message, axis, [(i, i ^ bit) for i in range(size)])


def pieces_of(message, count):
    return [(message, place if count > 1 else None) for place in range(count)]


def spread(segment, axis):
    held = {0: (segment, None)}
    for bit in reversed(bits_of(lax.axis_size(axis))):
        gained = {}
        for group in messages_of(held, bit):
            message = exchange(combine([[held[d ^ bit]] for d in group]), axis, bit)
            gained.update(zip(group, pieces_of(message, len(group))))
        held.update(gained)
    return held


def delivery_groups(size):
    bit = 1
    rest = [d for d in range(size) if not d & bit]
    return tuple(reversed(messages_of(rest, bit))) + tuple((d,) for d in rest)


def deliver(messages, axis):
    size = lax.axis_size(axis)
    held = {}
    for group, message in messages.items():
        held.update({d: [piece] for d, piece in zip(group, pieces_of(message, len(group)))})
    for bit in bits_of(size):
        kept = [d for d in held if not d & bit]
        for group in reversed(messages_of(kept, bit)):
            message = messages.get(group) if bit == 1 else combine([held[d] for d in group])
            message = exchange(message, axis, bit)
            for d, piece in zip(group, pieces_of(message, len(group))):
                held[d ^ bit].append(piece)
        held = {d: held[d] for d in kept}
    return held[0]


def direct_shards(rhs, diag_inv, blocks, blk_target, blk_source, blk_count):
    levels = rhs.shape[0]
    n_row, n_col = lax.axis_size("row"), lax.axis_size("col")
    right = rhs.reshape((levels,) + rhs.shape[-2:])
    inverse = diag_inv.reshape((levels,) + diag_inv.shape[-2:])
    weights = blocks.reshape((levels - 1,) + blocks.shape[-3:])
    target = blk_target.reshape(levels - 1, -1)
    source = blk_source.reshape(levels - 1, -1)
    count = blk_count.reshape(levels - 1)
    place = jnp.stack([lax.axis_index("row"), lax.axis_index("col")]).astype(jnp.int32)
    coupling = [
        gather_blocks(level, target, source, count, place, weights, n_row, n_col)
        for level in range(levels - 1)
    ]
    over_row, over_col = delivery_groups(n_row), delivery_groups(n_col)
    forward = [solve(right, inverse, 0, [], False)]
    for level in range(1, levels):
        partial = couple(spread(forward[-1], "row"), *coupling[level - 1], over_col, False)
        forward.append(solve(right, inverse, level, deliver(partial, "col"), False))
    backward = [None] * levels
    backward[-1] = solve(forward[-1], inverse, levels - 1, [], True)
    for level in range(levels - 2, -1, -1):
        partial = couple(spread(backward[level + 1], "col"), *coupling[level], over_row, True)
        backward[level] = solve(forward[level], inverse, level, deliver(partial, "row"), True)
    return (
        jnp.stack(forward).reshape(rhs.shape),
        jnp.stack(backward).reshape(rhs.shape),
    )


def fold_for(index, piece):
    entry_count = piece.shape[0]
    onehot = (index[:, None] == jnp.arange(entry_count, dtype=jnp.int32)[None, :]).astype(
        jnp.float32
    )
    return jnp.dot(
        onehot,
        piece.reshape(entry_count, -1),
        precision=HIGH_PRECISION,
        preferred_element_type=jnp.float32,
    )


def route_sum(index, entry_count, block_products, width):
    slot_count = block_products.shape[0]
    active_flags = jnp.arange(slot_count, dtype=jnp.int32) < entry_count
    routing_table = (
        (index[None, :] == jnp.arange(width, dtype=jnp.int32)[:, None]) & active_flags[None, :]
    ).astype(jnp.float32)
    return jnp.dot(
        routing_table,
        block_products.reshape(slot_count, -1),
        precision=HIGH_PRECISION,
        preferred_element_type=jnp.float32,
    )


def forward_level(previous, weight_matrix, target, source, entry_count):
    slot_count = weight_matrix.shape[0]
    slots, rhs_column_count, block_ordering = previous.shape
    selected_blocks = fold_for(source, lax.all_gather(previous, "row", axis=0, tiled=True))
    block_products = jnp.einsum(
        "ado,aon->adn",
        selected_blocks.reshape(slot_count, rhs_column_count, block_ordering),
        weight_matrix,
        precision=HIGH_PRECISION,
    )
    ncol = lax.axis_size("col")
    buckets = route_sum(target, entry_count, block_products, ncol * slots).reshape(
        ncol, slots, rhs_column_count, block_ordering
    )
    own = lax.psum_scatter(buckets, "col", scatter_dimension=0, tiled=True)[0]
    return own


def backward_level(upper, weight_matrix, target, source, entry_count):
    slot_count = weight_matrix.shape[0]
    slots, rhs_column_count, block_ordering = upper.shape
    selected_blocks = fold_for(target, lax.all_gather(upper, "col", axis=0, tiled=True))
    block_products = jnp.einsum(
        "mlv,mtv->mlt",
        selected_blocks.reshape(slot_count, rhs_column_count, block_ordering),
        weight_matrix,
        precision=HIGH_PRECISION,
    )
    nrow = lax.axis_size("row")
    buckets = route_sum(source, entry_count, block_products, nrow * slots).reshape(
        nrow, slots, rhs_column_count, block_ordering
    )
    own = lax.psum_scatter(buckets, "row", scatter_dimension=0, tiled=True)[0]
    return own


def shards(rhs, diag_inv, blocks, blk_target, blk_source, blk_count):
    levels = rhs.shape[0]
    right = rhs[:, 0, 0]
    inverse = diag_inv[:, 0, 0]
    weight_matrix = blocks[:, 0, 0]
    targets = blk_target[:, 0, 0]
    sources = blk_source[:, 0, 0]
    counts = blk_count[:, 0, 0]
    forward = [jnp.einsum("srb,sbc->src", right[0], inverse[0], precision=HIGH_PRECISION)]
    for level in range(1, levels):
        own = forward_level(
            forward[-1],
            weight_matrix[level - 1],
            targets[level - 1],
            sources[level - 1],
            counts[level - 1],
        )
        forward.append(
            jnp.einsum("srb,sbc->src", right[level] - own, inverse[level], precision=HIGH_PRECISION)
        )
    backward = [None] * levels
    backward[levels - 1] = jnp.einsum(
        "src,sbc->srb", forward[levels - 1], inverse[levels - 1], precision=HIGH_PRECISION
    )
    for level in range(levels - 2, -1, -1):
        own = backward_level(
            backward[level + 1], weight_matrix[level], targets[level], sources[level], counts[level]
        )
        backward[level] = jnp.einsum(
            "src,sbc->srb", forward[level] - own, inverse[level], precision=HIGH_PRECISION
        )
    forward_out = jnp.stack(forward)[:, None, None]
    backward_out = jnp.stack(backward)[:, None, None]
    return (forward_out, backward_out)


def solution(mesh):
    placed = (
        P(None, "row", "col", None, None, None),
        P(None, "row", "col", None, None, None),
        P(None, "row", "col", None, None, None),
        P(None, "row", "col", None),
        P(None, "row", "col", None),
        P(None, "row", "col"),
    )
    n_row, n_col = mesh.shape["row"], mesh.shape["col"]

    def local(rhs, diag_inv, blocks, blk_target, blk_source, blk_count):
        sizes = (n_row, n_col)
        dense = n_row * n_col <= blocks.shape[3] and rhs.shape[3] == 1
        even = all(size & (size - 1) == 0 for size in sizes)
        run = direct_shards if dense and even else shards
        return run(rhs, diag_inv, blocks, blk_target, blk_source, blk_count)

    return jax.shard_map(
        local,
        mesh=mesh,
        in_specs=placed,
        out_specs=(
            P(None, "row", "col", None, None, None),
            P(None, "row", "col", None, None, None),
        ),
        check_vma=False,
    )
```

```python
import functools

import jax
import jax.numpy as jnp
from jax import lax
from jax.experimental import pallas as pl
from jax.experimental.pallas import tpu as pltpu
from jax.sharding import PartitionSpec as P

HIGH_PRECISION = lax.Precision.HIGHEST
MIB = 1024 * 1024
VMEM = pltpu.MemorySpace.VMEM
SMEM = pltpu.MemorySpace.SMEM


def halves(value):
    high = value.astype(jnp.bfloat16)
    low = (value - high.astype(jnp.float32)).astype(jnp.bfloat16)
    return high, low


def product(left, right, transposed):
    contract = (((1,), (1 if transposed else 0,)), ((), ()))
    dot = functools.partial(
        lax.dot_general, dimension_numbers=contract, preferred_element_type=jnp.float32
    )
    return dot(left[0], right[0]) + (dot(left[0], right[1]) + dot(left[1], right[0]))


def gather_blocks_kernel(
    n_col, level, target_ref, source_ref, count_ref, place_ref, blocks_ref, *refs
):
    high_ref, low_ref, slots, total, arrived = refs[-5:]
    slot_count, block = slots.shape[:2]
    count = count_ref[level]

    def fetch(slot):
        return pltpu.make_async_copy(blocks_ref.at[level, slot], slots.at[slot], arrived.at[slot])

    for slot in range(slot_count):
        pl.when(slot < count)(fetch(slot).start)
    total[...] = jnp.zeros_like(total)

    def add(slot, carry):
        fetch(slot).wait()
        above = target_ref[level, slot] ^ place_ref[0]
        total[source_ref[level, slot] * n_col + above] += slots[slot]
        return carry

    lax.fori_loop(0, count, add, 0)
    for pair in range(total.shape[0]):
        rows = pl.ds(pair // n_col * block, block)
        lanes = pl.ds(pair % n_col * block, block)
        high, low = halves(total[pair])
        high_ref[rows, lanes] = high
        low_ref[rows, lanes] = low


def gather_blocks(level, target, source, count, place, blocks, n_row, n_col, after):
    slot_count, block = blocks.shape[1], blocks.shape[2]
    shape = (n_row * block, n_col * block)
    scalars = pl.BlockSpec(memory_space=SMEM)
    whole = pl.BlockSpec(memory_space=VMEM)
    return pl.pallas_call(
        functools.partial(gather_blocks_kernel, n_col, level),
        out_shape=[jax.ShapeDtypeStruct(shape, jnp.bfloat16)] * 2,
        in_specs=[scalars] * 4
        + [pl.BlockSpec(memory_space=pltpu.MemorySpace.HBM)]
        + [pl.BlockSpec(memory_space=pl.ANY)] * len(after),
        out_specs=[whole, whole],
        scratch_shapes=[
            pltpu.VMEM((slot_count, block, block), jnp.float32),
            pltpu.VMEM((n_row * n_col, block, block), jnp.float32),
            pltpu.SemaphoreType.DMA((slot_count,)),
        ],
        compiler_params=pltpu.CompilerParams(vmem_limit_bytes=(16 if after else 51) * MIB),
        cost_estimate=pl.CostEstimate(
            flops=2 * shape[0] * shape[1], bytes_accessed=8 * shape[0] * shape[1], transcendentals=0
        ),
        name=f"gather_blocks_{level}",
    )(target, source, count, place, blocks, *after)


def read(term, refs):
    number, place = term
    return refs[number][...] if place is None else refs[number][place]


def total_of(terms, refs):
    value = read(terms[0], refs)
    for term in terms[1:]:
        value += read(term, refs)
    return value


def write(ref, values):
    if len(ref.shape) == 2:
        ref[...] = values[0]
    else:
        for place, value in enumerate(values):
            ref[place] = value


class Operands:
    def __init__(self):
        self.arrays = []

    def term(self, piece):
        array, place = piece
        for number, known in enumerate(self.arrays):
            if known is array:
                return number, place
        self.arrays.append(array)
        return len(self.arrays) - 1, place


def couple_kernel(transposed, terms, high_ref, low_ref, *refs):
    n_in = 1 + max(number for number, _ in terms)
    ins, outs = refs[:n_in], refs[n_in:]
    block = ins[0].shape[-1]
    joined = jnp.concatenate([read(term, ins) for term in terms], axis=1)
    result = product(halves(joined), (high_ref[...], low_ref[...]), transposed)
    pieces = [result[:, at : at + block] for at in range(0, result.shape[1], block)]
    if len(outs) == 1:
        write(outs[0], pieces)
    else:
        for ref, piece in zip(outs, pieces):
            ref[...] = piece


def couple(pieces, high, low, transposed):
    operands = Operands()
    terms = [operands.term(piece) for piece in pieces]
    rows, block = operands.arrays[0].shape[-2:]
    n_out = high.shape[0 if transposed else 1] // block
    shapes = [(n_out, rows, block)] if transposed else [(rows, block)] * n_out
    whole = pl.BlockSpec(memory_space=VMEM)
    return pl.pallas_call(
        functools.partial(couple_kernel, transposed, terms),
        out_shape=[jax.ShapeDtypeStruct(shape, jnp.float32) for shape in shapes],
        in_specs=[whole] * (2 + len(operands.arrays)),
        out_specs=[whole] * len(shapes),
        compiler_params=pltpu.CompilerParams(vmem_limit_bytes=16 * MIB),
        cost_estimate=pl.CostEstimate(
            flops=6 * rows * high.size, bytes_accessed=4 * high.size, transcendentals=0
        ),
        name="couple_up" if not transposed else "couple_down",
    )(high, low, *operands.arrays)


def first_solve_kernel(right_ref, inverse_ref, out_ref, copies_ref, right, inverse, arrived):
    fetches = [
        pltpu.make_async_copy(right_ref.at[0], right, arrived.at[0]),
        pltpu.make_async_copy(inverse_ref.at[0], inverse, arrived.at[1]),
    ]
    for fetch in fetches:
        fetch.start()
    for fetch in fetches:
        fetch.wait()
    result = product(halves(right[...]), halves(inverse[...]), False)
    out_ref[...] = result
    write(copies_ref, [result] * copies_ref.shape[0])


def first_solve(right, inverse, n_copies):
    rows, block = right.shape[-2:]
    whole = pl.BlockSpec(memory_space=VMEM)
    return pl.pallas_call(
        first_solve_kernel,
        out_shape=[
            jax.ShapeDtypeStruct((rows, block), jnp.float32),
            jax.ShapeDtypeStruct((n_copies, rows, block), jnp.float32),
        ],
        in_specs=[pl.BlockSpec(memory_space=pl.ANY)] * 2,
        out_specs=[whole] * 2,
        scratch_shapes=[
            pltpu.VMEM((rows, block), jnp.float32),
            pltpu.VMEM((block, block), jnp.float32),
            pltpu.SemaphoreType.DMA((2,)),
        ],
        compiler_params=pltpu.CompilerParams(vmem_limit_bytes=60 * MIB),
        name="first_solve",
    )(right, inverse)


def solve_kernel(transposed, level, terms, n_ins, n_copies, *refs):
    right_ref, inverse_ref = refs[:2]
    ins = refs[2 : 2 + n_ins]
    outs = refs[-2:] if n_copies else refs[-1:]
    value = right_ref[level] if len(right_ref.shape) == 3 else right_ref[...]
    if terms:
        value -= total_of(terms, ins)
    result = product(halves(value), halves(inverse_ref[level]), transposed)
    outs[0][...] = result
    if n_copies:
        write(outs[1], [result] * n_copies)


def solve(right, inverse, level, pieces, transposed, n_copies=0, after=()):
    rows, block = right.shape[-2:]
    operands = Operands()
    terms = [operands.term(piece) for piece in pieces]
    whole = pl.BlockSpec(memory_space=VMEM)
    out_shape = [jax.ShapeDtypeStruct((rows, block), jnp.float32)]
    if n_copies:
        out_shape.append(jax.ShapeDtypeStruct((n_copies, rows, block), jnp.float32))
    return pl.pallas_call(
        functools.partial(
            solve_kernel, transposed, level, terms, len(operands.arrays), n_copies
        ),
        out_shape=out_shape,
        in_specs=[whole] * (2 + len(operands.arrays))
        + [pl.BlockSpec(memory_space=pl.ANY)] * len(after),
        out_specs=[whole] * len(out_shape),
        compiler_params=pltpu.CompilerParams(vmem_limit_bytes=8 * MIB),
        cost_estimate=pl.CostEstimate(
            flops=6 * rows * block * block, bytes_accessed=4 * block * block, transcendentals=0
        ),
        name="solve_up" if not transposed else "solve_down",
    )(right, inverse, *operands.arrays, *after)


def stack_kernel(n_forward, *refs):
    ins, (forward_ref, backward_ref) = refs[:-2], refs[-2:]
    write(forward_ref, [ref[...] for ref in ins[:n_forward]])
    write(backward_ref, [ref[...] for ref in ins[n_forward:]])


def stack(forward, backward):
    whole = pl.BlockSpec(memory_space=VMEM)
    shape = jax.ShapeDtypeStruct((len(forward),) + forward[0].shape, jnp.float32)
    return pl.pallas_call(
        functools.partial(stack_kernel, len(forward)),
        out_shape=[shape, shape],
        in_specs=[whole] * (2 * len(forward)),
        out_specs=[whole] * 2,
        compiler_params=pltpu.CompilerParams(vmem_limit_bytes=8 * MIB),
        name="stack",
    )(*forward, *backward)


def exchange_all(stacked, axis):
    received = lax.all_to_all(stacked, axis, 0, 0, tiled=True)
    return [(received, place) for place in range(stacked.shape[0])]


def exchange_each(messages, axis):
    size = lax.axis_size(axis)
    received = [messages[0]] + [
        lax.ppermute(messages[d], axis, [(i, i ^ d) for i in range(size)])
        for d in range(1, size)
    ]
    return [(message, None) for message in received]


def direct_shards(rhs, diag_inv, blocks, blk_target, blk_source, blk_count):
    levels = rhs.shape[0]
    n_row, n_col = lax.axis_size("row"), lax.axis_size("col")
    right = rhs.reshape((levels,) + rhs.shape[-2:])
    inverse = diag_inv.reshape((levels,) + diag_inv.shape[-2:])
    weights = blocks.reshape((levels - 1,) + blocks.shape[-3:])
    target = blk_target.reshape(levels - 1, -1)
    source = blk_source.reshape(levels - 1, -1)
    count = blk_count.reshape(levels - 1)
    place = lax.axis_index("col").astype(jnp.int32).reshape(1)
    gather = lambda level, after: gather_blocks(
        level, target, source, count, place, weights, n_row, n_col, after
    )
    first, copies = first_solve(right, inverse, n_row)
    coupling = [gather(0, ())]
    forward = [first]
    for level in range(1, levels):
        partial = couple(exchange_all(copies, "row"), *coupling[level - 1], False)
        last = level == levels - 1
        if not last:
            coupling.append(gather(level, (partial[0],)))
        after = () if last else coupling[level][:1]
        pieces = exchange_each(partial, "col")
        solved = solve(right, inverse, level, pieces, False, 0 if last else n_row, after)
        forward.append(solved[0])
        copies = solved[-1]
    backward = [None] * levels
    (backward[-1],) = solve(forward[-1], inverse, levels - 1, [], True)
    for level in range(levels - 2, -1, -1):
        pieces = exchange_each([backward[level + 1]] * n_col, "col")
        (partial,) = couple(pieces, *coupling[level], True)
        pieces = exchange_all(partial, "row")
        (backward[level],) = solve(forward[level], inverse, level, pieces, True)
    outs = stack(forward, backward)
    return tuple(out.reshape(rhs.shape) for out in outs)


def fold_for(index, piece):
    entry_count = piece.shape[0]
    onehot = (index[:, None] == jnp.arange(entry_count, dtype=jnp.int32)[None, :]).astype(
        jnp.float32
    )
    return jnp.dot(
        onehot,
        piece.reshape(entry_count, -1),
        precision=HIGH_PRECISION,
        preferred_element_type=jnp.float32,
    )


def route_sum(index, entry_count, block_products, width):
    slot_count = block_products.shape[0]
    active_flags = jnp.arange(slot_count, dtype=jnp.int32) < entry_count
    routing_table = (
        (index[None, :] == jnp.arange(width, dtype=jnp.int32)[:, None]) & active_flags[None, :]
    ).astype(jnp.float32)
    return jnp.dot(
        routing_table,
        block_products.reshape(slot_count, -1),
        precision=HIGH_PRECISION,
        preferred_element_type=jnp.float32,
    )


def forward_level(previous, weight_matrix, target, source, entry_count):
    slot_count = weight_matrix.shape[0]
    slots, rhs_column_count, block_ordering = previous.shape
    selected_blocks = fold_for(source, lax.all_gather(previous, "row", axis=0, tiled=True))
    block_products = jnp.einsum(
        "ado,aon->adn",
        selected_blocks.reshape(slot_count, rhs_column_count, block_ordering),
        weight_matrix,
        precision=HIGH_PRECISION,
    )
    ncol = lax.axis_size("col")
    buckets = route_sum(target, entry_count, block_products, ncol * slots).reshape(
        ncol, slots, rhs_column_count, block_ordering
    )
    own = lax.psum_scatter(buckets, "col", scatter_dimension=0, tiled=True)[0]
    return own


def backward_level(upper, weight_matrix, target, source, entry_count):
    slot_count = weight_matrix.shape[0]
    slots, rhs_column_count, block_ordering = upper.shape
    selected_blocks = fold_for(target, lax.all_gather(upper, "col", axis=0, tiled=True))
    block_products = jnp.einsum(
        "mlv,mtv->mlt",
        selected_blocks.reshape(slot_count, rhs_column_count, block_ordering),
        weight_matrix,
        precision=HIGH_PRECISION,
    )
    nrow = lax.axis_size("row")
    buckets = route_sum(source, entry_count, block_products, nrow * slots).reshape(
        nrow, slots, rhs_column_count, block_ordering
    )
    own = lax.psum_scatter(buckets, "row", scatter_dimension=0, tiled=True)[0]
    return own


def shards(rhs, diag_inv, blocks, blk_target, blk_source, blk_count):
    levels = rhs.shape[0]
    right = rhs[:, 0, 0]
    inverse = diag_inv[:, 0, 0]
    weight_matrix = blocks[:, 0, 0]
    targets = blk_target[:, 0, 0]
    sources = blk_source[:, 0, 0]
    counts = blk_count[:, 0, 0]
    forward = [jnp.einsum("srb,sbc->src", right[0], inverse[0], precision=HIGH_PRECISION)]
    for level in range(1, levels):
        own = forward_level(
            forward[-1],
            weight_matrix[level - 1],
            targets[level - 1],
            sources[level - 1],
            counts[level - 1],
        )
        forward.append(
            jnp.einsum("srb,sbc->src", right[level] - own, inverse[level], precision=HIGH_PRECISION)
        )
    backward = [None] * levels
    backward[levels - 1] = jnp.einsum(
        "src,sbc->srb", forward[levels - 1], inverse[levels - 1], precision=HIGH_PRECISION
    )
    for level in range(levels - 2, -1, -1):
        own = backward_level(
            backward[level + 1], weight_matrix[level], targets[level], sources[level], counts[level]
        )
        backward[level] = jnp.einsum(
            "src,sbc->srb", forward[level] - own, inverse[level], precision=HIGH_PRECISION
        )
    forward_out = jnp.stack(forward)[:, None, None]
    backward_out = jnp.stack(backward)[:, None, None]
    return (forward_out, backward_out)


def solution(mesh):
    placed = (
        P(None, "row", "col", None, None, None),
        P(None, "row", "col", None, None, None),
        P(None, "row", "col", None, None, None),
        P(None, "row", "col", None),
        P(None, "row", "col", None),
        P(None, "row", "col"),
    )
    n_row, n_col = mesh.shape["row"], mesh.shape["col"]

    def local(rhs, diag_inv, blocks, blk_target, blk_source, blk_count):
        sizes = (n_row, n_col)
        dense = n_row * n_col <= blocks.shape[3] and rhs.shape[3] == 1
        even = all(size & (size - 1) == 0 for size in sizes)
        run = direct_shards if dense and even else shards
        return run(rhs, diag_inv, blocks, blk_target, blk_source, blk_count)

    return jax.shard_map(
        local,
        mesh=mesh,
        in_specs=placed,
        out_specs=(
            P(None, "row", "col", None, None, None),
            P(None, "row", "col", None, None, None),
        ),
        check_vma=False,
    )
```

```python
import functools

import jax
import jax.numpy as jnp
from jax import lax
from jax.experimental import pallas as pl
from jax.experimental.pallas import tpu as pltpu
from jax.sharding import PartitionSpec as P

HIGH_PRECISION = lax.Precision.HIGHEST
MIB = 1024 * 1024
VMEM = pltpu.MemorySpace.VMEM
SMEM = pltpu.MemorySpace.SMEM


def halves(value):
    high = value.astype(jnp.bfloat16)
    low = (value - high.astype(jnp.float32)).astype(jnp.bfloat16)
    return high, low


def product(left, right, transposed):
    contract = (((1,), (1 if transposed else 0,)), ((), ()))
    dot = functools.partial(
        lax.dot_general, dimension_numbers=contract, preferred_element_type=jnp.float32
    )
    return dot(left[0], right[0]) + (dot(left[0], right[1]) + dot(left[1], right[0]))


def gather_blocks_kernel(
    n_row, n_col, level, chunk, target_ref, source_ref, count_ref, place_ref, blocks_ref, *refs
):
    total, slots, arrived = refs[-3:]
    count = count_ref[level]
    half = n_row // 2
    side = place_ref[0] // half

    def fetch(number):
        span = pl.ds(number * chunk, chunk)
        return pltpu.make_async_copy(
            blocks_ref.at[level, span], slots.at[span], arrived.at[number]
        )

    for number in range(arrived.shape[0]):
        pl.when(number * chunk < count)(fetch(number).start)
    total[...] = jnp.zeros_like(total)

    def add(slot, carry):
        pl.when(lax.rem(slot, chunk) == 0)(fetch(slot // chunk).wait)
        source = source_ref[level, slot]
        below = lax.rem(source, half) * 2 + ((source // half) ^ side)
        above = target_ref[level, slot] ^ place_ref[1]
        total[below * n_col + above] += slots[slot]
        return carry

    lax.fori_loop(0, count, add, 0)


def gather_blocks(level, target, source, count, place, blocks, n_row, n_col, after):
    slot_count, block = blocks.shape[1], blocks.shape[2]
    chunk = max(1, slot_count // 4)
    shape = (n_row * n_col, block, block)
    scalars = pl.BlockSpec(memory_space=SMEM)
    return pl.pallas_call(
        functools.partial(gather_blocks_kernel, n_row, n_col, level, chunk),
        out_shape=jax.ShapeDtypeStruct(shape, jnp.float32),
        in_specs=[scalars] * 4 + [pl.BlockSpec(memory_space=pl.ANY)] * (1 + len(after)),
        out_specs=pl.BlockSpec(memory_space=VMEM),
        scratch_shapes=[
            pltpu.VMEM((slot_count, block, block), jnp.float32),
            pltpu.SemaphoreType.DMA((slot_count // chunk,)),
        ],
        compiler_params=pltpu.CompilerParams(vmem_limit_bytes=(51 if level == 0 else 16) * MIB),
        cost_estimate=pl.CostEstimate(
            flops=slot_count * block * block,
            bytes_accessed=8 * slot_count * block * block,
            transcendentals=0,
        ),
        name=f"gather_blocks_{level}",
    )(target, source, count, place, blocks, *after)


def split_kernel(n_col, total_ref, *refs):
    high_ref, low_ref = refs[-2:]
    block = total_ref.shape[-1]
    for pair in range(total_ref.shape[0]):
        rows = pl.ds(pair // n_col * block, block)
        lanes = pl.ds(pair % n_col * block, block)
        high, low = halves(total_ref[pair])
        high_ref[rows, lanes] = high
        low_ref[rows, lanes] = low


def split(total, n_row, n_col, after):
    block = total.shape[-1]
    shape = jax.ShapeDtypeStruct((n_row * block, n_col * block), jnp.bfloat16)
    whole = pl.BlockSpec(memory_space=VMEM)
    return pl.pallas_call(
        functools.partial(split_kernel, n_col),
        out_shape=[shape, shape],
        in_specs=[whole] + [pl.BlockSpec(memory_space=pl.ANY)] * len(after),
        out_specs=[whole, whole],
        compiler_params=pltpu.CompilerParams(vmem_limit_bytes=8 * MIB),
        cost_estimate=pl.CostEstimate(
            flops=3 * total.size, bytes_accessed=8 * total.size, transcendentals=0
        ),
        name="split",
    )(total, *after)


def read(term, refs):
    number, place = term
    return refs[number][...] if place is None else refs[number][place]


def total_of(terms, refs):
    value = read(terms[0], refs)
    for term in terms[1:]:
        value += read(term, refs)
    return value


def write(ref, values):
    if len(ref.shape) == 2:
        ref[...] = values[0]
    else:
        for place, value in enumerate(values):
            ref[place] = value


class Operands:
    def __init__(self):
        self.arrays = []

    def term(self, piece):
        array, place = piece
        for number, known in enumerate(self.arrays):
            if known is array:
                return number, place
        self.arrays.append(array)
        return len(self.arrays) - 1, place


def couple_kernel(transposed, terms, high_ref, low_ref, *refs):
    n_in = 1 + max(number for number, _ in terms)
    ins, outs = refs[:n_in], refs[n_in:]
    block = ins[0].shape[-1]
    joined = jnp.concatenate([read(term, ins) for term in terms], axis=1)
    result = product(halves(joined), (high_ref[...], low_ref[...]), transposed)
    pieces = [result[:, at : at + block] for at in range(0, result.shape[1], block)]
    if len(outs) == 1:
        write(outs[0], pieces)
    else:
        for ref, piece in zip(outs, pieces):
            ref[...] = piece


def couple(pieces, high, low, transposed):
    operands = Operands()
    terms = [operands.term(piece) for piece in pieces]
    rows, block = operands.arrays[0].shape[-2:]
    n_out = high.shape[0 if transposed else 1] // block
    shapes = [(n_out, rows, block)] if transposed else [(rows, block)] * n_out
    whole = pl.BlockSpec(memory_space=VMEM)
    return pl.pallas_call(
        functools.partial(couple_kernel, transposed, terms),
        out_shape=[jax.ShapeDtypeStruct(shape, jnp.float32) for shape in shapes],
        in_specs=[whole] * (2 + len(operands.arrays)),
        out_specs=[whole] * len(shapes),
        compiler_params=pltpu.CompilerParams(vmem_limit_bytes=16 * MIB),
        cost_estimate=pl.CostEstimate(
            flops=6 * rows * high.size, bytes_accessed=4 * high.size, transcendentals=0
        ),
        name="couple_up" if not transposed else "couple_down",
    )(high, low, *operands.arrays)


def first_solve_kernel(right_ref, inverse_ref, out_ref, right, inverse, arrived):
    fetches = [
        pltpu.make_async_copy(right_ref.at[0], right, arrived.at[0]),
        pltpu.make_async_copy(inverse_ref.at[0], inverse, arrived.at[1]),
    ]
    for fetch in fetches:
        fetch.start()
    for fetch in fetches:
        fetch.wait()
    out_ref[...] = product(halves(right[...]), halves(inverse[...]), False)


def first_solve(right, inverse):
    rows, block = right.shape[-2:]
    return pl.pallas_call(
        first_solve_kernel,
        out_shape=jax.ShapeDtypeStruct((rows, block), jnp.float32),
        in_specs=[pl.BlockSpec(memory_space=pl.ANY)] * 2,
        out_specs=pl.BlockSpec(memory_space=VMEM),
        scratch_shapes=[
            pltpu.VMEM((rows, block), jnp.float32),
            pltpu.VMEM((block, block), jnp.float32),
            pltpu.SemaphoreType.DMA((2,)),
        ],
        compiler_params=pltpu.CompilerParams(vmem_limit_bytes=60 * MIB),
        name="first_solve",
    )(right, inverse)


def solve_kernel(transposed, level, terms, n_ins, *refs):
    right_ref, inverse_ref = refs[:2]
    ins, out_ref = refs[2 : 2 + n_ins], refs[-1]
    value = right_ref[level] if len(right_ref.shape) == 3 else right_ref[...]
    if terms:
        value -= total_of(terms, ins)
    out_ref[...] = product(halves(value), halves(inverse_ref[level]), transposed)


def solve(right, inverse, level, pieces, transposed, after=()):
    rows, block = right.shape[-2:]
    operands = Operands()
    terms = [operands.term(piece) for piece in pieces]
    whole = pl.BlockSpec(memory_space=VMEM)
    return pl.pallas_call(
        functools.partial(solve_kernel, transposed, level, terms, len(operands.arrays)),
        out_shape=jax.ShapeDtypeStruct((rows, block), jnp.float32),
        in_specs=[whole] * (2 + len(operands.arrays))
        + [pl.BlockSpec(memory_space=pl.ANY)] * len(after),
        out_specs=whole,
        compiler_params=pltpu.CompilerParams(vmem_limit_bytes=8 * MIB),
        cost_estimate=pl.CostEstimate(
            flops=6 * rows * block * block, bytes_accessed=4 * block * block, transcendentals=0
        ),
        name="solve_up" if not transposed else "solve_down",
    )(right, inverse, *operands.arrays, *after)


def combine_kernel(sums, n_ins, *refs):
    ins, outs = refs[:n_ins], refs[-len(sums) :]
    for terms, ref in zip(sums, outs):
        write(ref, [total_of(entry, ins) for entry in terms])


def combine(sums, after=()):
    operands = Operands()
    sums = [[[operands.term(piece) for piece in entry] for entry in entries] for entries in sums]
    rows, block = operands.arrays[0].shape[-2:]
    whole = pl.BlockSpec(memory_space=VMEM)
    shapes = [(rows, block) if len(e) == 1 else (len(e), rows, block) for e in sums]
    return pl.pallas_call(
        functools.partial(combine_kernel, sums, len(operands.arrays)),
        out_shape=[jax.ShapeDtypeStruct(shape, jnp.float32) for shape in shapes],
        in_specs=[whole] * len(operands.arrays)
        + [pl.BlockSpec(memory_space=pl.ANY)] * len(after),
        out_specs=[whole] * len(sums),
        compiler_params=pltpu.CompilerParams(vmem_limit_bytes=8 * MIB),
        cost_estimate=pl.CostEstimate(
            flops=rows * block, bytes_accessed=4 * rows * block, transcendentals=0
        ),
        name="combine",
    )(*operands.arrays, *after)


def stack_kernel(n_forward, *refs):
    ins, (forward_ref, backward_ref) = refs[:-2], refs[-2:]
    write(forward_ref, [ref[...] for ref in ins[:n_forward]])
    write(backward_ref, [ref[...] for ref in ins[n_forward:]])


def stack(forward, backward):
    whole = pl.BlockSpec(memory_space=VMEM)
    shape = jax.ShapeDtypeStruct((len(forward),) + forward[0].shape, jnp.float32)
    return pl.pallas_call(
        functools.partial(stack_kernel, len(forward)),
        out_shape=[shape, shape],
        in_specs=[whole] * (2 * len(forward)),
        out_specs=[whole] * 2,
        compiler_params=pltpu.CompilerParams(vmem_limit_bytes=8 * MIB),
        name="stack",
    )(*forward, *backward)


def near_exchange(stacked, axis):
    half = lax.axis_size(axis) // 2
    groups = [list(range(half)), list(range(half, 2 * half))]
    return lax.all_to_all(stacked, axis, 0, 0, axis_index_groups=groups, tiled=True)


def far_exchange(segment, axis):
    size = lax.axis_size(axis)
    return lax.ppermute(segment, axis, [(i, i ^ (size // 2)) for i in range(size)])


def gather_row(segment, after):
    half = lax.axis_size("row") // 2
    received = far_exchange(segment, "row")
    (stacked,) = combine([[[(segment, None)], [(received, None)]] * half], after)
    received = near_exchange(stacked, "row")
    return [(received, place) for place in range(2 * half)]


def deliver_row(stacked):
    half = lax.axis_size("row") // 2
    received = near_exchange(stacked, "row")
    mine, other = combine(
        [[[(received, 2 * place + side) for place in range(half)]] for side in range(2)]
    )
    return [(mine, None), (far_exchange(other, "row"), None)]


def exchange_each(messages, axis):
    size = lax.axis_size(axis)
    received = [messages[0]] + [
        lax.ppermute(messages[d], axis, [(i, i ^ d) for i in range(size)])
        for d in range(1, size)
    ]
    return [(message, None) for message in received]


def direct_shards(rhs, diag_inv, blocks, blk_target, blk_source, blk_count):
    levels = rhs.shape[0]
    n_row, n_col = lax.axis_size("row"), lax.axis_size("col")
    right = rhs.reshape((levels,) + rhs.shape[-2:])
    inverse = diag_inv.reshape((levels,) + diag_inv.shape[-2:])
    weights = blocks.reshape((levels - 1,) + blocks.shape[-3:])
    target = blk_target.reshape(levels - 1, -1)
    source = blk_source.reshape(levels - 1, -1)
    count = blk_count.reshape(levels - 1)
    place = jnp.stack([lax.axis_index("row"), lax.axis_index("col")]).astype(jnp.int32)
    gather = lambda level, after: gather_blocks(
        level, target, source, count, place, weights, n_row, n_col, after
    )
    forward = [first_solve(right, inverse)]
    total = gather(0, forward[:1])
    coupling = []
    for level in range(1, levels):
        coupling.append(split(total, n_row, n_col, forward[-1:]))
        pieces = gather_row(forward[-1], coupling[-1][:1])
        partial = couple(pieces, *coupling[-1], False)
        after = ()
        if level < levels - 1:
            total = gather(level, partial[:1])
            after = (total,)
        pieces = exchange_each(partial, "col")
        forward.append(solve(right, inverse, level, pieces, False, after))
    backward = [None] * levels
    backward[-1] = solve(forward[-1], inverse, levels - 1, [], True)
    for level in range(levels - 2, -1, -1):
        pieces = exchange_each([backward[level + 1]] * n_col, "col")
        (partial,) = couple(pieces, *coupling[level], True)
        backward[level] = solve(forward[level], inverse, level, deliver_row(partial), True)
    outs = stack(forward, backward)
    return tuple(out.reshape(rhs.shape) for out in outs)


def fold_for(index, piece):
    entry_count = piece.shape[0]
    onehot = (index[:, None] == jnp.arange(entry_count, dtype=jnp.int32)[None, :]).astype(
        jnp.float32
    )
    return jnp.dot(
        onehot,
        piece.reshape(entry_count, -1),
        precision=HIGH_PRECISION,
        preferred_element_type=jnp.float32,
    )


def route_sum(index, entry_count, block_products, width):
    slot_count = block_products.shape[0]
    active_flags = jnp.arange(slot_count, dtype=jnp.int32) < entry_count
    routing_table = (
        (index[None, :] == jnp.arange(width, dtype=jnp.int32)[:, None]) & active_flags[None, :]
    ).astype(jnp.float32)
    return jnp.dot(
        routing_table,
        block_products.reshape(slot_count, -1),
        precision=HIGH_PRECISION,
        preferred_element_type=jnp.float32,
    )


def forward_level(previous, weight_matrix, target, source, entry_count):
    slot_count = weight_matrix.shape[0]
    slots, rhs_column_count, block_ordering = previous.shape
    selected_blocks = fold_for(source, lax.all_gather(previous, "row", axis=0, tiled=True))
    block_products = jnp.einsum(
        "ado,aon->adn",
        selected_blocks.reshape(slot_count, rhs_column_count, block_ordering),
        weight_matrix,
        precision=HIGH_PRECISION,
    )
    ncol = lax.axis_size("col")
    buckets = route_sum(target, entry_count, block_products, ncol * slots).reshape(
        ncol, slots, rhs_column_count, block_ordering
    )
    own = lax.psum_scatter(buckets, "col", scatter_dimension=0, tiled=True)[0]
    return own


def backward_level(upper, weight_matrix, target, source, entry_count):
    slot_count = weight_matrix.shape[0]
    slots, rhs_column_count, block_ordering = upper.shape
    selected_blocks = fold_for(target, lax.all_gather(upper, "col", axis=0, tiled=True))
    block_products = jnp.einsum(
        "mlv,mtv->mlt",
        selected_blocks.reshape(slot_count, rhs_column_count, block_ordering),
        weight_matrix,
        precision=HIGH_PRECISION,
    )
    nrow = lax.axis_size("row")
    buckets = route_sum(source, entry_count, block_products, nrow * slots).reshape(
        nrow, slots, rhs_column_count, block_ordering
    )
    own = lax.psum_scatter(buckets, "row", scatter_dimension=0, tiled=True)[0]
    return own


def shards(rhs, diag_inv, blocks, blk_target, blk_source, blk_count):
    levels = rhs.shape[0]
    right = rhs[:, 0, 0]
    inverse = diag_inv[:, 0, 0]
    weight_matrix = blocks[:, 0, 0]
    targets = blk_target[:, 0, 0]
    sources = blk_source[:, 0, 0]
    counts = blk_count[:, 0, 0]
    forward = [jnp.einsum("srb,sbc->src", right[0], inverse[0], precision=HIGH_PRECISION)]
    for level in range(1, levels):
        own = forward_level(
            forward[-1],
            weight_matrix[level - 1],
            targets[level - 1],
            sources[level - 1],
            counts[level - 1],
        )
        forward.append(
            jnp.einsum("srb,sbc->src", right[level] - own, inverse[level], precision=HIGH_PRECISION)
        )
    backward = [None] * levels
    backward[levels - 1] = jnp.einsum(
        "src,sbc->srb", forward[levels - 1], inverse[levels - 1], precision=HIGH_PRECISION
    )
    for level in range(levels - 2, -1, -1):
        own = backward_level(
            backward[level + 1], weight_matrix[level], targets[level], sources[level], counts[level]
        )
        backward[level] = jnp.einsum(
            "src,sbc->srb", forward[level] - own, inverse[level], precision=HIGH_PRECISION
        )
    forward_out = jnp.stack(forward)[:, None, None]
    backward_out = jnp.stack(backward)[:, None, None]
    return (forward_out, backward_out)


def solution(mesh):
    placed = (
        P(None, "row", "col", None, None, None),
        P(None, "row", "col", None, None, None),
        P(None, "row", "col", None, None, None),
        P(None, "row", "col", None),
        P(None, "row", "col", None),
        P(None, "row", "col"),
    )
    n_row, n_col = mesh.shape["row"], mesh.shape["col"]

    def local(rhs, diag_inv, blocks, blk_target, blk_source, blk_count):
        sizes = (n_row, n_col)
        dense = n_row * n_col <= blocks.shape[3] and rhs.shape[3] == 1
        even = all(size > 1 and size & (size - 1) == 0 for size in sizes)
        run = direct_shards if dense and even else shards
        return run(rhs, diag_inv, blocks, blk_target, blk_source, blk_count)

    return jax.shard_map(
        local,
        mesh=mesh,
        in_specs=placed,
        out_specs=(
            P(None, "row", "col", None, None, None),
            P(None, "row", "col", None, None, None),
        ),
        check_vma=False,
    )
```

```python
import functools

import jax
import jax.numpy as jnp
from jax import lax
from jax.experimental import pallas as pl
from jax.experimental.pallas import tpu as pltpu
from jax.sharding import PartitionSpec as P

HIGH_PRECISION = lax.Precision.HIGHEST
MIB = 1024 * 1024
VMEM = pltpu.MemorySpace.VMEM
SMEM = pltpu.MemorySpace.SMEM


def halves(value):
    high = value.astype(jnp.bfloat16)
    low = (value - high.astype(jnp.float32)).astype(jnp.bfloat16)
    return high, low


def product(left, right, transposed):
    contract = (((1,), (1 if transposed else 0,)), ((), ()))
    dot = functools.partial(
        lax.dot_general, dimension_numbers=contract, preferred_element_type=jnp.float32
    )
    return dot(left[0], right[0]) + (dot(left[0], right[1]) + dot(left[1], right[0]))


def gather_blocks_kernel(
    n_row, n_col, level, chunk, target_ref, source_ref, count_ref, place_ref, blocks_ref, *refs
):
    total, slots, arrived = refs[-3:]
    count = count_ref[level, 0, 0]
    half = n_row // 2
    side = place_ref[0] // half

    def fetch(number):
        span = pl.ds(number * chunk, chunk)
        return pltpu.make_async_copy(
            blocks_ref.at[level, span], slots.at[span], arrived.at[number]
        )

    for number in range(arrived.shape[0]):
        pl.when(number * chunk < count)(fetch(number).start)
    total[...] = jnp.zeros_like(total)

    def add(slot, carry):
        pl.when(lax.rem(slot, chunk) == 0)(fetch(slot // chunk).wait)
        source = source_ref[level, 0, 0, slot]
        near = lax.rem(source, half) ^ lax.rem(place_ref[0], half)
        below = near * 2 + ((source // half) ^ side)
        above = target_ref[level, 0, 0, slot] ^ place_ref[1]
        total[below * n_col + above] += slots[slot]
        return carry

    lax.fori_loop(0, count, add, 0)


def gather_blocks(level, target, source, count, place, blocks, n_row, n_col, after):
    slot_count, block = blocks.shape[1], blocks.shape[2]
    chunk = max(1, slot_count // 4)
    shape = (n_row * n_col, block, block)
    scalars = pl.BlockSpec(memory_space=SMEM)
    return pl.pallas_call(
        functools.partial(gather_blocks_kernel, n_row, n_col, level, chunk),
        out_shape=jax.ShapeDtypeStruct(shape, jnp.float32),
        in_specs=[scalars] * 4 + [pl.BlockSpec(memory_space=pl.ANY)] * (1 + len(after)),
        out_specs=pl.BlockSpec(memory_space=VMEM),
        scratch_shapes=[
            pltpu.VMEM((slot_count, block, block), jnp.float32),
            pltpu.SemaphoreType.DMA((slot_count // chunk,)),
        ],
        compiler_params=pltpu.CompilerParams(vmem_limit_bytes=(51 if level == 0 else 16) * MIB),
        cost_estimate=pl.CostEstimate(
            flops=slot_count * block * block,
            bytes_accessed=8 * slot_count * block * block,
            transcendentals=0,
        ),
        name=f"gather_blocks_{level}",
    )(target, source, count, place, blocks, *after)


def split_kernel(n_col, total_ref, *refs):
    high_ref, low_ref = refs[-2:]
    block = total_ref.shape[-1]
    for pair in range(total_ref.shape[0]):
        rows = pl.ds(pair // n_col * block, block)
        lanes = pl.ds(pair % n_col * block, block)
        high, low = halves(total_ref[pair])
        high_ref[rows, lanes] = high
        low_ref[rows, lanes] = low


def split(total, n_row, n_col, after):
    block = total.shape[-1]
    shape = jax.ShapeDtypeStruct((n_row * block, n_col * block), jnp.bfloat16)
    whole = pl.BlockSpec(memory_space=VMEM)
    return pl.pallas_call(
        functools.partial(split_kernel, n_col),
        out_shape=[shape, shape],
        in_specs=[whole] + [pl.BlockSpec(memory_space=pl.ANY)] * len(after),
        out_specs=[whole, whole],
        compiler_params=pltpu.CompilerParams(vmem_limit_bytes=8 * MIB),
        cost_estimate=pl.CostEstimate(
            flops=3 * total.size, bytes_accessed=8 * total.size, transcendentals=0
        ),
        name="split",
    )(total, *after)


def read(term, refs):
    number, place = term
    return refs[number][...] if place is None else refs[number][place]


def total_of(terms, refs):
    value = read(terms[0], refs)
    for term in terms[1:]:
        value += read(term, refs)
    return value


def write(ref, values):
    if len(ref.shape) == 2:
        ref[...] = values[0]
    else:
        for place, value in enumerate(values):
            ref[place] = value


class Operands:
    def __init__(self):
        self.arrays = []

    def term(self, piece):
        array, place = piece
        for number, known in enumerate(self.arrays):
            if known is array:
                return number, place
        self.arrays.append(array)
        return len(self.arrays) - 1, place


def couple_kernel(transposed, terms, span, high_ref, low_ref, *refs):
    n_in = 1 + max(number for number, _ in terms)
    ins, outs = refs[:n_in], refs[n_in:]
    block = ins[0].shape[-1]
    joined = jnp.concatenate([read(term, ins) for term in terms], axis=1)
    wanted = pl.ds(span[0] * block, (span[1] - span[0]) * block)
    chosen = (wanted, slice(None)) if transposed else (slice(None), wanted)
    result = product(halves(joined), (high_ref[chosen], low_ref[chosen]), transposed)
    pieces = [result[:, at : at + block] for at in range(0, result.shape[1], block)]
    each = len(pieces) // len(outs)
    for number, ref in enumerate(outs):
        write(ref, pieces[number * each : (number + 1) * each])


def couple(pieces, high, low, transposed, span, each):
    operands = Operands()
    terms = [operands.term(piece) for piece in pieces]
    rows, block = operands.arrays[0].shape[-2:]
    shape = (rows, block) if each == 1 else (each, rows, block)
    n_out = (span[1] - span[0]) // each
    whole = pl.BlockSpec(memory_space=VMEM)
    work = rows * block * block * len(terms) * (span[1] - span[0])
    return pl.pallas_call(
        functools.partial(couple_kernel, transposed, terms, span),
        out_shape=[jax.ShapeDtypeStruct(shape, jnp.float32)] * n_out,
        in_specs=[whole] * (2 + len(operands.arrays)),
        out_specs=[whole] * n_out,
        compiler_params=pltpu.CompilerParams(vmem_limit_bytes=16 * MIB),
        cost_estimate=pl.CostEstimate(
            flops=6 * work, bytes_accessed=4 * work // rows, transcendentals=0
        ),
        name="couple_up" if not transposed else "couple_down",
    )(high, low, *operands.arrays)


def first_solve_kernel(right_ref, inverse_ref, out_ref, right, inverse, arrived):
    fetches = [
        pltpu.make_async_copy(right_ref.at[0], right, arrived.at[0]),
        pltpu.make_async_copy(inverse_ref.at[0], inverse, arrived.at[1]),
    ]
    for fetch in fetches:
        fetch.start()
    for fetch in fetches:
        fetch.wait()
    out_ref[...] = product(halves(right[...]), halves(inverse[...]), False)


def first_solve(right, inverse):
    rows, block = right.shape[-2:]
    return pl.pallas_call(
        first_solve_kernel,
        out_shape=jax.ShapeDtypeStruct((rows, block), jnp.float32),
        in_specs=[pl.BlockSpec(memory_space=pl.ANY)] * 2,
        out_specs=pl.BlockSpec(memory_space=VMEM),
        scratch_shapes=[
            pltpu.VMEM((rows, block), jnp.float32),
            pltpu.VMEM((block, block), jnp.float32),
            pltpu.SemaphoreType.DMA((2,)),
        ],
        compiler_params=pltpu.CompilerParams(vmem_limit_bytes=60 * MIB),
        name="first_solve",
    )(right, inverse)


def solve_kernel(transposed, level, terms, n_ins, *refs):
    right_ref, inverse_ref = refs[:2]
    ins, out_ref = refs[2 : 2 + n_ins], refs[-1]
    value = right_ref[level] if len(right_ref.shape) == 3 else right_ref[...]
    if terms:
        value -= total_of(terms, ins)
    out_ref[...] = product(halves(value), halves(inverse_ref[level]), transposed)


def solve(right, inverse, level, pieces, transposed, after=()):
    rows, block = right.shape[-2:]
    operands = Operands()
    terms = [operands.term(piece) for piece in pieces]
    whole = pl.BlockSpec(memory_space=VMEM)
    return pl.pallas_call(
        functools.partial(solve_kernel, transposed, level, terms, len(operands.arrays)),
        out_shape=jax.ShapeDtypeStruct((rows, block), jnp.float32),
        in_specs=[whole] * (2 + len(operands.arrays))
        + [pl.BlockSpec(memory_space=pl.ANY)] * len(after),
        out_specs=whole,
        compiler_params=pltpu.CompilerParams(vmem_limit_bytes=8 * MIB),
        cost_estimate=pl.CostEstimate(
            flops=6 * rows * block * block, bytes_accessed=4 * block * block, transcendentals=0
        ),
        name="solve_up" if not transposed else "solve_down",
    )(right, inverse, *operands.arrays, *after)


def combine_kernel(sums, n_ins, *refs):
    ins, outs = refs[:n_ins], refs[-len(sums) :]
    for terms, ref in zip(sums, outs):
        write(ref, [total_of(entry, ins) for entry in terms])


def combine(sums, after=()):
    operands = Operands()
    sums = [[[operands.term(piece) for piece in entry] for entry in entries] for entries in sums]
    rows, block = operands.arrays[0].shape[-2:]
    whole = pl.BlockSpec(memory_space=VMEM)
    shapes = [(rows, block) if len(e) == 1 else (len(e), rows, block) for e in sums]
    return pl.pallas_call(
        functools.partial(combine_kernel, sums, len(operands.arrays)),
        out_shape=[jax.ShapeDtypeStruct(shape, jnp.float32) for shape in shapes],
        in_specs=[whole] * len(operands.arrays)
        + [pl.BlockSpec(memory_space=pl.ANY)] * len(after),
        out_specs=[whole] * len(sums),
        compiler_params=pltpu.CompilerParams(vmem_limit_bytes=8 * MIB),
        cost_estimate=pl.CostEstimate(
            flops=rows * block, bytes_accessed=4 * rows * block, transcendentals=0
        ),
        name="combine",
    )(*operands.arrays, *after)


def stack_kernel(n_forward, *refs):
    ins, (forward_ref, backward_ref) = refs[:-2], refs[-2:]
    write(forward_ref, [ref[...] for ref in ins[:n_forward]])
    write(backward_ref, [ref[...] for ref in ins[n_forward:]])


def stack(forward, backward):
    whole = pl.BlockSpec(memory_space=VMEM)
    shape = jax.ShapeDtypeStruct((len(forward),) + forward[0].shape, jnp.float32)
    return pl.pallas_call(
        functools.partial(stack_kernel, len(forward)),
        out_shape=[shape, shape],
        in_specs=[whole] * (2 * len(forward)),
        out_specs=[whole] * 2,
        compiler_params=pltpu.CompilerParams(vmem_limit_bytes=8 * MIB),
        name="stack",
    )(*forward, *backward)


def far_exchange(segment, axis):
    size = lax.axis_size(axis)
    return lax.ppermute(segment, axis, [(i, i ^ (size // 2)) for i in range(size)])


def gather_row(segment, after):
    half = lax.axis_size("row") // 2
    received = far_exchange(segment, "row")
    (both,) = combine([[[(segment, None)], [(received, None)]]], after)
    messages = exchange_each([both] * half, "row")
    return [(message, side) for message in messages for side in range(2)]


def deliver_row(messages):
    received = exchange_each(messages, "row")
    mine, other = combine(
        [[[(message, side) for message in received]] for side in range(2)]
    )
    return [(mine, None), (far_exchange(other, "row"), None)]


def exchange_each(messages, axis):
    size = lax.axis_size(axis)
    received = {0: messages[0]}
    for d in reversed(range(1, len(messages))):
        received[d] = lax.ppermute(messages[d], axis, [(i, i ^ d) for i in range(size)])
    return [received[d] for d in range(len(messages))]


def direct_shards(rhs, diag_inv, blocks, blk_target, blk_source, blk_count):
    levels = rhs.shape[0]
    n_row, n_col = lax.axis_size("row"), lax.axis_size("col")
    right = rhs.reshape((levels,) + rhs.shape[-2:])
    inverse = diag_inv.reshape((levels,) + diag_inv.shape[-2:])
    weights = blocks.reshape((levels - 1,) + blocks.shape[-3:])
    place = jnp.stack([lax.axis_index("row"), lax.axis_index("col")]).astype(jnp.int32)
    gather = lambda level, after: gather_blocks(
        level, blk_target, blk_source, blk_count, place, weights, n_row, n_col, after
    )
    plain = lambda messages: [(message, None) for message in messages]
    forward = [first_solve(right, inverse)]
    total = gather(0, ())
    coupling = []
    for level in range(1, levels):
        coupling.append(split(total, n_row, n_col, forward[-1:] if level > 1 else ()))
        pieces = gather_row(forward[-1], coupling[-1][:1])
        far = couple(pieces, *coupling[-1], False, (n_col // 2, n_col), 1)
        near = couple(pieces, *coupling[-1], False, (0, n_col // 2), 1)
        after = ()
        if level < levels - 1:
            total = gather(level, near[:1])
            after = (total,)
        pieces = plain(exchange_each(near + far, "col"))
        forward.append(solve(right, inverse, level, pieces, False, after))
    backward = [None] * levels
    backward[-1] = solve(forward[-1], inverse, levels - 1, [], True)
    for level in range(levels - 2, -1, -1):
        pieces = plain(exchange_each([backward[level + 1]] * n_col, "col"))
        sent = couple(pieces, *coupling[level], True, (2, n_row), 2)
        kept = couple(pieces, *coupling[level], True, (0, 2), 2)
        pieces = deliver_row(kept + sent)
        backward[level] = solve(forward[level], inverse, level, pieces, True)
    outs = stack(forward, backward)
    return tuple(out.reshape(rhs.shape) for out in outs)


def fold_for(index, piece):
    entry_count = piece.shape[0]
    onehot = (index[:, None] == jnp.arange(entry_count, dtype=jnp.int32)[None, :]).astype(
        jnp.float32
    )
    return jnp.dot(
        onehot,
        piece.reshape(entry_count, -1),
        precision=HIGH_PRECISION,
        preferred_element_type=jnp.float32,
    )


def route_sum(index, entry_count, block_products, width):
    slot_count = block_products.shape[0]
    active_flags = jnp.arange(slot_count, dtype=jnp.int32) < entry_count
    routing_table = (
        (index[None, :] == jnp.arange(width, dtype=jnp.int32)[:, None]) & active_flags[None, :]
    ).astype(jnp.float32)
    return jnp.dot(
        routing_table,
        block_products.reshape(slot_count, -1),
        precision=HIGH_PRECISION,
        preferred_element_type=jnp.float32,
    )


def forward_level(previous, weight_matrix, target, source, entry_count):
    slot_count = weight_matrix.shape[0]
    slots, rhs_column_count, block_ordering = previous.shape
    selected_blocks = fold_for(source, lax.all_gather(previous, "row", axis=0, tiled=True))
    block_products = jnp.einsum(
        "ado,aon->adn",
        selected_blocks.reshape(slot_count, rhs_column_count, block_ordering),
        weight_matrix,
        precision=HIGH_PRECISION,
    )
    ncol = lax.axis_size("col")
    buckets = route_sum(target, entry_count, block_products, ncol * slots).reshape(
        ncol, slots, rhs_column_count, block_ordering
    )
    own = lax.psum_scatter(buckets, "col", scatter_dimension=0, tiled=True)[0]
    return own


def backward_level(upper, weight_matrix, target, source, entry_count):
    slot_count = weight_matrix.shape[0]
    slots, rhs_column_count, block_ordering = upper.shape
    selected_blocks = fold_for(target, lax.all_gather(upper, "col", axis=0, tiled=True))
    block_products = jnp.einsum(
        "mlv,mtv->mlt",
        selected_blocks.reshape(slot_count, rhs_column_count, block_ordering),
        weight_matrix,
        precision=HIGH_PRECISION,
    )
    nrow = lax.axis_size("row")
    buckets = route_sum(source, entry_count, block_products, nrow * slots).reshape(
        nrow, slots, rhs_column_count, block_ordering
    )
    own = lax.psum_scatter(buckets, "row", scatter_dimension=0, tiled=True)[0]
    return own


def shards(rhs, diag_inv, blocks, blk_target, blk_source, blk_count):
    levels = rhs.shape[0]
    right = rhs[:, 0, 0]
    inverse = diag_inv[:, 0, 0]
    weight_matrix = blocks[:, 0, 0]
    targets = blk_target[:, 0, 0]
    sources = blk_source[:, 0, 0]
    counts = blk_count[:, 0, 0]
    forward = [jnp.einsum("srb,sbc->src", right[0], inverse[0], precision=HIGH_PRECISION)]
    for level in range(1, levels):
        own = forward_level(
            forward[-1],
            weight_matrix[level - 1],
            targets[level - 1],
            sources[level - 1],
            counts[level - 1],
        )
        forward.append(
            jnp.einsum("srb,sbc->src", right[level] - own, inverse[level], precision=HIGH_PRECISION)
        )
    backward = [None] * levels
    backward[levels - 1] = jnp.einsum(
        "src,sbc->srb", forward[levels - 1], inverse[levels - 1], precision=HIGH_PRECISION
    )
    for level in range(levels - 2, -1, -1):
        own = backward_level(
            backward[level + 1], weight_matrix[level], targets[level], sources[level], counts[level]
        )
        backward[level] = jnp.einsum(
            "src,sbc->srb", forward[level] - own, inverse[level], precision=HIGH_PRECISION
        )
    forward_out = jnp.stack(forward)[:, None, None]
    backward_out = jnp.stack(backward)[:, None, None]
    return (forward_out, backward_out)


def solution(mesh):
    placed = (
        P(None, "row", "col", None, None, None),
        P(None, "row", "col", None, None, None),
        P(None, "row", "col", None, None, None),
        P(None, "row", "col", None),
        P(None, "row", "col", None),
        P(None, "row", "col"),
    )
    n_row, n_col = mesh.shape["row"], mesh.shape["col"]

    def local(rhs, diag_inv, blocks, blk_target, blk_source, blk_count):
        sizes = (n_row, n_col)
        dense = n_row * n_col <= blocks.shape[3] and rhs.shape[3] == 1
        even = all(size > 1 and size & (size - 1) == 0 for size in sizes)
        run = direct_shards if dense and even else shards
        return run(rhs, diag_inv, blocks, blk_target, blk_source, blk_count)

    return jax.shard_map(
        local,
        mesh=mesh,
        in_specs=placed,
        out_specs=(
            P(None, "row", "col", None, None, None),
            P(None, "row", "col", None, None, None),
        ),
        check_vma=False,
    )
```

```python
import functools

import jax
import jax.numpy as jnp
from jax import lax
from jax.experimental import pallas as pl
from jax.experimental.pallas import tpu as pltpu
from jax.sharding import PartitionSpec as P

HIGH_PRECISION = lax.Precision.HIGHEST
MIB = 1024 * 1024
VMEM = pltpu.MemorySpace.VMEM
SMEM = pltpu.MemorySpace.SMEM


def halves(value):
    high = value.astype(jnp.bfloat16)
    low = (value - high.astype(jnp.float32)).astype(jnp.bfloat16)
    return high, low


def product(left, right, transposed):
    contract = (((1,), (1 if transposed else 0,)), ((), ()))
    dot = functools.partial(
        lax.dot_general, dimension_numbers=contract, preferred_element_type=jnp.float32
    )
    return dot(left[0], right[0]) + (dot(left[0], right[1]) + dot(left[1], right[0]))


def gather_blocks_kernel(
    n_row, n_col, level, chunk, target_ref, source_ref, count_ref, place_ref, blocks_ref, *refs
):
    total, slots, arrived = refs[-3:]
    count = count_ref[level, 0, 0]
    half = n_row // 2
    side = place_ref[0] // half

    def fetch(number):
        span = pl.ds(number * chunk, chunk)
        return pltpu.make_async_copy(
            blocks_ref.at[level, span], slots.at[span], arrived.at[number]
        )

    for number in range(arrived.shape[0]):
        pl.when(number * chunk < count)(fetch(number).start)
    total[...] = jnp.zeros_like(total)

    def add(slot, carry):
        pl.when(lax.rem(slot, chunk) == 0)(fetch(slot // chunk).wait)
        source = source_ref[level, 0, 0, slot]
        near = lax.rem(source, half) ^ lax.rem(place_ref[0], half)
        below = ((source // half) ^ side) * half + near
        above = target_ref[level, 0, 0, slot] ^ place_ref[1]
        total[below * n_col + above] += slots[slot]
        return carry

    lax.fori_loop(0, count, add, 0)


def gather_blocks(level, target, source, count, place, blocks, n_row, n_col, after):
    slot_count, block = blocks.shape[1], blocks.shape[2]
    chunk = max(1, slot_count // 4)
    shape = (n_row * n_col, block, block)
    scalars = pl.BlockSpec(memory_space=SMEM)
    return pl.pallas_call(
        functools.partial(gather_blocks_kernel, n_row, n_col, level, chunk),
        out_shape=jax.ShapeDtypeStruct(shape, jnp.float32),
        in_specs=[scalars] * 4 + [pl.BlockSpec(memory_space=pl.ANY)] * (1 + len(after)),
        out_specs=pl.BlockSpec(memory_space=VMEM),
        scratch_shapes=[
            pltpu.VMEM((slot_count, block, block), jnp.float32),
            pltpu.SemaphoreType.DMA((slot_count // chunk,)),
        ],
        compiler_params=pltpu.CompilerParams(vmem_limit_bytes=(51 if level == 0 else 16) * MIB),
        cost_estimate=pl.CostEstimate(
            flops=slot_count * block * block,
            bytes_accessed=8 * slot_count * block * block,
            transcendentals=0,
        ),
        name=f"gather_blocks_{level}",
    )(target, source, count, place, blocks, *after)


def split_kernel(n_col, total_ref, high_ref, low_ref):
    block = total_ref.shape[-1]
    for pair in range(total_ref.shape[0]):
        rows = pl.ds(pair // n_col * block, block)
        lanes = pl.ds(pair % n_col * block, block)
        high, low = halves(total_ref[pair])
        high_ref[rows, lanes] = high
        low_ref[rows, lanes] = low


def split(total, n_row, n_col):
    block = total.shape[-1]
    shape = jax.ShapeDtypeStruct((n_row * block, n_col * block), jnp.bfloat16)
    whole = pl.BlockSpec(memory_space=VMEM)
    return pl.pallas_call(
        functools.partial(split_kernel, n_col),
        out_shape=[shape, shape],
        in_specs=[whole],
        out_specs=[whole, whole],
        compiler_params=pltpu.CompilerParams(vmem_limit_bytes=8 * MIB),
        cost_estimate=pl.CostEstimate(
            flops=3 * total.size, bytes_accessed=8 * total.size, transcendentals=0
        ),
        name="split",
    )(total)


def read(term, refs):
    number, place = term
    return refs[number][...] if place is None else refs[number][place]


def total_of(terms, refs):
    value = read(terms[0], refs)
    for term in terms[1:]:
        value += read(term, refs)
    return value


def write(ref, values):
    if len(ref.shape) == 2:
        ref[...] = values[0]
    else:
        for place, value in enumerate(values):
            ref[place] = value


class Operands:
    def __init__(self):
        self.arrays = []

    def term(self, piece):
        array, place = piece
        for number, known in enumerate(self.arrays):
            if known is array:
                return number, place
        self.arrays.append(array)
        return len(self.arrays) - 1, place


def couple_kernel(transposed, terms, span, high_ref, low_ref, *refs):
    n_in = 1 + max(number for number, _ in terms)
    ins, outs = refs[:n_in], refs[n_in:]
    block = ins[0].shape[-1]
    joined = jnp.concatenate([read(term, ins) for term in terms], axis=1)
    wanted = pl.ds(span[0] * block, (span[1] - span[0]) * block)
    chosen = (wanted, slice(None)) if transposed else (slice(None), wanted)
    result = product(halves(joined), (high_ref[chosen], low_ref[chosen]), transposed)
    pieces = [result[:, at : at + block] for at in range(0, result.shape[1], block)]
    each = len(pieces) // len(outs)
    for number, ref in enumerate(outs):
        write(ref, pieces[number * each : (number + 1) * each])


def couple(pieces, high, low, transposed, span, each):
    operands = Operands()
    terms = [operands.term(piece) for piece in pieces]
    rows, block = operands.arrays[0].shape[-2:]
    shape = (rows, block) if each == 1 else (each, rows, block)
    n_out = (span[1] - span[0]) // each
    whole = pl.BlockSpec(memory_space=VMEM)
    work = rows * block * block * len(terms) * (span[1] - span[0])
    return pl.pallas_call(
        functools.partial(couple_kernel, transposed, terms, span),
        out_shape=[jax.ShapeDtypeStruct(shape, jnp.float32)] * n_out,
        in_specs=[whole] * (2 + len(operands.arrays)),
        out_specs=[whole] * n_out,
        compiler_params=pltpu.CompilerParams(vmem_limit_bytes=16 * MIB),
        cost_estimate=pl.CostEstimate(
            flops=6 * work, bytes_accessed=4 * work // rows, transcendentals=0
        ),
        name="couple_up" if not transposed else "couple_down",
    )(high, low, *operands.arrays)


def first_solve_kernel(right_ref, inverse_ref, out_ref, right, inverse, arrived):
    fetches = [
        pltpu.make_async_copy(right_ref.at[0], right, arrived.at[0]),
        pltpu.make_async_copy(inverse_ref.at[0], inverse, arrived.at[1]),
    ]
    for fetch in fetches:
        fetch.start()
    for fetch in fetches:
        fetch.wait()
    out_ref[...] = product(halves(right[...]), halves(inverse[...]), False)


def first_solve(right, inverse):
    rows, block = right.shape[-2:]
    return pl.pallas_call(
        first_solve_kernel,
        out_shape=jax.ShapeDtypeStruct((rows, block), jnp.float32),
        in_specs=[pl.BlockSpec(memory_space=pl.ANY)] * 2,
        out_specs=pl.BlockSpec(memory_space=VMEM),
        scratch_shapes=[
            pltpu.VMEM((rows, block), jnp.float32),
            pltpu.VMEM((block, block), jnp.float32),
            pltpu.SemaphoreType.DMA((2,)),
        ],
        compiler_params=pltpu.CompilerParams(vmem_limit_bytes=60 * MIB),
        name="first_solve",
    )(right, inverse)


def solve_kernel(transposed, level, terms, n_ins, *refs):
    right_ref, inverse_ref = refs[:2]
    ins, out_ref = refs[2 : 2 + n_ins], refs[-1]
    value = right_ref[level] if len(right_ref.shape) == 3 else right_ref[...]
    if terms:
        value -= total_of(terms, ins)
    out_ref[...] = product(halves(value), halves(inverse_ref[level]), transposed)


def solve(right, inverse, level, pieces, transposed, after=()):
    rows, block = right.shape[-2:]
    operands = Operands()
    terms = [operands.term(piece) for piece in pieces]
    whole = pl.BlockSpec(memory_space=VMEM)
    return pl.pallas_call(
        functools.partial(solve_kernel, transposed, level, terms, len(operands.arrays)),
        out_shape=jax.ShapeDtypeStruct((rows, block), jnp.float32),
        in_specs=[whole] * (2 + len(operands.arrays))
        + [pl.BlockSpec(memory_space=pl.ANY)] * len(after),
        out_specs=whole,
        compiler_params=pltpu.CompilerParams(vmem_limit_bytes=8 * MIB),
        cost_estimate=pl.CostEstimate(
            flops=6 * rows * block * block, bytes_accessed=4 * block * block, transcendentals=0
        ),
        name="solve_up" if not transposed else "solve_down",
    )(right, inverse, *operands.arrays, *after)


def combine_kernel(sums, n_ins, *refs):
    ins, outs = refs[:n_ins], refs[-len(sums) :]
    for terms, ref in zip(sums, outs):
        write(ref, [total_of(entry, ins) for entry in terms])


def combine(sums, after=()):
    operands = Operands()
    sums = [[[operands.term(piece) for piece in entry] for entry in entries] for entries in sums]
    rows, block = operands.arrays[0].shape[-2:]
    whole = pl.BlockSpec(memory_space=VMEM)
    shapes = [(rows, block) if len(e) == 1 else (len(e), rows, block) for e in sums]
    return pl.pallas_call(
        functools.partial(combine_kernel, sums, len(operands.arrays)),
        out_shape=[jax.ShapeDtypeStruct(shape, jnp.float32) for shape in shapes],
        in_specs=[whole] * len(operands.arrays)
        + [pl.BlockSpec(memory_space=pl.ANY)] * len(after),
        out_specs=[whole] * len(sums),
        compiler_params=pltpu.CompilerParams(vmem_limit_bytes=8 * MIB),
        cost_estimate=pl.CostEstimate(
            flops=rows * block, bytes_accessed=4 * rows * block, transcendentals=0
        ),
        name="combine",
    )(*operands.arrays, *after)


def stack_kernel(n_forward, *refs):
    ins, (forward_ref, backward_ref) = refs[:-2], refs[-2:]
    write(forward_ref, [ref[...] for ref in ins[:n_forward]])
    write(backward_ref, [ref[...] for ref in ins[n_forward:]])


def stack(forward, backward):
    whole = pl.BlockSpec(memory_space=VMEM)
    shape = jax.ShapeDtypeStruct((len(forward),) + forward[0].shape, jnp.float32)
    return pl.pallas_call(
        functools.partial(stack_kernel, len(forward)),
        out_shape=[shape, shape],
        in_specs=[whole] * (2 * len(forward)),
        out_specs=[whole] * 2,
        compiler_params=pltpu.CompilerParams(vmem_limit_bytes=8 * MIB),
        name="stack",
    )(*forward, *backward)


def far_exchange(segment, axis):
    size = lax.axis_size(axis)
    return lax.ppermute(segment, axis, [(i, i ^ (size // 2)) for i in range(size)])


def gather_row(segment, after):
    half = lax.axis_size("row") // 2
    received = far_exchange(segment, "row")
    (again,) = combine([[[(segment, None)]]], after)
    mine = exchange_each([segment] + [again] * (half - 1), "row")
    other = exchange_each([received] * half, "row")
    return plain(mine + other)


def deliver_row(mine, other):
    other = exchange_each(other, "row")
    (summed,) = combine([[plain([other[0], *reversed(other[1:])])]])
    far = far_exchange(summed, "row")
    later = combine([[[(message, None)]] for message in mine[1:-1]], (summed,))
    mine = exchange_each([mine[0], *later, mine[-1]], "row")
    (early,) = combine([[plain([far, mine[0], mine[-1]])]])
    return plain([early, *mine[1:-1]])


def plain(messages):
    return [(message, None) for message in messages]


def exchange_each(messages, axis):
    size = lax.axis_size(axis)
    received = {0: messages[0]}
    for d in reversed(range(1, len(messages))):
        received[d] = lax.ppermute(messages[d], axis, [(i, i ^ d) for i in range(size)])
    return [received[d] for d in range(len(messages))]


def direct_shards(rhs, diag_inv, blocks, blk_target, blk_source, blk_count):
    levels = rhs.shape[0]
    n_row, n_col = lax.axis_size("row"), lax.axis_size("col")
    right = rhs.reshape((levels,) + rhs.shape[-2:])
    inverse = diag_inv.reshape((levels,) + diag_inv.shape[-2:])
    weights = blocks.reshape((levels - 1,) + blocks.shape[-3:])
    place = jnp.stack([lax.axis_index("row"), lax.axis_index("col")]).astype(jnp.int32)
    gather = lambda level, after: gather_blocks(
        level, blk_target, blk_source, blk_count, place, weights, n_row, n_col, after
    )
    forward = [first_solve(right, inverse)]
    coupling = [split(gather(0, ()), n_row, n_col)]
    for level in range(1, levels):
        pieces = gather_row(forward[-1], coupling[-1][:1])
        far = couple(pieces, *coupling[level - 1], False, (n_col // 2, n_col), 1)
        near = couple(pieces, *coupling[level - 1], False, (0, n_col // 2), 1)
        after = ()
        if level < levels - 1:
            coupling.append(split(gather(level, near[:1]), n_row, n_col))
            after = coupling[-1][:1]
        pieces = plain(exchange_each(near + far, "col"))
        forward.append(solve(right, inverse, level, pieces, False, after))
    backward = [None] * levels
    backward[-1] = solve(forward[-1], inverse, levels - 1, [], True)
    for level in range(levels - 2, -1, -1):
        pieces = plain(exchange_each([backward[level + 1]] * n_col, "col"))
        half = n_row // 2
        other = couple(pieces, *coupling[level], True, (half, n_row), 1)
        mine = couple(pieces, *coupling[level], True, (0, half), 1)
        pieces = deliver_row(mine, other)
        backward[level] = solve(forward[level], inverse, level, pieces, True)
    outs = stack(forward, backward)
    return tuple(out.reshape(rhs.shape) for out in outs)


def fold_for(index, piece):
    entry_count = piece.shape[0]
    onehot = (index[:, None] == jnp.arange(entry_count, dtype=jnp.int32)[None, :]).astype(
        jnp.float32
    )
    return jnp.dot(
        onehot,
        piece.reshape(entry_count, -1),
        precision=HIGH_PRECISION,
        preferred_element_type=jnp.float32,
    )


def route_sum(index, entry_count, block_products, width):
    slot_count = block_products.shape[0]
    active_flags = jnp.arange(slot_count, dtype=jnp.int32) < entry_count
    routing_table = (
        (index[None, :] == jnp.arange(width, dtype=jnp.int32)[:, None]) & active_flags[None, :]
    ).astype(jnp.float32)
    return jnp.dot(
        routing_table,
        block_products.reshape(slot_count, -1),
        precision=HIGH_PRECISION,
        preferred_element_type=jnp.float32,
    )


def forward_level(previous, weight_matrix, target, source, entry_count):
    slot_count = weight_matrix.shape[0]
    slots, rhs_column_count, block_ordering = previous.shape
    selected_blocks = fold_for(source, lax.all_gather(previous, "row", axis=0, tiled=True))
    block_products = jnp.einsum(
        "ado,aon->adn",
        selected_blocks.reshape(slot_count, rhs_column_count, block_ordering),
        weight_matrix,
        precision=HIGH_PRECISION,
    )
    ncol = lax.axis_size("col")
    buckets = route_sum(target, entry_count, block_products, ncol * slots).reshape(
        ncol, slots, rhs_column_count, block_ordering
    )
    own = lax.psum_scatter(buckets, "col", scatter_dimension=0, tiled=True)[0]
    return own


def backward_level(upper, weight_matrix, target, source, entry_count):
    slot_count = weight_matrix.shape[0]
    slots, rhs_column_count, block_ordering = upper.shape
    selected_blocks = fold_for(target, lax.all_gather(upper, "col", axis=0, tiled=True))
    block_products = jnp.einsum(
        "mlv,mtv->mlt",
        selected_blocks.reshape(slot_count, rhs_column_count, block_ordering),
        weight_matrix,
        precision=HIGH_PRECISION,
    )
    nrow = lax.axis_size("row")
    buckets = route_sum(source, entry_count, block_products, nrow * slots).reshape(
        nrow, slots, rhs_column_count, block_ordering
    )
    own = lax.psum_scatter(buckets, "row", scatter_dimension=0, tiled=True)[0]
    return own


def shards(rhs, diag_inv, blocks, blk_target, blk_source, blk_count):
    levels = rhs.shape[0]
    right = rhs[:, 0, 0]
    inverse = diag_inv[:, 0, 0]
    weight_matrix = blocks[:, 0, 0]
    targets = blk_target[:, 0, 0]
    sources = blk_source[:, 0, 0]
    counts = blk_count[:, 0, 0]
    forward = [jnp.einsum("srb,sbc->src", right[0], inverse[0], precision=HIGH_PRECISION)]
    for level in range(1, levels):
        own = forward_level(
            forward[-1],
            weight_matrix[level - 1],
            targets[level - 1],
            sources[level - 1],
            counts[level - 1],
        )
        forward.append(
            jnp.einsum("srb,sbc->src", right[level] - own, inverse[level], precision=HIGH_PRECISION)
        )
    backward = [None] * levels
    backward[levels - 1] = jnp.einsum(
        "src,sbc->srb", forward[levels - 1], inverse[levels - 1], precision=HIGH_PRECISION
    )
    for level in range(levels - 2, -1, -1):
        own = backward_level(
            backward[level + 1], weight_matrix[level], targets[level], sources[level], counts[level]
        )
        backward[level] = jnp.einsum(
            "src,sbc->srb", forward[level] - own, inverse[level], precision=HIGH_PRECISION
        )
    forward_out = jnp.stack(forward)[:, None, None]
    backward_out = jnp.stack(backward)[:, None, None]
    return (forward_out, backward_out)


def solution(mesh):
    placed = (
        P(None, "row", "col", None, None, None),
        P(None, "row", "col", None, None, None),
        P(None, "row", "col", None, None, None),
        P(None, "row", "col", None),
        P(None, "row", "col", None),
        P(None, "row", "col"),
    )
    n_row, n_col = mesh.shape["row"], mesh.shape["col"]

    def local(rhs, diag_inv, blocks, blk_target, blk_source, blk_count):
        sizes = (n_row, n_col)
        dense = n_row * n_col <= blocks.shape[3] and rhs.shape[3] == 1
        even = n_row >= 8 and n_col >= 2 and all(size & (size - 1) == 0 for size in sizes)
        run = direct_shards if dense and even else shards
        return run(rhs, diag_inv, blocks, blk_target, blk_source, blk_count)

    return jax.shard_map(
        local,
        mesh=mesh,
        in_specs=placed,
        out_specs=(
            P(None, "row", "col", None, None, None),
            P(None, "row", "col", None, None, None),
        ),
        check_vma=False,
    )
```

```python
import functools

import jax
import jax.numpy as jnp
from jax import lax
from jax.experimental import pallas as pl
from jax.experimental.pallas import tpu as pltpu
from jax.sharding import PartitionSpec as P

HIGH_PRECISION = lax.Precision.HIGHEST
MIB = 1024 * 1024
VMEM = pltpu.MemorySpace.VMEM
SMEM = pltpu.MemorySpace.SMEM


def halves(value):
    high = value.astype(jnp.bfloat16)
    low = (value - high.astype(jnp.float32)).astype(jnp.bfloat16)
    return high, low


def product(left, right, transposed):
    contract = (((1,), (1 if transposed else 0,)), ((), ()))
    dot = functools.partial(
        lax.dot_general, dimension_numbers=contract, preferred_element_type=jnp.float32
    )
    return dot(left[0], right[0]) + (dot(left[0], right[1]) + dot(left[1], right[0]))


def gather_blocks_kernel(
    n_row, n_col, level, chunk, slots_ref, blocks_ref, *refs
):
    total, slots, arrived = refs[-3:]
    slot_count = slots.shape[0]
    count, row, col = (slots_ref[level, 2 * slot_count + place] for place in range(3))
    half = n_row // 2
    side = row // half

    def fetch(number):
        span = pl.ds(number * chunk, chunk)
        return pltpu.make_async_copy(
            blocks_ref.at[level, span], slots.at[span], arrived.at[number]
        )

    for number in range(arrived.shape[0]):
        pl.when(number * chunk < count)(fetch(number).start)
    total[...] = jnp.zeros_like(total)

    def add(slot, carry):
        pl.when(lax.rem(slot, chunk) == 0)(fetch(slot // chunk).wait)
        source = slots_ref[level, slot_count + slot]
        near = lax.rem(source, half) ^ lax.rem(row, half)
        below = near * 2 + ((source // half) ^ side)
        above = slots_ref[level, slot] ^ col
        total[below * n_col + above] += slots[slot]
        return carry

    lax.fori_loop(0, count, add, 0)


def gather_blocks(level, slots, blocks, n_row, n_col, after):
    slot_count, block = blocks.shape[1], blocks.shape[2]
    chunk = max(1, slot_count // 4)
    shape = (n_row * n_col, block, block)
    scalars = pl.BlockSpec(memory_space=SMEM)
    return pl.pallas_call(
        functools.partial(gather_blocks_kernel, n_row, n_col, level, chunk),
        out_shape=jax.ShapeDtypeStruct(shape, jnp.float32),
        in_specs=[scalars] + [pl.BlockSpec(memory_space=pl.ANY)] * (1 + len(after)),
        out_specs=pl.BlockSpec(memory_space=VMEM),
        scratch_shapes=[
            pltpu.VMEM((slot_count, block, block), jnp.float32),
            pltpu.SemaphoreType.DMA((slot_count // chunk,)),
        ],
        compiler_params=pltpu.CompilerParams(vmem_limit_bytes=(51 if level == 0 else 16) * MIB),
        cost_estimate=pl.CostEstimate(
            flops=slot_count * block * block,
            bytes_accessed=8 * slot_count * block * block,
            transcendentals=0,
        ),
        name=f"gather_blocks_{level}",
    )(slots, blocks, *after)


def split_kernel(n_col, flipped, total_ref, *refs):
    high_ref, low_ref = refs[-2:]
    block = total_ref.shape[-1]
    for pair in range(total_ref.shape[0]):
        at = (pair % n_col, pair // n_col) if flipped else (pair // n_col, pair % n_col)
        rows, lanes = (pl.ds(place * block, block) for place in at)
        high, low = halves(total_ref[pair].T if flipped else total_ref[pair])
        high_ref[rows, lanes] = high
        low_ref[rows, lanes] = low


def split(total, n_row, n_col, flipped, after):
    block = total.shape[-1]
    sizes = (n_col, n_row) if flipped else (n_row, n_col)
    shape = jax.ShapeDtypeStruct(tuple(size * block for size in sizes), jnp.bfloat16)
    whole = pl.BlockSpec(memory_space=VMEM)
    return pl.pallas_call(
        functools.partial(split_kernel, n_col, flipped),
        out_shape=[shape, shape],
        in_specs=[whole] + [pl.BlockSpec(memory_space=pl.ANY)] * len(after),
        out_specs=[whole, whole],
        compiler_params=pltpu.CompilerParams(vmem_limit_bytes=8 * MIB),
        cost_estimate=pl.CostEstimate(
            flops=3 * total.size, bytes_accessed=8 * total.size, transcendentals=0
        ),
        name="flip" if flipped else "split",
    )(total, *after)


def read(term, refs):
    number, place = term
    return refs[number][...] if place is None else refs[number][place]


def total_of(terms, refs):
    value = read(terms[0], refs)
    for term in terms[1:]:
        value += read(term, refs)
    return value


def write(ref, values):
    if len(ref.shape) == 2:
        ref[...] = values[0]
    else:
        for place, value in enumerate(values):
            ref[place] = value


class Operands:
    def __init__(self):
        self.arrays = []

    def term(self, piece):
        array, place = piece
        for number, known in enumerate(self.arrays):
            if known is array:
                return number, place
        self.arrays.append(array)
        return len(self.arrays) - 1, place


def couple_kernel(terms, span, high_ref, low_ref, *refs):
    n_in = 1 + max(number for number, _ in terms)
    ins, outs = refs[:n_in], refs[n_in:]
    block = ins[0].shape[-1]
    joined = jnp.concatenate([read(term, ins) for term in terms], axis=1)
    wanted = pl.ds(span[0] * block, (span[1] - span[0]) * block)
    result = product(halves(joined), (high_ref[:, wanted], low_ref[:, wanted]), False)
    pieces = [result[:, at : at + block] for at in range(0, result.shape[1], block)]
    each = len(pieces) // len(outs)
    for number, ref in enumerate(outs):
        write(ref, pieces[number * each : (number + 1) * each])


def couple(pieces, high, low, span, each):
    operands = Operands()
    terms = [operands.term(piece) for piece in pieces]
    rows, block = operands.arrays[0].shape[-2:]
    shape = (rows, block) if each == 1 else (each, rows, block)
    n_out = (span[1] - span[0]) // each
    whole = pl.BlockSpec(memory_space=VMEM)
    work = rows * block * block * len(terms) * (span[1] - span[0])
    return pl.pallas_call(
        functools.partial(couple_kernel, terms, span),
        out_shape=[jax.ShapeDtypeStruct(shape, jnp.float32)] * n_out,
        in_specs=[whole] * (2 + len(operands.arrays)),
        out_specs=[whole] * n_out,
        compiler_params=pltpu.CompilerParams(vmem_limit_bytes=16 * MIB),
        cost_estimate=pl.CostEstimate(
            flops=6 * work, bytes_accessed=4 * work // rows, transcendentals=0
        ),
        name="couple",
    )(high, low, *operands.arrays)


def first_solve_kernel(right_ref, inverse_ref, out_ref, right, inverse, arrived):
    fetches = [
        pltpu.make_async_copy(right_ref.at[0], right, arrived.at[0]),
        pltpu.make_async_copy(inverse_ref.at[0], inverse, arrived.at[1]),
    ]
    for fetch in fetches:
        fetch.start()
    for fetch in fetches:
        fetch.wait()
    out_ref[...] = product(halves(right[...]), halves(inverse[...]), False)


def first_solve(right, inverse):
    rows, block = right.shape[-2:]
    return pl.pallas_call(
        first_solve_kernel,
        out_shape=jax.ShapeDtypeStruct((rows, block), jnp.float32),
        in_specs=[pl.BlockSpec(memory_space=pl.ANY)] * 2,
        out_specs=pl.BlockSpec(memory_space=VMEM),
        scratch_shapes=[
            pltpu.VMEM((rows, block), jnp.float32),
            pltpu.VMEM((block, block), jnp.float32),
            pltpu.SemaphoreType.DMA((2,)),
        ],
        compiler_params=pltpu.CompilerParams(vmem_limit_bytes=60 * MIB),
        name="first_solve",
    )(right, inverse)


def solve_kernel(transposed, level, terms, n_ins, *refs):
    right_ref, inverse_ref = refs[:2]
    ins, out_ref = refs[2 : 2 + n_ins], refs[-1]
    value = right_ref[level] if len(right_ref.shape) == 3 else right_ref[...]
    if terms:
        value -= total_of(terms, ins)
    out_ref[...] = product(halves(value), halves(inverse_ref[level]), transposed)


def solve(right, inverse, level, pieces, transposed, after=()):
    rows, block = right.shape[-2:]
    operands = Operands()
    terms = [operands.term(piece) for piece in pieces]
    whole = pl.BlockSpec(memory_space=VMEM)
    return pl.pallas_call(
        functools.partial(solve_kernel, transposed, level, terms, len(operands.arrays)),
        out_shape=jax.ShapeDtypeStruct((rows, block), jnp.float32),
        in_specs=[whole] * (2 + len(operands.arrays))
        + [pl.BlockSpec(memory_space=pl.ANY)] * len(after),
        out_specs=whole,
        compiler_params=pltpu.CompilerParams(vmem_limit_bytes=8 * MIB),
        cost_estimate=pl.CostEstimate(
            flops=6 * rows * block * block, bytes_accessed=4 * block * block, transcendentals=0
        ),
        name="solve_up" if not transposed else "solve_down",
    )(right, inverse, *operands.arrays, *after)


def combine_kernel(sums, n_ins, *refs):
    ins, outs = refs[:n_ins], refs[-len(sums) :]
    for terms, ref in zip(sums, outs):
        write(ref, [total_of(entry, ins) for entry in terms])


def combine(sums, after=()):
    operands = Operands()
    sums = [[[operands.term(piece) for piece in entry] for entry in entries] for entries in sums]
    rows, block = operands.arrays[0].shape[-2:]
    whole = pl.BlockSpec(memory_space=VMEM)
    shapes = [(rows, block) if len(e) == 1 else (len(e), rows, block) for e in sums]
    return pl.pallas_call(
        functools.partial(combine_kernel, sums, len(operands.arrays)),
        out_shape=[jax.ShapeDtypeStruct(shape, jnp.float32) for shape in shapes],
        in_specs=[whole] * len(operands.arrays)
        + [pl.BlockSpec(memory_space=pl.ANY)] * len(after),
        out_specs=[whole] * len(sums),
        compiler_params=pltpu.CompilerParams(vmem_limit_bytes=8 * MIB),
        cost_estimate=pl.CostEstimate(
            flops=rows * block, bytes_accessed=4 * rows * block, transcendentals=0
        ),
        name="combine",
    )(*operands.arrays, *after)


def stack_kernel(n_ins, *refs):
    write(refs[-1], [ref[...] for ref in refs[:n_ins]])


def stack(segments, after=()):
    whole = pl.BlockSpec(memory_space=VMEM)
    shape = (len(segments),) + segments[0].shape
    return pl.pallas_call(
        functools.partial(stack_kernel, len(segments)),
        out_shape=jax.ShapeDtypeStruct(shape, jnp.float32),
        in_specs=[whole] * len(segments) + [pl.BlockSpec(memory_space=pl.ANY)] * len(after),
        out_specs=whole,
        compiler_params=pltpu.CompilerParams(vmem_limit_bytes=8 * MIB),
        name="stack",
    )(*segments, *after)


def far_exchange(segment, axis):
    size = lax.axis_size(axis)
    return lax.ppermute(segment, axis, [(i, i ^ (size // 2)) for i in range(size)])


def gather_row(segment, after):
    half = lax.axis_size("row") // 2
    received = far_exchange(segment, "row")
    (both,) = combine([[[(segment, None)], [(received, None)]]], after)
    messages = exchange_each([both] * half, "row")
    return [(message, side) for message in messages for side in range(2)]


def deliver_row(messages):
    received = exchange_each(messages, "row")
    mine, other = combine(
        [
            [[(message, side) for message in [received[0], *reversed(received[1:])]]]
            for side in range(2)
        ]
    )
    return [(mine, None), (far_exchange(other, "row"), None)]


def exchange_each(messages, axis):
    size = lax.axis_size(axis)
    received = {0: messages[0]}
    for d in reversed(range(1, len(messages))):
        received[d] = lax.ppermute(messages[d], axis, [(i, i ^ d) for i in range(size)])
    return [received[d] for d in range(len(messages))]


def direct_shards(rhs, diag_inv, blocks, blk_target, blk_source, blk_count):
    levels = rhs.shape[0]
    n_row, n_col = lax.axis_size("row"), lax.axis_size("col")
    right = rhs.reshape((levels,) + rhs.shape[-2:])
    inverse = diag_inv.reshape((levels,) + diag_inv.shape[-2:])
    weights = blocks.reshape((levels - 1,) + blocks.shape[-3:])
    here = [lax.axis_index(axis).astype(jnp.int32) for axis in ("row", "col")]
    slots = jnp.concatenate(
        [blk_target.reshape(levels - 1, -1), blk_source.reshape(levels - 1, -1)]
        + [blk_count.reshape(levels - 1, 1)]
        + [jnp.full((levels - 1, 1), index) for index in here],
        axis=1,
    )
    gather = lambda level, after: gather_blocks(level, slots, weights, n_row, n_col, after)
    tidy = lambda level, flipped, after: split(totals[level], n_row, n_col, flipped, after)
    forward = [first_solve(right, inverse)]
    totals = [gather(0, ())]
    up, down = [], []
    for level in range(1, levels):
        solved = forward[-1:]
        up.append(tidy(level - 1, False, solved if level > 1 else ()))
        if level > 1:
            down.append(tidy(level - 2, True, solved))
        pieces = gather_row(forward[-1], [pair[0] for pair in up[-1:] + down[-1:]])
        far = couple(pieces, *up[-1], (n_col // 2, n_col), 1)
        near = couple(pieces, *up[-1], (0, n_col // 2), 1)
        if level < levels - 1:
            totals.append(gather(level, near[:1]))
            after = totals[-1:]
        else:
            down.append(tidy(level - 1, True, near[:1]))
            after = down[-1][:1]
        pieces = plain(exchange_each(near + far, "col"))
        forward.append(solve(right, inverse, level, pieces, False, after))
    backward = [None] * levels
    backward[-1] = solve(forward[-1], inverse, levels - 1, [], True)
    for level in range(levels - 2, -1, -1):
        pieces = plain(exchange_each([backward[level + 1]] * n_col, "col"))
        sent = couple(pieces, *down[level], (2, n_row), 2)
        kept = couple(pieces, *down[level], (0, 2), 2)
        if level == levels - 2:
            forward_out = stack(forward, kept[:1])
        pieces = deliver_row(kept + sent)
        after = (forward_out,) if level == levels - 2 else ()
        backward[level] = solve(forward[level], inverse, level, pieces, True, after)
    return forward_out.reshape(rhs.shape), stack(backward).reshape(rhs.shape)


def plain(messages):
    return [(message, None) for message in messages]


def fold_for(index, piece):
    entry_count = piece.shape[0]
    onehot = (index[:, None] == jnp.arange(entry_count, dtype=jnp.int32)[None, :]).astype(
        jnp.float32
    )
    return jnp.dot(
        onehot,
        piece.reshape(entry_count, -1),
        precision=HIGH_PRECISION,
        preferred_element_type=jnp.float32,
    )


def route_sum(index, entry_count, block_products, width):
    slot_count = block_products.shape[0]
    active_flags = jnp.arange(slot_count, dtype=jnp.int32) < entry_count
    routing_table = (
        (index[None, :] == jnp.arange(width, dtype=jnp.int32)[:, None]) & active_flags[None, :]
    ).astype(jnp.float32)
    return jnp.dot(
        routing_table,
        block_products.reshape(slot_count, -1),
        precision=HIGH_PRECISION,
        preferred_element_type=jnp.float32,
    )


def forward_level(previous, weight_matrix, target, source, entry_count):
    slot_count = weight_matrix.shape[0]
    slots, rhs_column_count, block_ordering = previous.shape
    selected_blocks = fold_for(source, lax.all_gather(previous, "row", axis=0, tiled=True))
    block_products = jnp.einsum(
        "ado,aon->adn",
        selected_blocks.reshape(slot_count, rhs_column_count, block_ordering),
        weight_matrix,
        precision=HIGH_PRECISION,
    )
    ncol = lax.axis_size("col")
    buckets = route_sum(target, entry_count, block_products, ncol * slots).reshape(
        ncol, slots, rhs_column_count, block_ordering
    )
    own = lax.psum_scatter(buckets, "col", scatter_dimension=0, tiled=True)[0]
    return own


def backward_level(upper, weight_matrix, target, source, entry_count):
    slot_count = weight_matrix.shape[0]
    slots, rhs_column_count, block_ordering = upper.shape
    selected_blocks = fold_for(target, lax.all_gather(upper, "col", axis=0, tiled=True))
    block_products = jnp.einsum(
        "mlv,mtv->mlt",
        selected_blocks.reshape(slot_count, rhs_column_count, block_ordering),
        weight_matrix,
        precision=HIGH_PRECISION,
    )
    nrow = lax.axis_size("row")
    buckets = route_sum(source, entry_count, block_products, nrow * slots).reshape(
        nrow, slots, rhs_column_count, block_ordering
    )
    own = lax.psum_scatter(buckets, "row", scatter_dimension=0, tiled=True)[0]
    return own


def shards(rhs, diag_inv, blocks, blk_target, blk_source, blk_count):
    levels = rhs.shape[0]
    right = rhs[:, 0, 0]
    inverse = diag_inv[:, 0, 0]
    weight_matrix = blocks[:, 0, 0]
    targets = blk_target[:, 0, 0]
    sources = blk_source[:, 0, 0]
    counts = blk_count[:, 0, 0]
    forward = [jnp.einsum("srb,sbc->src", right[0], inverse[0], precision=HIGH_PRECISION)]
    for level in range(1, levels):
        own = forward_level(
            forward[-1],
            weight_matrix[level - 1],
            targets[level - 1],
            sources[level - 1],
            counts[level - 1],
        )
        forward.append(
            jnp.einsum("srb,sbc->src", right[level] - own, inverse[level], precision=HIGH_PRECISION)
        )
    backward = [None] * levels
    backward[levels - 1] = jnp.einsum(
        "src,sbc->srb", forward[levels - 1], inverse[levels - 1], precision=HIGH_PRECISION
    )
    for level in range(levels - 2, -1, -1):
        own = backward_level(
            backward[level + 1], weight_matrix[level], targets[level], sources[level], counts[level]
        )
        backward[level] = jnp.einsum(
            "src,sbc->srb", forward[level] - own, inverse[level], precision=HIGH_PRECISION
        )
    forward_out = jnp.stack(forward)[:, None, None]
    backward_out = jnp.stack(backward)[:, None, None]
    return (forward_out, backward_out)


def solution(mesh):
    placed = (
        P(None, "row", "col", None, None, None),
        P(None, "row", "col", None, None, None),
        P(None, "row", "col", None, None, None),
        P(None, "row", "col", None),
        P(None, "row", "col", None),
        P(None, "row", "col"),
    )
    n_row, n_col = mesh.shape["row"], mesh.shape["col"]

    def local(rhs, diag_inv, blocks, blk_target, blk_source, blk_count):
        sizes = (n_row, n_col)
        dense = n_row * n_col <= blocks.shape[3] and rhs.shape[3] == 1
        even = all(size > 1 and size & (size - 1) == 0 for size in sizes)
        run = direct_shards if dense and even else shards
        return run(rhs, diag_inv, blocks, blk_target, blk_source, blk_count)

    return jax.shard_map(
        local,
        mesh=mesh,
        in_specs=placed,
        out_specs=(
            P(None, "row", "col", None, None, None),
            P(None, "row", "col", None, None, None),
        ),
        check_vma=False,
    )
```

```python
import functools

import jax
import jax.numpy as jnp
from jax import lax
from jax.experimental import pallas as pl
from jax.experimental.pallas import tpu as pltpu
from jax.sharding import PartitionSpec as P

HIGH_PRECISION = lax.Precision.HIGHEST
MIB = 1024 * 1024
VMEM = pltpu.MemorySpace.VMEM
SMEM = pltpu.MemorySpace.SMEM


def halves(value):
    high = value.astype(jnp.bfloat16)
    low = (value - high.astype(jnp.float32)).astype(jnp.bfloat16)
    return high, low


def product(left, right, transposed):
    contract = (((1,), (1 if transposed else 0,)), ((), ()))
    dot = functools.partial(
        lax.dot_general, dimension_numbers=contract, preferred_element_type=jnp.float32
    )
    return dot(left[0], right[0]) + (dot(left[0], right[1]) + dot(left[1], right[0]))


def gather_blocks_kernel(
    n_row, n_col, level, chunk, slots_ref, blocks_ref, *refs
):
    total, slots, arrived = refs[-3:]
    slot_count = slots.shape[0]
    count, row, col = (slots_ref[level, 2 * slot_count + place] for place in range(3))
    half = n_row // 2
    side = row // half

    def fetch(number):
        span = pl.ds(number * chunk, chunk)
        return pltpu.make_async_copy(
            blocks_ref.at[level, span], slots.at[span], arrived.at[number]
        )

    for number in range(arrived.shape[0]):
        pl.when(number * chunk < count)(fetch(number).start)
    total[...] = jnp.zeros_like(total)

    def add(slot, carry):
        pl.when(lax.rem(slot, chunk) == 0)(fetch(slot // chunk).wait)
        source = slots_ref[level, slot_count + slot]
        near = lax.rem(source, half) ^ lax.rem(row, half)
        near = jnp.where(lax.rem(col, 2) == 1, mirrored(near, half), near)
        below = near * 2 + ((source // half) ^ side)
        above = slots_ref[level, slot] ^ col
        total[below * n_col + above] += slots[slot]
        return carry

    lax.fori_loop(0, count, add, 0)


def gather_blocks(level, slots, blocks, n_row, n_col, after):
    slot_count, block = blocks.shape[1], blocks.shape[2]
    chunk = max(1, slot_count // 4)
    shape = (n_row * n_col, block, block)
    scalars = pl.BlockSpec(memory_space=SMEM)
    return pl.pallas_call(
        functools.partial(gather_blocks_kernel, n_row, n_col, level, chunk),
        out_shape=jax.ShapeDtypeStruct(shape, jnp.float32),
        in_specs=[scalars] + [pl.BlockSpec(memory_space=pl.ANY)] * (1 + len(after)),
        out_specs=pl.BlockSpec(memory_space=VMEM),
        scratch_shapes=[
            pltpu.VMEM((slot_count, block, block), jnp.float32),
            pltpu.SemaphoreType.DMA((slot_count // chunk,)),
        ],
        compiler_params=pltpu.CompilerParams(vmem_limit_bytes=(51 if level == 0 else 16) * MIB),
        cost_estimate=pl.CostEstimate(
            flops=slot_count * block * block,
            bytes_accessed=8 * slot_count * block * block,
            transcendentals=0,
        ),
        name=f"gather_blocks_{level}",
    )(slots, blocks, *after)


def split_kernel(n_col, flipped, total_ref, *refs):
    high_ref, low_ref = refs[-2:]
    block = total_ref.shape[-1]
    for pair in range(total_ref.shape[0]):
        at = (pair % n_col, pair // n_col) if flipped else (pair // n_col, pair % n_col)
        rows, lanes = (pl.ds(place * block, block) for place in at)
        high, low = halves(total_ref[pair].T if flipped else total_ref[pair])
        high_ref[rows, lanes] = high
        low_ref[rows, lanes] = low


def split(total, n_row, n_col, flipped, after):
    block = total.shape[-1]
    sizes = (n_col, n_row) if flipped else (n_row, n_col)
    shape = jax.ShapeDtypeStruct(tuple(size * block for size in sizes), jnp.bfloat16)
    whole = pl.BlockSpec(memory_space=VMEM)
    return pl.pallas_call(
        functools.partial(split_kernel, n_col, flipped),
        out_shape=[shape, shape],
        in_specs=[whole] + [pl.BlockSpec(memory_space=pl.ANY)] * len(after),
        out_specs=[whole, whole],
        compiler_params=pltpu.CompilerParams(vmem_limit_bytes=8 * MIB),
        cost_estimate=pl.CostEstimate(
            flops=3 * total.size, bytes_accessed=8 * total.size, transcendentals=0
        ),
        name="flip" if flipped else "split",
    )(total, *after)


def read(term, refs):
    number, place = term
    return refs[number][...] if place is None else refs[number][place]


def total_of(terms, refs):
    value = read(terms[0], refs)
    for term in terms[1:]:
        value += read(term, refs)
    return value


def write(ref, values):
    if len(ref.shape) == 2:
        ref[...] = values[0]
    else:
        for place, value in enumerate(values):
            ref[place] = value


class Operands:
    def __init__(self):
        self.arrays = []

    def term(self, piece):
        array, place = piece
        for number, known in enumerate(self.arrays):
            if known is array:
                return number, place
        self.arrays.append(array)
        return len(self.arrays) - 1, place


def couple_kernel(terms, span, high_ref, low_ref, *refs):
    n_in = 1 + max(number for number, _ in terms)
    ins, outs = refs[:n_in], refs[n_in:]
    block = ins[0].shape[-1]
    joined = jnp.concatenate([read(term, ins) for term in terms], axis=1)
    wanted = pl.ds(span[0] * block, (span[1] - span[0]) * block)
    result = product(halves(joined), (high_ref[:, wanted], low_ref[:, wanted]), False)
    pieces = [result[:, at : at + block] for at in range(0, result.shape[1], block)]
    each = len(pieces) // len(outs)
    for number, ref in enumerate(outs):
        write(ref, pieces[number * each : (number + 1) * each])


def couple(pieces, high, low, span, each):
    operands = Operands()
    terms = [operands.term(piece) for piece in pieces]
    rows, block = operands.arrays[0].shape[-2:]
    shape = (rows, block) if each == 1 else (each, rows, block)
    n_out = (span[1] - span[0]) // each
    whole = pl.BlockSpec(memory_space=VMEM)
    work = rows * block * block * len(terms) * (span[1] - span[0])
    return pl.pallas_call(
        functools.partial(couple_kernel, terms, span),
        out_shape=[jax.ShapeDtypeStruct(shape, jnp.float32)] * n_out,
        in_specs=[whole] * (2 + len(operands.arrays)),
        out_specs=[whole] * n_out,
        compiler_params=pltpu.CompilerParams(vmem_limit_bytes=16 * MIB),
        cost_estimate=pl.CostEstimate(
            flops=6 * work, bytes_accessed=4 * work // rows, transcendentals=0
        ),
        name="couple",
    )(high, low, *operands.arrays)


def first_solve_kernel(right_ref, inverse_ref, out_ref, right, inverse, arrived):
    fetches = [
        pltpu.make_async_copy(right_ref.at[0], right, arrived.at[0]),
        pltpu.make_async_copy(inverse_ref.at[0], inverse, arrived.at[1]),
    ]
    for fetch in fetches:
        fetch.start()
    for fetch in fetches:
        fetch.wait()
    out_ref[...] = product(halves(right[...]), halves(inverse[...]), False)


def first_solve(right, inverse):
    rows, block = right.shape[-2:]
    return pl.pallas_call(
        first_solve_kernel,
        out_shape=jax.ShapeDtypeStruct((rows, block), jnp.float32),
        in_specs=[pl.BlockSpec(memory_space=pl.ANY)] * 2,
        out_specs=pl.BlockSpec(memory_space=VMEM),
        scratch_shapes=[
            pltpu.VMEM((rows, block), jnp.float32),
            pltpu.VMEM((block, block), jnp.float32),
            pltpu.SemaphoreType.DMA((2,)),
        ],
        compiler_params=pltpu.CompilerParams(vmem_limit_bytes=60 * MIB),
        name="first_solve",
    )(right, inverse)


def solve_kernel(transposed, level, terms, n_ins, *refs):
    right_ref, inverse_ref = refs[:2]
    ins, out_ref = refs[2 : 2 + n_ins], refs[-1]
    value = right_ref[level] if len(right_ref.shape) == 3 else right_ref[...]
    if terms:
        value -= total_of(terms, ins)
    out_ref[...] = product(halves(value), halves(inverse_ref[level]), transposed)


def solve(right, inverse, level, pieces, transposed, after=()):
    rows, block = right.shape[-2:]
    operands = Operands()
    terms = [operands.term(piece) for piece in pieces]
    whole = pl.BlockSpec(memory_space=VMEM)
    return pl.pallas_call(
        functools.partial(solve_kernel, transposed, level, terms, len(operands.arrays)),
        out_shape=jax.ShapeDtypeStruct((rows, block), jnp.float32),
        in_specs=[whole] * (2 + len(operands.arrays))
        + [pl.BlockSpec(memory_space=pl.ANY)] * len(after),
        out_specs=whole,
        compiler_params=pltpu.CompilerParams(vmem_limit_bytes=8 * MIB),
        cost_estimate=pl.CostEstimate(
            flops=6 * rows * block * block, bytes_accessed=4 * block * block, transcendentals=0
        ),
        name="solve_up" if not transposed else "solve_down",
    )(right, inverse, *operands.arrays, *after)


def combine_kernel(sums, n_ins, *refs):
    ins, outs = refs[:n_ins], refs[-len(sums) :]
    for terms, ref in zip(sums, outs):
        write(ref, [total_of(entry, ins) for entry in terms])


def combine(sums, after=()):
    operands = Operands()
    sums = [[[operands.term(piece) for piece in entry] for entry in entries] for entries in sums]
    rows, block = operands.arrays[0].shape[-2:]
    whole = pl.BlockSpec(memory_space=VMEM)
    shapes = [(rows, block) if len(e) == 1 else (len(e), rows, block) for e in sums]
    return pl.pallas_call(
        functools.partial(combine_kernel, sums, len(operands.arrays)),
        out_shape=[jax.ShapeDtypeStruct(shape, jnp.float32) for shape in shapes],
        in_specs=[whole] * len(operands.arrays)
        + [pl.BlockSpec(memory_space=pl.ANY)] * len(after),
        out_specs=[whole] * len(sums),
        compiler_params=pltpu.CompilerParams(vmem_limit_bytes=8 * MIB),
        cost_estimate=pl.CostEstimate(
            flops=rows * block, bytes_accessed=4 * rows * block, transcendentals=0
        ),
        name="combine",
    )(*operands.arrays, *after)


def stack_kernel(n_ins, *refs):
    write(refs[-1], [ref[...] for ref in refs[:n_ins]])


def stack(segments, after=()):
    whole = pl.BlockSpec(memory_space=VMEM)
    shape = (len(segments),) + segments[0].shape
    return pl.pallas_call(
        functools.partial(stack_kernel, len(segments)),
        out_shape=jax.ShapeDtypeStruct(shape, jnp.float32),
        in_specs=[whole] * len(segments) + [pl.BlockSpec(memory_space=pl.ANY)] * len(after),
        out_specs=whole,
        compiler_params=pltpu.CompilerParams(vmem_limit_bytes=8 * MIB),
        name="stack",
    )(*segments, *after)


def far_exchange(segment, axis):
    size = lax.axis_size(axis)
    return lax.ppermute(segment, axis, [(i, i ^ (size // 2)) for i in range(size)])


def mirrored(number, size):
    bits = size.bit_length() - 1
    return sum(((number >> bit) & 1) << (bits - 1 - bit) for bit in range(bits))


def near_exchange(messages):
    n_row, n_col = lax.axis_size("row"), lax.axis_size("col")
    half = n_row // 2
    received = {0: messages[0]}
    for d in reversed(range(1, half)):
        pairs = []
        for row in range(n_row):
            for col in range(n_col):
                partner = row ^ (mirrored(d, half) if col % 2 else d)
                pairs.append((row * n_col + col, partner * n_col + col))
        received[d] = lax.ppermute(messages[d], ("row", "col"), pairs)
    return [received[d] for d in range(half)]


def gather_row(segment, after):
    half = lax.axis_size("row") // 2
    received = far_exchange(segment, "row")
    (both,) = combine([[[(segment, None)], [(received, None)]]], after)
    messages = near_exchange([both] * half)
    return [(message, side) for message in messages for side in range(2)]


def deliver_row(messages):
    received = near_exchange(messages)
    mine, other = combine(
        [
            [[(message, side) for message in [received[0], *reversed(received[1:])]]]
            for side in range(2)
        ]
    )
    return [(mine, None), (far_exchange(other, "row"), None)]


def exchange_each(messages, axis):
    size = lax.axis_size(axis)
    received = {0: messages[0]}
    for d in reversed(range(1, len(messages))):
        received[d] = lax.ppermute(messages[d], axis, [(i, i ^ d) for i in range(size)])
    return [received[d] for d in range(len(messages))]


def direct_shards(rhs, diag_inv, blocks, blk_target, blk_source, blk_count):
    levels = rhs.shape[0]
    n_row, n_col = lax.axis_size("row"), lax.axis_size("col")
    right = rhs.reshape((levels,) + rhs.shape[-2:])
    inverse = diag_inv.reshape((levels,) + diag_inv.shape[-2:])
    weights = blocks.reshape((levels - 1,) + blocks.shape[-3:])
    here = [lax.axis_index(axis).astype(jnp.int32) for axis in ("row", "col")]
    slots = jnp.concatenate(
        [blk_target.reshape(levels - 1, -1), blk_source.reshape(levels - 1, -1)]
        + [blk_count.reshape(levels - 1, 1)]
        + [jnp.full((levels - 1, 1), index) for index in here],
        axis=1,
    )
    gather = lambda level, after: gather_blocks(level, slots, weights, n_row, n_col, after)
    tidy = lambda level, flipped, after: split(totals[level], n_row, n_col, flipped, after)
    forward = [first_solve(right, inverse)]
    totals = [gather(0, ())]
    up, down = [], []
    for level in range(1, levels):
        solved = forward[-1:]
        up.append(tidy(level - 1, False, solved if level > 1 else ()))
        if level > 1:
            down.append(tidy(level - 2, True, solved))
        pieces = gather_row(forward[-1], [pair[0] for pair in up[-1:] + down[-1:]])
        far = couple(pieces, *up[-1], (n_col // 2, n_col), 1)
        near = couple(pieces, *up[-1], (0, n_col // 2), 1)
        if level < levels - 1:
            totals.append(gather(level, near[:1]))
            after = totals[-1:]
        else:
            down.append(tidy(level - 1, True, near[:1]))
            after = down[-1][:1]
        pieces = plain(reversed(exchange_each(near + far, "col")))
        forward.append(solve(right, inverse, level, pieces, False, after))
    backward = [None] * levels
    backward[-1] = solve(forward[-1], inverse, levels - 1, [], True)
    for level in range(levels - 2, -1, -1):
        pieces = plain(exchange_each([backward[level + 1]] * n_col, "col"))
        sent = couple(pieces, *down[level], (2, n_row), 2)
        kept = couple(pieces, *down[level], (0, 2), 2)
        if level == levels - 2:
            forward_out = stack(forward, kept[:1])
        pieces = deliver_row(kept + sent)
        after = (forward_out,) if level == levels - 2 else ()
        backward[level] = solve(forward[level], inverse, level, pieces, True, after)
    return forward_out.reshape(rhs.shape), stack(backward).reshape(rhs.shape)


def plain(messages):
    return [(message, None) for message in messages]


def fold_for(index, piece):
    entry_count = piece.shape[0]
    onehot = (index[:, None] == jnp.arange(entry_count, dtype=jnp.int32)[None, :]).astype(
        jnp.float32
    )
    return jnp.dot(
        onehot,
        piece.reshape(entry_count, -1),
        precision=HIGH_PRECISION,
        preferred_element_type=jnp.float32,
    )


def route_sum(index, entry_count, block_products, width):
    slot_count = block_products.shape[0]
    active_flags = jnp.arange(slot_count, dtype=jnp.int32) < entry_count
    routing_table = (
        (index[None, :] == jnp.arange(width, dtype=jnp.int32)[:, None]) & active_flags[None, :]
    ).astype(jnp.float32)
    return jnp.dot(
        routing_table,
        block_products.reshape(slot_count, -1),
        precision=HIGH_PRECISION,
        preferred_element_type=jnp.float32,
    )


def forward_level(previous, weight_matrix, target, source, entry_count):
    slot_count = weight_matrix.shape[0]
    slots, rhs_column_count, block_ordering = previous.shape
    selected_blocks = fold_for(source, lax.all_gather(previous, "row", axis=0, tiled=True))
    block_products = jnp.einsum(
        "ado,aon->adn",
        selected_blocks.reshape(slot_count, rhs_column_count, block_ordering),
        weight_matrix,
        precision=HIGH_PRECISION,
    )
    ncol = lax.axis_size("col")
    buckets = route_sum(target, entry_count, block_products, ncol * slots).reshape(
        ncol, slots, rhs_column_count, block_ordering
    )
    own = lax.psum_scatter(buckets, "col", scatter_dimension=0, tiled=True)[0]
    return own


def backward_level(upper, weight_matrix, target, source, entry_count):
    slot_count = weight_matrix.shape[0]
    slots, rhs_column_count, block_ordering = upper.shape
    selected_blocks = fold_for(target, lax.all_gather(upper, "col", axis=0, tiled=True))
    block_products = jnp.einsum(
        "mlv,mtv->mlt",
        selected_blocks.reshape(slot_count, rhs_column_count, block_ordering),
        weight_matrix,
        precision=HIGH_PRECISION,
    )
    nrow = lax.axis_size("row")
    buckets = route_sum(source, entry_count, block_products, nrow * slots).reshape(
        nrow, slots, rhs_column_count, block_ordering
    )
    own = lax.psum_scatter(buckets, "row", scatter_dimension=0, tiled=True)[0]
    return own


def shards(rhs, diag_inv, blocks, blk_target, blk_source, blk_count):
    levels = rhs.shape[0]
    right = rhs[:, 0, 0]
    inverse = diag_inv[:, 0, 0]
    weight_matrix = blocks[:, 0, 0]
    targets = blk_target[:, 0, 0]
    sources = blk_source[:, 0, 0]
    counts = blk_count[:, 0, 0]
    forward = [jnp.einsum("srb,sbc->src", right[0], inverse[0], precision=HIGH_PRECISION)]
    for level in range(1, levels):
        own = forward_level(
            forward[-1],
            weight_matrix[level - 1],
            targets[level - 1],
            sources[level - 1],
            counts[level - 1],
        )
        forward.append(
            jnp.einsum("srb,sbc->src", right[level] - own, inverse[level], precision=HIGH_PRECISION)
        )
    backward = [None] * levels
    backward[levels - 1] = jnp.einsum(
        "src,sbc->srb", forward[levels - 1], inverse[levels - 1], precision=HIGH_PRECISION
    )
    for level in range(levels - 2, -1, -1):
        own = backward_level(
            backward[level + 1], weight_matrix[level], targets[level], sources[level], counts[level]
        )
        backward[level] = jnp.einsum(
            "src,sbc->srb", forward[level] - own, inverse[level], precision=HIGH_PRECISION
        )
    forward_out = jnp.stack(forward)[:, None, None]
    backward_out = jnp.stack(backward)[:, None, None]
    return (forward_out, backward_out)


def solution(mesh):
    placed = (
        P(None, "row", "col", None, None, None),
        P(None, "row", "col", None, None, None),
        P(None, "row", "col", None, None, None),
        P(None, "row", "col", None),
        P(None, "row", "col", None),
        P(None, "row", "col"),
    )
    n_row, n_col = mesh.shape["row"], mesh.shape["col"]

    def local(rhs, diag_inv, blocks, blk_target, blk_source, blk_count):
        sizes = (n_row, n_col)
        dense = n_row * n_col <= blocks.shape[3] and rhs.shape[3] == 1
        even = all(size > 1 and size & (size - 1) == 0 for size in sizes)
        run = direct_shards if dense and even else shards
        return run(rhs, diag_inv, blocks, blk_target, blk_source, blk_count)

    return jax.shard_map(
        local,
        mesh=mesh,
        in_specs=placed,
        out_specs=(
            P(None, "row", "col", None, None, None),
            P(None, "row", "col", None, None, None),
        ),
        check_vma=False,
    )
```

```python
import functools

import jax
import jax.numpy as jnp
from jax import lax
from jax.experimental import pallas as pl
from jax.experimental.pallas import tpu as pltpu
from jax.sharding import PartitionSpec as P

HIGH_PRECISION = lax.Precision.HIGHEST
MIB = 1024 * 1024
VMEM = pltpu.MemorySpace.VMEM
SMEM = pltpu.MemorySpace.SMEM


def halves(value):
    high = value.astype(jnp.bfloat16)
    low = (value - high.astype(jnp.float32)).astype(jnp.bfloat16)
    return high, low


def product(left, right, transposed):
    contract = (((1,), (1 if transposed else 0,)), ((), ()))
    dot = functools.partial(
        lax.dot_general, dimension_numbers=contract, preferred_element_type=jnp.float32
    )
    return dot(left[0], right[0]) + (dot(left[0], right[1]) + dot(left[1], right[0]))


def gather_blocks_kernel(
    n_row, n_col, level, chunk, slots_ref, blocks_ref, *refs
):
    total, slots, arrived = refs[-3:]
    slot_count = slots.shape[0]
    count, row, col = (slots_ref[level, 2 * slot_count + place] for place in range(3))
    half = n_row // 2
    side = row // half

    def fetch(number):
        span = pl.ds(number * chunk, chunk)
        return pltpu.make_async_copy(
            blocks_ref.at[level, span], slots.at[span], arrived.at[number]
        )

    for number in range(arrived.shape[0]):
        pl.when(number * chunk < count)(fetch(number).start)
    total[...] = jnp.zeros_like(total)

    def add(slot, carry):
        pl.when(lax.rem(slot, chunk) == 0)(fetch(slot // chunk).wait)
        source = slots_ref[level, slot_count + slot]
        near = lax.rem(source, half) ^ lax.rem(row, half)
        near = jnp.where(lax.rem(col, 2) == 1, mirrored(near, half), near)
        below = near * 2 + ((source // half) ^ side)
        above = slots_ref[level, slot] ^ col
        total[below * n_col + above] += slots[slot]
        return carry

    lax.fori_loop(0, count, add, 0)


def gather_blocks(level, slots, blocks, n_row, n_col, after):
    slot_count, block = blocks.shape[1], blocks.shape[2]
    chunk = max(1, slot_count // 4)
    shape = (n_row * n_col, block, block)
    scalars = pl.BlockSpec(memory_space=SMEM)
    return pl.pallas_call(
        functools.partial(gather_blocks_kernel, n_row, n_col, level, chunk),
        out_shape=jax.ShapeDtypeStruct(shape, jnp.float32),
        in_specs=[scalars] + [pl.BlockSpec(memory_space=pl.ANY)] * (1 + len(after)),
        out_specs=pl.BlockSpec(memory_space=VMEM),
        scratch_shapes=[
            pltpu.VMEM((slot_count, block, block), jnp.float32),
            pltpu.SemaphoreType.DMA((slot_count // chunk,)),
        ],
        compiler_params=pltpu.CompilerParams(vmem_limit_bytes=(51 if level == 0 else 16) * MIB),
        cost_estimate=pl.CostEstimate(
            flops=slot_count * block * block,
            bytes_accessed=8 * slot_count * block * block,
            transcendentals=0,
        ),
        name=f"gather_blocks_{level}",
    )(slots, blocks, *after)


def split_kernel(n_col, flipped, total_ref, *refs):
    high_ref, low_ref = refs[-2:]
    block = total_ref.shape[-1]
    for pair in range(total_ref.shape[0]):
        at = (pair % n_col, pair // n_col) if flipped else (pair // n_col, pair % n_col)
        rows, lanes = (pl.ds(place * block, block) for place in at)
        high, low = halves(total_ref[pair].T if flipped else total_ref[pair])
        high_ref[rows, lanes] = high
        low_ref[rows, lanes] = low


def split(total, n_row, n_col, flipped, after):
    block = total.shape[-1]
    sizes = (n_col, n_row) if flipped else (n_row, n_col)
    shape = jax.ShapeDtypeStruct(tuple(size * block for size in sizes), jnp.bfloat16)
    whole = pl.BlockSpec(memory_space=VMEM)
    return pl.pallas_call(
        functools.partial(split_kernel, n_col, flipped),
        out_shape=[shape, shape],
        in_specs=[whole] + [pl.BlockSpec(memory_space=pl.ANY)] * len(after),
        out_specs=[whole, whole],
        compiler_params=pltpu.CompilerParams(vmem_limit_bytes=8 * MIB),
        cost_estimate=pl.CostEstimate(
            flops=3 * total.size, bytes_accessed=8 * total.size, transcendentals=0
        ),
        name="flip" if flipped else "split",
    )(total, *after)


def read(term, refs):
    number, place = term
    return refs[number][...] if place is None else refs[number][place]


def total_of(terms, refs):
    value = read(terms[0], refs)
    for term in terms[1:]:
        value += read(term, refs)
    return value


def write(ref, values):
    if len(ref.shape) == 2:
        ref[...] = values[0]
    else:
        for place, value in enumerate(values):
            ref[place] = value


class Operands:
    def __init__(self):
        self.arrays = []

    def term(self, piece):
        array, place = piece
        for number, known in enumerate(self.arrays):
            if known is array:
                return number, place
        self.arrays.append(array)
        return len(self.arrays) - 1, place


def couple_kernel(terms, span, high_ref, low_ref, *refs):
    n_in = 1 + max(number for number, _ in terms)
    ins, outs = refs[:n_in], refs[n_in:]
    block = ins[0].shape[-1]
    joined = jnp.concatenate([read(term, ins) for term in terms], axis=1)
    wanted = pl.ds(span[0] * block, (span[1] - span[0]) * block)
    result = product(halves(joined), (high_ref[:, wanted], low_ref[:, wanted]), False)
    pieces = [result[:, at : at + block] for at in range(0, result.shape[1], block)]
    each = len(pieces) // len(outs)
    for number, ref in enumerate(outs):
        write(ref, pieces[number * each : (number + 1) * each])


def couple(pieces, high, low, span, each):
    operands = Operands()
    terms = [operands.term(piece) for piece in pieces]
    rows, block = operands.arrays[0].shape[-2:]
    shape = (rows, block) if each == 1 else (each, rows, block)
    n_out = (span[1] - span[0]) // each
    whole = pl.BlockSpec(memory_space=VMEM)
    work = rows * block * block * len(terms) * (span[1] - span[0])
    return pl.pallas_call(
        functools.partial(couple_kernel, terms, span),
        out_shape=[jax.ShapeDtypeStruct(shape, jnp.float32)] * n_out,
        in_specs=[whole] * (2 + len(operands.arrays)),
        out_specs=[whole] * n_out,
        compiler_params=pltpu.CompilerParams(vmem_limit_bytes=16 * MIB),
        cost_estimate=pl.CostEstimate(
            flops=6 * work, bytes_accessed=4 * work // rows, transcendentals=0
        ),
        name="couple",
    )(high, low, *operands.arrays)


def first_solve_kernel(right_ref, inverse_ref, out_ref, right, inverse, arrived):
    fetches = [
        pltpu.make_async_copy(right_ref.at[0], right, arrived.at[0]),
        pltpu.make_async_copy(inverse_ref.at[0], inverse, arrived.at[1]),
    ]
    for fetch in fetches:
        fetch.start()
    for fetch in fetches:
        fetch.wait()
    out_ref[...] = product(halves(right[...]), halves(inverse[...]), False)


def first_solve(right, inverse):
    rows, block = right.shape[-2:]
    return pl.pallas_call(
        first_solve_kernel,
        out_shape=jax.ShapeDtypeStruct((rows, block), jnp.float32),
        in_specs=[pl.BlockSpec(memory_space=pl.ANY)] * 2,
        out_specs=pl.BlockSpec(memory_space=VMEM),
        scratch_shapes=[
            pltpu.VMEM((rows, block), jnp.float32),
            pltpu.VMEM((block, block), jnp.float32),
            pltpu.SemaphoreType.DMA((2,)),
        ],
        compiler_params=pltpu.CompilerParams(vmem_limit_bytes=60 * MIB),
        name="first_solve",
    )(right, inverse)


def solve_kernel(transposed, level, terms, n_ins, *refs):
    right_ref, inverse_ref = refs[:2]
    ins, out_ref = refs[2 : 2 + n_ins], refs[-1]
    value = right_ref[level] if len(right_ref.shape) == 3 else right_ref[...]
    if terms:
        value -= total_of(terms, ins)
    out_ref[...] = product(halves(value), halves(inverse_ref[level]), transposed)


def solve(right, inverse, level, pieces, transposed, after=()):
    rows, block = right.shape[-2:]
    operands = Operands()
    terms = [operands.term(piece) for piece in pieces]
    whole = pl.BlockSpec(memory_space=VMEM)
    return pl.pallas_call(
        functools.partial(solve_kernel, transposed, level, terms, len(operands.arrays)),
        out_shape=jax.ShapeDtypeStruct((rows, block), jnp.float32),
        in_specs=[whole] * (2 + len(operands.arrays))
        + [pl.BlockSpec(memory_space=pl.ANY)] * len(after),
        out_specs=whole,
        compiler_params=pltpu.CompilerParams(vmem_limit_bytes=8 * MIB),
        cost_estimate=pl.CostEstimate(
            flops=6 * rows * block * block, bytes_accessed=4 * block * block, transcendentals=0
        ),
        name="solve_up" if not transposed else "solve_down",
    )(right, inverse, *operands.arrays, *after)


def combine_kernel(sums, n_ins, *refs):
    ins, outs = refs[:n_ins], refs[-len(sums) :]
    for terms, ref in zip(sums, outs):
        write(ref, [total_of(entry, ins) for entry in terms])


def combine(sums, after=()):
    operands = Operands()
    sums = [[[operands.term(piece) for piece in entry] for entry in entries] for entries in sums]
    rows, block = operands.arrays[0].shape[-2:]
    whole = pl.BlockSpec(memory_space=VMEM)
    shapes = [(rows, block) if len(e) == 1 else (len(e), rows, block) for e in sums]
    return pl.pallas_call(
        functools.partial(combine_kernel, sums, len(operands.arrays)),
        out_shape=[jax.ShapeDtypeStruct(shape, jnp.float32) for shape in shapes],
        in_specs=[whole] * len(operands.arrays)
        + [pl.BlockSpec(memory_space=pl.ANY)] * len(after),
        out_specs=[whole] * len(sums),
        compiler_params=pltpu.CompilerParams(vmem_limit_bytes=8 * MIB),
        cost_estimate=pl.CostEstimate(
            flops=rows * block, bytes_accessed=4 * rows * block, transcendentals=0
        ),
        name="combine",
    )(*operands.arrays, *after)


def stack_kernel(n_ins, *refs):
    write(refs[-1], [ref[...] for ref in refs[:n_ins]])


def stack(segments, after=()):
    whole = pl.BlockSpec(memory_space=VMEM)
    shape = (len(segments),) + segments[0].shape
    return pl.pallas_call(
        functools.partial(stack_kernel, len(segments)),
        out_shape=jax.ShapeDtypeStruct(shape, jnp.float32),
        in_specs=[whole] * len(segments) + [pl.BlockSpec(memory_space=pl.ANY)] * len(after),
        out_specs=whole,
        compiler_params=pltpu.CompilerParams(vmem_limit_bytes=8 * MIB),
        name="stack",
    )(*segments, *after)


def far_exchange(segment, axis):
    size = lax.axis_size(axis)
    return lax.ppermute(segment, axis, [(i, i ^ (size // 2)) for i in range(size)])


def mirrored(number, size):
    bits = size.bit_length() - 1
    return sum(((number >> bit) & 1) << (bits - 1 - bit) for bit in range(bits))


def near_exchange(message, bit):
    n_row, n_col = lax.axis_size("row"), lax.axis_size("col")
    pairs = []
    for row in range(n_row):
        for col in range(n_col):
            partner = row ^ (mirrored(bit, n_row // 2) if col % 2 else bit)
            pairs.append((row * n_col + col, partner * n_col + col))
    return lax.ppermute(message, ("row", "col"), pairs)


def bits_below(size):
    return [1 << place for place in range(size.bit_length() - 1)]


def both_sides(message):
    return [(message, side) for side in range(2)]


def gather_row(segment, after):
    half = lax.axis_size("row") // 2
    received = far_exchange(segment, "row")
    (both,) = combine([[[(segment, None)], [(received, None)]]], after)
    held = {0: both}
    for bit in reversed(bits_below(half)):
        for d in sorted(held):
            held[d | bit] = near_exchange(held[d], bit)
    return [piece for d in range(half) for piece in both_sides(held[d])]


def deliver_row(messages):
    held = {d: [message] for d, message in enumerate(messages)}
    for bit in bits_below(len(messages)):
        for d in sorted((d for d in held if d & bit), reverse=True):
            parts = held.pop(d)
            message = parts[0]
            if len(parts) > 1:
                sides = [list(pieces) for pieces in zip(*map(both_sides, parts))]
                (message,) = combine([sides])
            held[d ^ bit].append(near_exchange(message, bit))
    sides = [list(pieces) for pieces in zip(*map(both_sides, held[0]))]
    mine, other = combine([[side] for side in sides])
    return [(mine, None), (far_exchange(other, "row"), None)]


def exchange_each(messages, axis):
    size = lax.axis_size(axis)
    received = {0: messages[0]}
    for d in reversed(range(1, len(messages))):
        received[d] = lax.ppermute(messages[d], axis, [(i, i ^ d) for i in range(size)])
    return [received[d] for d in range(len(messages))]


def direct_shards(rhs, diag_inv, blocks, blk_target, blk_source, blk_count):
    levels = rhs.shape[0]
    n_row, n_col = lax.axis_size("row"), lax.axis_size("col")
    right = rhs.reshape((levels,) + rhs.shape[-2:])
    inverse = diag_inv.reshape((levels,) + diag_inv.shape[-2:])
    weights = blocks.reshape((levels - 1,) + blocks.shape[-3:])
    here = [lax.axis_index(axis).astype(jnp.int32) for axis in ("row", "col")]
    slots = jnp.concatenate(
        [blk_target.reshape(levels - 1, -1), blk_source.reshape(levels - 1, -1)]
        + [blk_count.reshape(levels - 1, 1)]
        + [jnp.full((levels - 1, 1), index) for index in here],
        axis=1,
    )
    gather = lambda level, after: gather_blocks(level, slots, weights, n_row, n_col, after)
    tidy = lambda level, flipped, after: split(totals[level], n_row, n_col, flipped, after)
    forward = [first_solve(right, inverse)]
    totals = [gather(0, ())]
    up, down = [], []
    for level in range(1, levels):
        solved = forward[-1:]
        up.append(tidy(level - 1, False, solved if level > 1 else ()))
        if level > 1:
            down.append(tidy(level - 2, True, solved))
        pieces = gather_row(forward[-1], [pair[0] for pair in up[-1:] + down[-1:]])
        far = couple(pieces, *up[-1], (n_col // 2, n_col), 1)
        near = couple(pieces, *up[-1], (0, n_col // 2), 1)
        if level < levels - 1:
            totals.append(gather(level, near[:1]))
            after = totals[-1:]
        else:
            down.append(tidy(level - 1, True, near[:1]))
            after = down[-1][:1]
        pieces = plain(reversed(exchange_each(near + far, "col")))
        forward.append(solve(right, inverse, level, pieces, False, after))
    backward = [None] * levels
    backward[-1] = solve(forward[-1], inverse, levels - 1, [], True)
    for level in range(levels - 2, -1, -1):
        pieces = plain(exchange_each([backward[level + 1]] * n_col, "col"))
        first = couple(pieces, *down[level], (n_row - 2, n_row), 2)
        later = couple(pieces, *down[level], (0, n_row - 2), 2)
        if level == levels - 2:
            forward_out = stack(forward, later[:1])
        pieces = deliver_row(later + first)
        after = (forward_out,) if level == levels - 2 else ()
        backward[level] = solve(forward[level], inverse, level, pieces, True, after)
    return forward_out.reshape(rhs.shape), stack(backward).reshape(rhs.shape)


def plain(messages):
    return [(message, None) for message in messages]


def fold_for(index, piece):
    entry_count = piece.shape[0]
    onehot = (index[:, None] == jnp.arange(entry_count, dtype=jnp.int32)[None, :]).astype(
        jnp.float32
    )
    return jnp.dot(
        onehot,
        piece.reshape(entry_count, -1),
        precision=HIGH_PRECISION,
        preferred_element_type=jnp.float32,
    )


def route_sum(index, entry_count, block_products, width):
    slot_count = block_products.shape[0]
    active_flags = jnp.arange(slot_count, dtype=jnp.int32) < entry_count
    routing_table = (
        (index[None, :] == jnp.arange(width, dtype=jnp.int32)[:, None]) & active_flags[None, :]
    ).astype(jnp.float32)
    return jnp.dot(
        routing_table,
        block_products.reshape(slot_count, -1),
        precision=HIGH_PRECISION,
        preferred_element_type=jnp.float32,
    )


def forward_level(previous, weight_matrix, target, source, entry_count):
    slot_count = weight_matrix.shape[0]
    slots, rhs_column_count, block_ordering = previous.shape
    selected_blocks = fold_for(source, lax.all_gather(previous, "row", axis=0, tiled=True))
    block_products = jnp.einsum(
        "ado,aon->adn",
        selected_blocks.reshape(slot_count, rhs_column_count, block_ordering),
        weight_matrix,
        precision=HIGH_PRECISION,
    )
    ncol = lax.axis_size("col")
    buckets = route_sum(target, entry_count, block_products, ncol * slots).reshape(
        ncol, slots, rhs_column_count, block_ordering
    )
    own = lax.psum_scatter(buckets, "col", scatter_dimension=0, tiled=True)[0]
    return own


def backward_level(upper, weight_matrix, target, source, entry_count):
    slot_count = weight_matrix.shape[0]
    slots, rhs_column_count, block_ordering = upper.shape
    selected_blocks = fold_for(target, lax.all_gather(upper, "col", axis=0, tiled=True))
    block_products = jnp.einsum(
        "mlv,mtv->mlt",
        selected_blocks.reshape(slot_count, rhs_column_count, block_ordering),
        weight_matrix,
        precision=HIGH_PRECISION,
    )
    nrow = lax.axis_size("row")
    buckets = route_sum(source, entry_count, block_products, nrow * slots).reshape(
        nrow, slots, rhs_column_count, block_ordering
    )
    own = lax.psum_scatter(buckets, "row", scatter_dimension=0, tiled=True)[0]
    return own


def shards(rhs, diag_inv, blocks, blk_target, blk_source, blk_count):
    levels = rhs.shape[0]
    right = rhs[:, 0, 0]
    inverse = diag_inv[:, 0, 0]
    weight_matrix = blocks[:, 0, 0]
    targets = blk_target[:, 0, 0]
    sources = blk_source[:, 0, 0]
    counts = blk_count[:, 0, 0]
    forward = [jnp.einsum("srb,sbc->src", right[0], inverse[0], precision=HIGH_PRECISION)]
    for level in range(1, levels):
        own = forward_level(
            forward[-1],
            weight_matrix[level - 1],
            targets[level - 1],
            sources[level - 1],
            counts[level - 1],
        )
        forward.append(
            jnp.einsum("srb,sbc->src", right[level] - own, inverse[level], precision=HIGH_PRECISION)
        )
    backward = [None] * levels
    backward[levels - 1] = jnp.einsum(
        "src,sbc->srb", forward[levels - 1], inverse[levels - 1], precision=HIGH_PRECISION
    )
    for level in range(levels - 2, -1, -1):
        own = backward_level(
            backward[level + 1], weight_matrix[level], targets[level], sources[level], counts[level]
        )
        backward[level] = jnp.einsum(
            "src,sbc->srb", forward[level] - own, inverse[level], precision=HIGH_PRECISION
        )
    forward_out = jnp.stack(forward)[:, None, None]
    backward_out = jnp.stack(backward)[:, None, None]
    return (forward_out, backward_out)


def solution(mesh):
    placed = (
        P(None, "row", "col", None, None, None),
        P(None, "row", "col", None, None, None),
        P(None, "row", "col", None, None, None),
        P(None, "row", "col", None),
        P(None, "row", "col", None),
        P(None, "row", "col"),
    )
    n_row, n_col = mesh.shape["row"], mesh.shape["col"]

    def local(rhs, diag_inv, blocks, blk_target, blk_source, blk_count):
        sizes = (n_row, n_col)
        dense = n_row * n_col <= blocks.shape[3] and rhs.shape[3] == 1
        even = n_row > 2 and n_col > 1 and all(size & (size - 1) == 0 for size in sizes)
        run = direct_shards if dense and even else shards
        return run(rhs, diag_inv, blocks, blk_target, blk_source, blk_count)

    return jax.shard_map(
        local,
        mesh=mesh,
        in_specs=placed,
        out_specs=(
            P(None, "row", "col", None, None, None),
            P(None, "row", "col", None, None, None),
        ),
        check_vma=False,
    )
```

```python
import functools

import jax
import jax.numpy as jnp
from jax import lax
from jax.experimental import pallas as pl
from jax.experimental.pallas import tpu as pltpu
from jax.sharding import PartitionSpec as P

HIGH_PRECISION = lax.Precision.HIGHEST
MIB = 1024 * 1024
VMEM = pltpu.MemorySpace.VMEM
SMEM = pltpu.MemorySpace.SMEM


def halves(value):
    high = value.astype(jnp.bfloat16)
    low = (value - high.astype(jnp.float32)).astype(jnp.bfloat16)
    return high, low


def product(left, right, transposed):
    contract = (((1,), (1 if transposed else 0,)), ((), ()))
    dot = functools.partial(
        lax.dot_general, dimension_numbers=contract, preferred_element_type=jnp.float32
    )
    return dot(left[0], right[0]) + (dot(left[0], right[1]) + dot(left[1], right[0]))


def gather_blocks_kernel(
    n_row, n_col, level, chunk, slots_ref, blocks_ref, *refs
):
    total, slots, arrived = refs[-3:]
    slot_count = slots.shape[0]
    count, row, col = (slots_ref[level, 2 * slot_count + place] for place in range(3))
    half = n_row // 2
    side = row // half

    def fetch(number):
        span = pl.ds(number * chunk, chunk)
        return pltpu.make_async_copy(
            blocks_ref.at[level, span], slots.at[span], arrived.at[number]
        )

    for number in range(arrived.shape[0]):
        pl.when(number * chunk < count)(fetch(number).start)
    total[...] = jnp.zeros_like(total)

    def add(slot, carry):
        pl.when(lax.rem(slot, chunk) == 0)(fetch(slot // chunk).wait)
        source = slots_ref[level, slot_count + slot]
        near = lax.rem(source, half) ^ lax.rem(row, half)
        near = jnp.where(lax.rem(col, 2) == 1, lax.rem(half - near, half), near)
        below = near * 2 + ((source // half) ^ side)
        above = slots_ref[level, slot] ^ col
        total[below * n_col + above] += slots[slot]
        return carry

    lax.fori_loop(0, count, add, 0)


def gather_blocks(level, slots, blocks, n_row, n_col, after):
    slot_count, block = blocks.shape[1], blocks.shape[2]
    chunk = max(1, slot_count // 4)
    shape = (n_row * n_col, block, block)
    scalars = pl.BlockSpec(memory_space=SMEM)
    return pl.pallas_call(
        functools.partial(gather_blocks_kernel, n_row, n_col, level, chunk),
        out_shape=jax.ShapeDtypeStruct(shape, jnp.float32),
        in_specs=[scalars] + [pl.BlockSpec(memory_space=pl.ANY)] * (1 + len(after)),
        out_specs=pl.BlockSpec(memory_space=VMEM),
        scratch_shapes=[
            pltpu.VMEM((slot_count, block, block), jnp.float32),
            pltpu.SemaphoreType.DMA((slot_count // chunk,)),
        ],
        compiler_params=pltpu.CompilerParams(vmem_limit_bytes=(51 if level == 0 else 16) * MIB),
        cost_estimate=pl.CostEstimate(
            flops=slot_count * block * block,
            bytes_accessed=8 * slot_count * block * block,
            transcendentals=0,
        ),
        name=f"gather_blocks_{level}",
    )(slots, blocks, *after)


def split_kernel(n_col, flipped, total_ref, *refs):
    high_ref, low_ref = refs[-2:]
    block = total_ref.shape[-1]
    for pair in range(total_ref.shape[0]):
        at = (pair % n_col, pair // n_col) if flipped else (pair // n_col, pair % n_col)
        rows, lanes = (pl.ds(place * block, block) for place in at)
        high, low = halves(total_ref[pair].T if flipped else total_ref[pair])
        high_ref[rows, lanes] = high
        low_ref[rows, lanes] = low


def split(total, n_row, n_col, flipped, after):
    block = total.shape[-1]
    sizes = (n_col, n_row) if flipped else (n_row, n_col)
    shape = jax.ShapeDtypeStruct(tuple(size * block for size in sizes), jnp.bfloat16)
    whole = pl.BlockSpec(memory_space=VMEM)
    return pl.pallas_call(
        functools.partial(split_kernel, n_col, flipped),
        out_shape=[shape, shape],
        in_specs=[whole] + [pl.BlockSpec(memory_space=pl.ANY)] * len(after),
        out_specs=[whole, whole],
        compiler_params=pltpu.CompilerParams(vmem_limit_bytes=8 * MIB),
        cost_estimate=pl.CostEstimate(
            flops=3 * total.size, bytes_accessed=8 * total.size, transcendentals=0
        ),
        name="flip" if flipped else "split",
    )(total, *after)


def read(term, refs):
    number, place = term
    return refs[number][...] if place is None else refs[number][place]


def total_of(terms, refs):
    value = read(terms[0], refs)
    for term in terms[1:]:
        value += read(term, refs)
    return value


def write(ref, values):
    if len(ref.shape) == 2:
        ref[...] = values[0]
    else:
        for place, value in enumerate(values):
            ref[place] = value


class Operands:
    def __init__(self):
        self.arrays = []

    def term(self, piece):
        array, place = piece
        for number, known in enumerate(self.arrays):
            if known is array:
                return number, place
        self.arrays.append(array)
        return len(self.arrays) - 1, place


def couple_kernel(terms, span, high_ref, low_ref, *refs):
    n_in = 1 + max(number for number, _ in terms)
    ins, outs = refs[:n_in], refs[n_in:]
    block = ins[0].shape[-1]
    joined = jnp.concatenate([read(term, ins) for term in terms], axis=1)
    wanted = pl.ds(span[0] * block, (span[1] - span[0]) * block)
    result = product(halves(joined), (high_ref[:, wanted], low_ref[:, wanted]), False)
    pieces = [result[:, at : at + block] for at in range(0, result.shape[1], block)]
    each = len(pieces) // len(outs)
    for number, ref in enumerate(outs):
        write(ref, pieces[number * each : (number + 1) * each])


def couple(pieces, high, low, span, each):
    operands = Operands()
    terms = [operands.term(piece) for piece in pieces]
    rows, block = operands.arrays[0].shape[-2:]
    shape = (rows, block) if each == 1 else (each, rows, block)
    n_out = (span[1] - span[0]) // each
    whole = pl.BlockSpec(memory_space=VMEM)
    work = rows * block * block * len(terms) * (span[1] - span[0])
    return pl.pallas_call(
        functools.partial(couple_kernel, terms, span),
        out_shape=[jax.ShapeDtypeStruct(shape, jnp.float32)] * n_out,
        in_specs=[whole] * (2 + len(operands.arrays)),
        out_specs=[whole] * n_out,
        compiler_params=pltpu.CompilerParams(vmem_limit_bytes=16 * MIB),
        cost_estimate=pl.CostEstimate(
            flops=6 * work, bytes_accessed=4 * work // rows, transcendentals=0
        ),
        name="couple",
    )(high, low, *operands.arrays)


def first_solve_kernel(right_ref, inverse_ref, out_ref, right, inverse, arrived):
    fetches = [
        pltpu.make_async_copy(right_ref.at[0], right, arrived.at[0]),
        pltpu.make_async_copy(inverse_ref.at[0], inverse, arrived.at[1]),
    ]
    for fetch in fetches:
        fetch.start()
    for fetch in fetches:
        fetch.wait()
    out_ref[...] = product(halves(right[...]), halves(inverse[...]), False)


def first_solve(right, inverse):
    rows, block = right.shape[-2:]
    return pl.pallas_call(
        first_solve_kernel,
        out_shape=jax.ShapeDtypeStruct((rows, block), jnp.float32),
        in_specs=[pl.BlockSpec(memory_space=pl.ANY)] * 2,
        out_specs=pl.BlockSpec(memory_space=VMEM),
        scratch_shapes=[
            pltpu.VMEM((rows, block), jnp.float32),
            pltpu.VMEM((block, block), jnp.float32),
            pltpu.SemaphoreType.DMA((2,)),
        ],
        compiler_params=pltpu.CompilerParams(vmem_limit_bytes=60 * MIB),
        name="first_solve",
    )(right, inverse)


def solve_kernel(transposed, level, terms, n_ins, *refs):
    right_ref, inverse_ref = refs[:2]
    ins, out_ref = refs[2 : 2 + n_ins], refs[-1]
    value = right_ref[level] if len(right_ref.shape) == 3 else right_ref[...]
    if terms:
        value -= total_of(terms, ins)
    out_ref[...] = product(halves(value), halves(inverse_ref[level]), transposed)


def solve(right, inverse, level, pieces, transposed, after=()):
    rows, block = right.shape[-2:]
    operands = Operands()
    terms = [operands.term(piece) for piece in pieces]
    whole = pl.BlockSpec(memory_space=VMEM)
    return pl.pallas_call(
        functools.partial(solve_kernel, transposed, level, terms, len(operands.arrays)),
        out_shape=jax.ShapeDtypeStruct((rows, block), jnp.float32),
        in_specs=[whole] * (2 + len(operands.arrays))
        + [pl.BlockSpec(memory_space=pl.ANY)] * len(after),
        out_specs=whole,
        compiler_params=pltpu.CompilerParams(vmem_limit_bytes=8 * MIB),
        cost_estimate=pl.CostEstimate(
            flops=6 * rows * block * block, bytes_accessed=4 * block * block, transcendentals=0
        ),
        name="solve_up" if not transposed else "solve_down",
    )(right, inverse, *operands.arrays, *after)


def combine_kernel(sums, n_ins, *refs):
    ins, outs = refs[:n_ins], refs[-len(sums) :]
    for terms, ref in zip(sums, outs):
        write(ref, [total_of(entry, ins) for entry in terms])


def combine(sums, after=()):
    operands = Operands()
    sums = [[[operands.term(piece) for piece in entry] for entry in entries] for entries in sums]
    rows, block = operands.arrays[0].shape[-2:]
    whole = pl.BlockSpec(memory_space=VMEM)
    shapes = [(rows, block) if len(e) == 1 else (len(e), rows, block) for e in sums]
    return pl.pallas_call(
        functools.partial(combine_kernel, sums, len(operands.arrays)),
        out_shape=[jax.ShapeDtypeStruct(shape, jnp.float32) for shape in shapes],
        in_specs=[whole] * len(operands.arrays)
        + [pl.BlockSpec(memory_space=pl.ANY)] * len(after),
        out_specs=[whole] * len(sums),
        compiler_params=pltpu.CompilerParams(vmem_limit_bytes=8 * MIB),
        cost_estimate=pl.CostEstimate(
            flops=rows * block, bytes_accessed=4 * rows * block, transcendentals=0
        ),
        name="combine",
    )(*operands.arrays, *after)


def stack_kernel(n_ins, *refs):
    write(refs[-1], [ref[...] for ref in refs[:n_ins]])


def stack(segments, after=()):
    whole = pl.BlockSpec(memory_space=VMEM)
    shape = (len(segments),) + segments[0].shape
    return pl.pallas_call(
        functools.partial(stack_kernel, len(segments)),
        out_shape=jax.ShapeDtypeStruct(shape, jnp.float32),
        in_specs=[whole] * len(segments) + [pl.BlockSpec(memory_space=pl.ANY)] * len(after),
        out_specs=whole,
        compiler_params=pltpu.CompilerParams(vmem_limit_bytes=8 * MIB),
        name="stack",
    )(*segments, *after)


def far_exchange(segment, axis):
    size = lax.axis_size(axis)
    return lax.ppermute(segment, axis, [(i, i ^ (size // 2)) for i in range(size)])


def mirrored(number, size):
    return (size - number) % size


def near_exchange(messages):
    n_row, n_col = lax.axis_size("row"), lax.axis_size("col")
    half = n_row // 2
    received = {0: messages[0]}
    for d in reversed(range(1, half)):
        pairs = []
        for row in range(n_row):
            for col in range(n_col):
                partner = row ^ (mirrored(d, half) if col % 2 else d)
                pairs.append((row * n_col + col, partner * n_col + col))
        received[d] = lax.ppermute(messages[d], ("row", "col"), pairs)
    return [received[d] for d in range(half)]


def gather_row(segment, after):
    half = lax.axis_size("row") // 2
    received = far_exchange(segment, "row")
    (both,) = combine([[[(segment, None)], [(received, None)]]], after)
    messages = near_exchange([both] * half)
    return [(message, side) for message in messages for side in range(2)]


def deliver_row(messages):
    received = near_exchange(messages)
    mine, other = combine(
        [
            [[(message, side) for message in [received[0], *reversed(received[1:])]]]
            for side in range(2)
        ]
    )
    return [(mine, None), (far_exchange(other, "row"), None)]


def exchange_each(messages, axis):
    size = lax.axis_size(axis)
    received = {0: messages[0]}
    for d in reversed(range(1, len(messages))):
        received[d] = lax.ppermute(messages[d], axis, [(i, i ^ d) for i in range(size)])
    return [received[d] for d in range(len(messages))]


def direct_shards(rhs, diag_inv, blocks, blk_target, blk_source, blk_count):
    levels = rhs.shape[0]
    n_row, n_col = lax.axis_size("row"), lax.axis_size("col")
    right = rhs.reshape((levels,) + rhs.shape[-2:])
    inverse = diag_inv.reshape((levels,) + diag_inv.shape[-2:])
    weights = blocks.reshape((levels - 1,) + blocks.shape[-3:])
    here = [lax.axis_index(axis).astype(jnp.int32) for axis in ("row", "col")]
    slots = jnp.concatenate(
        [blk_target.reshape(levels - 1, -1), blk_source.reshape(levels - 1, -1)]
        + [blk_count.reshape(levels - 1, 1)]
        + [jnp.full((levels - 1, 1), index) for index in here],
        axis=1,
    )
    gather = lambda level, after: gather_blocks(level, slots, weights, n_row, n_col, after)
    tidy = lambda level, flipped, after: split(totals[level], n_row, n_col, flipped, after)
    forward = [first_solve(right, inverse)]
    totals = [gather(0, ())]
    up, down = [], []
    for level in range(1, levels):
        solved = forward[-1:]
        up.append(tidy(level - 1, False, solved if level > 1 else ()))
        if level > 1:
            down.append(tidy(level - 2, True, solved))
        pieces = gather_row(forward[-1], [pair[0] for pair in up[-1:] + down[-1:]])
        far = couple(pieces, *up[-1], (n_col // 2, n_col), 1)
        near = couple(pieces, *up[-1], (0, n_col // 2), 1)
        if level < levels - 1:
            totals.append(gather(level, near[:1]))
            after = totals[-1:]
        else:
            down.append(tidy(level - 1, True, near[:1]))
            after = down[-1][:1]
        pieces = plain(reversed(exchange_each(near + far, "col")))
        forward.append(solve(right, inverse, level, pieces, False, after))
    backward = [None] * levels
    backward[-1] = solve(forward[-1], inverse, levels - 1, [], True)
    for level in range(levels - 2, -1, -1):
        pieces = plain(exchange_each([backward[level + 1]] * n_col, "col"))
        sent = couple(pieces, *down[level], (2, n_row), 2)
        kept = couple(pieces, *down[level], (0, 2), 2)
        if level == levels - 2:
            forward_out = stack(forward, kept[:1])
        pieces = deliver_row(kept + sent)
        after = (forward_out,) if level == levels - 2 else ()
        backward[level] = solve(forward[level], inverse, level, pieces, True, after)
    return forward_out.reshape(rhs.shape), stack(backward).reshape(rhs.shape)


def plain(messages):
    return [(message, None) for message in messages]


def fold_for(index, piece):
    entry_count = piece.shape[0]
    onehot = (index[:, None] == jnp.arange(entry_count, dtype=jnp.int32)[None, :]).astype(
        jnp.float32
    )
    return jnp.dot(
        onehot,
        piece.reshape(entry_count, -1),
        precision=HIGH_PRECISION,
        preferred_element_type=jnp.float32,
    )


def route_sum(index, entry_count, block_products, width):
    slot_count = block_products.shape[0]
    active_flags = jnp.arange(slot_count, dtype=jnp.int32) < entry_count
    routing_table = (
        (index[None, :] == jnp.arange(width, dtype=jnp.int32)[:, None]) & active_flags[None, :]
    ).astype(jnp.float32)
    return jnp.dot(
        routing_table,
        block_products.reshape(slot_count, -1),
        precision=HIGH_PRECISION,
        preferred_element_type=jnp.float32,
    )


def forward_level(previous, weight_matrix, target, source, entry_count):
    slot_count = weight_matrix.shape[0]
    slots, rhs_column_count, block_ordering = previous.shape
    selected_blocks = fold_for(source, lax.all_gather(previous, "row", axis=0, tiled=True))
    block_products = jnp.einsum(
        "ado,aon->adn",
        selected_blocks.reshape(slot_count, rhs_column_count, block_ordering),
        weight_matrix,
        precision=HIGH_PRECISION,
    )
    ncol = lax.axis_size("col")
    buckets = route_sum(target, entry_count, block_products, ncol * slots).reshape(
        ncol, slots, rhs_column_count, block_ordering
    )
    own = lax.psum_scatter(buckets, "col", scatter_dimension=0, tiled=True)[0]
    return own


def backward_level(upper, weight_matrix, target, source, entry_count):
    slot_count = weight_matrix.shape[0]
    slots, rhs_column_count, block_ordering = upper.shape
    selected_blocks = fold_for(target, lax.all_gather(upper, "col", axis=0, tiled=True))
    block_products = jnp.einsum(
        "mlv,mtv->mlt",
        selected_blocks.reshape(slot_count, rhs_column_count, block_ordering),
        weight_matrix,
        precision=HIGH_PRECISION,
    )
    nrow = lax.axis_size("row")
    buckets = route_sum(source, entry_count, block_products, nrow * slots).reshape(
        nrow, slots, rhs_column_count, block_ordering
    )
    own = lax.psum_scatter(buckets, "row", scatter_dimension=0, tiled=True)[0]
    return own


def shards(rhs, diag_inv, blocks, blk_target, blk_source, blk_count):
    levels = rhs.shape[0]
    right = rhs[:, 0, 0]
    inverse = diag_inv[:, 0, 0]
    weight_matrix = blocks[:, 0, 0]
    targets = blk_target[:, 0, 0]
    sources = blk_source[:, 0, 0]
    counts = blk_count[:, 0, 0]
    forward = [jnp.einsum("srb,sbc->src", right[0], inverse[0], precision=HIGH_PRECISION)]
    for level in range(1, levels):
        own = forward_level(
            forward[-1],
            weight_matrix[level - 1],
            targets[level - 1],
            sources[level - 1],
            counts[level - 1],
        )
        forward.append(
            jnp.einsum("srb,sbc->src", right[level] - own, inverse[level], precision=HIGH_PRECISION)
        )
    backward = [None] * levels
    backward[levels - 1] = jnp.einsum(
        "src,sbc->srb", forward[levels - 1], inverse[levels - 1], precision=HIGH_PRECISION
    )
    for level in range(levels - 2, -1, -1):
        own = backward_level(
            backward[level + 1], weight_matrix[level], targets[level], sources[level], counts[level]
        )
        backward[level] = jnp.einsum(
            "src,sbc->srb", forward[level] - own, inverse[level], precision=HIGH_PRECISION
        )
    forward_out = jnp.stack(forward)[:, None, None]
    backward_out = jnp.stack(backward)[:, None, None]
    return (forward_out, backward_out)


def solution(mesh):
    placed = (
        P(None, "row", "col", None, None, None),
        P(None, "row", "col", None, None, None),
        P(None, "row", "col", None, None, None),
        P(None, "row", "col", None),
        P(None, "row", "col", None),
        P(None, "row", "col"),
    )
    n_row, n_col = mesh.shape["row"], mesh.shape["col"]

    def local(rhs, diag_inv, blocks, blk_target, blk_source, blk_count):
        sizes = (n_row, n_col)
        dense = n_row * n_col <= blocks.shape[3] and rhs.shape[3] == 1
        even = all(size > 1 and size & (size - 1) == 0 for size in sizes)
        run = direct_shards if dense and even else shards
        return run(rhs, diag_inv, blocks, blk_target, blk_source, blk_count)

    return jax.shard_map(
        local,
        mesh=mesh,
        in_specs=placed,
        out_specs=(
            P(None, "row", "col", None, None, None),
            P(None, "row", "col", None, None, None),
        ),
        check_vma=False,
    )
```

```python
import functools

import jax
import jax.numpy as jnp
from jax import lax
from jax.experimental import pallas as pl
from jax.experimental.pallas import tpu as pltpu
from jax.sharding import PartitionSpec as P

HIGH_PRECISION = lax.Precision.HIGHEST
MIB = 1024 * 1024
VMEM = pltpu.MemorySpace.VMEM
SMEM = pltpu.MemorySpace.SMEM


def halves(value):
    high = value.astype(jnp.bfloat16)
    low = (value - high.astype(jnp.float32)).astype(jnp.bfloat16)
    return high, low


def product(left, right, transposed):
    contract = (((1,), (1 if transposed else 0,)), ((), ()))
    dot = functools.partial(
        lax.dot_general, dimension_numbers=contract, preferred_element_type=jnp.float32
    )
    return dot(left[0], right[0]) + (dot(left[0], right[1]) + dot(left[1], right[0]))


def gather_blocks_kernel(
    n_row, n_col, level, chunk, slots_ref, blocks_ref, *refs
):
    total, slots, arrived = refs[-3:]
    slot_count = slots.shape[0]
    count, row, col = (slots_ref[level, 2 * slot_count + place] for place in range(3))
    half = n_row // 2
    side = row // half

    def fetch(number):
        span = pl.ds(number * chunk, chunk)
        return pltpu.make_async_copy(
            blocks_ref.at[level, span], slots.at[span], arrived.at[number]
        )

    for number in range(arrived.shape[0]):
        pl.when(number * chunk < count)(fetch(number).start)
    total[...] = jnp.zeros_like(total)

    def add(slot, carry):
        pl.when(lax.rem(slot, chunk) == 0)(fetch(slot // chunk).wait)
        source = slots_ref[level, slot_count + slot]
        near = lax.rem(source, half) ^ lax.rem(row, half)
        near = jnp.where(lax.rem(col, 2) == 1, mirrored(near, half), near)
        below = near * 2 + ((source // half) ^ side)
        above = slots_ref[level, slot] ^ col
        total[below * n_col + above] += slots[slot]
        return carry

    lax.fori_loop(0, count, add, 0)


def gather_blocks(level, slots, blocks, n_row, n_col, after):
    slot_count, block = blocks.shape[1], blocks.shape[2]
    chunk = max(1, slot_count // 4)
    shape = (n_row * n_col, block, block)
    scalars = pl.BlockSpec(memory_space=SMEM)
    return pl.pallas_call(
        functools.partial(gather_blocks_kernel, n_row, n_col, level, chunk),
        out_shape=jax.ShapeDtypeStruct(shape, jnp.float32),
        in_specs=[scalars] + [pl.BlockSpec(memory_space=pl.ANY)] * (1 + len(after)),
        out_specs=pl.BlockSpec(memory_space=VMEM),
        scratch_shapes=[
            pltpu.VMEM((slot_count, block, block), jnp.float32),
            pltpu.SemaphoreType.DMA((slot_count // chunk,)),
        ],
        compiler_params=pltpu.CompilerParams(vmem_limit_bytes=(51 if level == 0 else 16) * MIB),
        cost_estimate=pl.CostEstimate(
            flops=slot_count * block * block,
            bytes_accessed=8 * slot_count * block * block,
            transcendentals=0,
        ),
        name=f"gather_blocks_{level}",
    )(slots, blocks, *after)


def split_kernel(n_col, flipped, total_ref, *refs):
    high_ref, low_ref = refs[-2:]
    block = total_ref.shape[-1]
    for pair in range(total_ref.shape[0]):
        at = (pair % n_col, pair // n_col) if flipped else (pair // n_col, pair % n_col)
        rows, lanes = (pl.ds(place * block, block) for place in at)
        high, low = halves(total_ref[pair].T if flipped else total_ref[pair])
        high_ref[rows, lanes] = high
        low_ref[rows, lanes] = low


def split(total, n_row, n_col, flipped, after):
    block = total.shape[-1]
    sizes = (n_col, n_row) if flipped else (n_row, n_col)
    shape = jax.ShapeDtypeStruct(tuple(size * block for size in sizes), jnp.bfloat16)
    whole = pl.BlockSpec(memory_space=VMEM)
    return pl.pallas_call(
        functools.partial(split_kernel, n_col, flipped),
        out_shape=[shape, shape],
        in_specs=[whole] + [pl.BlockSpec(memory_space=pl.ANY)] * len(after),
        out_specs=[whole, whole],
        compiler_params=pltpu.CompilerParams(vmem_limit_bytes=8 * MIB),
        cost_estimate=pl.CostEstimate(
            flops=3 * total.size, bytes_accessed=8 * total.size, transcendentals=0
        ),
        name="flip" if flipped else "split",
    )(total, *after)


def read(term, refs):
    number, place = term
    return refs[number][...] if place is None else refs[number][place]


def total_of(terms, refs):
    value = read(terms[0], refs)
    for term in terms[1:]:
        value += read(term, refs)
    return value


def write(ref, values):
    if len(ref.shape) == 2:
        ref[...] = values[0]
    else:
        for place, value in enumerate(values):
            ref[place] = value


class Operands:
    def __init__(self):
        self.arrays = []

    def term(self, piece):
        array, place = piece
        for number, known in enumerate(self.arrays):
            if known is array:
                return number, place
        self.arrays.append(array)
        return len(self.arrays) - 1, place


def couple_kernel(terms, entries, span, n_in, high_ref, low_ref, *refs):
    ins, bases, outs = refs[:n_in], refs[n_in:-span[2]], refs[-span[2] :]
    block = ins[0].shape[-1]
    joined = jnp.concatenate([read(term, ins) for term in terms], axis=1)
    wanted = pl.ds(span[0] * block, (span[1] - span[0]) * block)
    parts = [
        jnp.concatenate([ref[pl.ds(entry * block, block), wanted] for entry in entries], axis=0)
        for ref in (high_ref, low_ref)
    ]
    result = product(halves(joined), parts, False)
    for base_ref in bases:
        result += base_ref[:, wanted]
    if len(outs) == 1 and outs[0].shape == result.shape:
        outs[0][...] = result
        return
    pieces = [result[:, at : at + block] for at in range(0, result.shape[1], block)]
    each = len(pieces) // len(outs)
    for number, ref in enumerate(outs):
        write(ref, pieces[number * each : (number + 1) * each])


def couple(pieces, entries, high, low, span, each, base=()):
    operands = Operands()
    terms = [operands.term(pieces[entry]) for entry in entries]
    rows, block = operands.arrays[0].shape[-2:]
    width = span[1] - span[0]
    shape = {0: (rows, width * block), 1: (rows, block)}.get(each, (each, rows, block))
    n_out = width // each if each else 1
    whole = pl.BlockSpec(memory_space=VMEM)
    work = rows * block * block * len(terms) * width
    return pl.pallas_call(
        functools.partial(couple_kernel, terms, entries, (*span, n_out), len(operands.arrays)),
        out_shape=[jax.ShapeDtypeStruct(shape, jnp.float32)] * n_out,
        in_specs=[whole] * (2 + len(operands.arrays) + len(base)),
        out_specs=[whole] * n_out,
        compiler_params=pltpu.CompilerParams(vmem_limit_bytes=16 * MIB),
        cost_estimate=pl.CostEstimate(
            flops=6 * work, bytes_accessed=4 * work // rows, transcendentals=0
        ),
        name="couple" if each else "couple_early",
    )(high, low, *operands.arrays, *base)


def first_solve_kernel(right_ref, inverse_ref, out_ref, right, inverse, arrived):
    fetches = [
        pltpu.make_async_copy(right_ref.at[0], right, arrived.at[0]),
        pltpu.make_async_copy(inverse_ref.at[0], inverse, arrived.at[1]),
    ]
    for fetch in fetches:
        fetch.start()
    for fetch in fetches:
        fetch.wait()
    out_ref[...] = product(halves(right[...]), halves(inverse[...]), False)


def first_solve(right, inverse):
    rows, block = right.shape[-2:]
    return pl.pallas_call(
        first_solve_kernel,
        out_shape=jax.ShapeDtypeStruct((rows, block), jnp.float32),
        in_specs=[pl.BlockSpec(memory_space=pl.ANY)] * 2,
        out_specs=pl.BlockSpec(memory_space=VMEM),
        scratch_shapes=[
            pltpu.VMEM((rows, block), jnp.float32),
            pltpu.VMEM((block, block), jnp.float32),
            pltpu.SemaphoreType.DMA((2,)),
        ],
        compiler_params=pltpu.CompilerParams(vmem_limit_bytes=60 * MIB),
        name="first_solve",
    )(right, inverse)


def solve_kernel(transposed, level, terms, n_ins, *refs):
    right_ref, inverse_ref = refs[:2]
    ins, out_ref = refs[2 : 2 + n_ins], refs[-1]
    value = right_ref[level] if len(right_ref.shape) == 3 else right_ref[...]
    if terms:
        value -= total_of(terms, ins)
    out_ref[...] = product(halves(value), halves(inverse_ref[level]), transposed)


def solve(right, inverse, level, pieces, transposed, after=()):
    rows, block = right.shape[-2:]
    operands = Operands()
    terms = [operands.term(piece) for piece in pieces]
    whole = pl.BlockSpec(memory_space=VMEM)
    return pl.pallas_call(
        functools.partial(solve_kernel, transposed, level, terms, len(operands.arrays)),
        out_shape=jax.ShapeDtypeStruct((rows, block), jnp.float32),
        in_specs=[whole] * (2 + len(operands.arrays))
        + [pl.BlockSpec(memory_space=pl.ANY)] * len(after),
        out_specs=whole,
        compiler_params=pltpu.CompilerParams(vmem_limit_bytes=8 * MIB),
        cost_estimate=pl.CostEstimate(
            flops=6 * rows * block * block, bytes_accessed=4 * block * block, transcendentals=0
        ),
        name="solve_up" if not transposed else "solve_down",
    )(right, inverse, *operands.arrays, *after)


def combine_kernel(sums, n_ins, *refs):
    ins, outs = refs[:n_ins], refs[-len(sums) :]
    for terms, ref in zip(sums, outs):
        write(ref, [total_of(entry, ins) for entry in terms])


def combine(sums, after=()):
    operands = Operands()
    sums = [[[operands.term(piece) for piece in entry] for entry in entries] for entries in sums]
    rows, block = operands.arrays[0].shape[-2:]
    whole = pl.BlockSpec(memory_space=VMEM)
    shapes = [(rows, block) if len(e) == 1 else (len(e), rows, block) for e in sums]
    return pl.pallas_call(
        functools.partial(combine_kernel, sums, len(operands.arrays)),
        out_shape=[jax.ShapeDtypeStruct(shape, jnp.float32) for shape in shapes],
        in_specs=[whole] * len(operands.arrays)
        + [pl.BlockSpec(memory_space=pl.ANY)] * len(after),
        out_specs=[whole] * len(sums),
        compiler_params=pltpu.CompilerParams(vmem_limit_bytes=8 * MIB),
        cost_estimate=pl.CostEstimate(
            flops=rows * block, bytes_accessed=4 * rows * block, transcendentals=0
        ),
        name="combine",
    )(*operands.arrays, *after)


def stack_kernel(n_ins, *refs):
    write(refs[-1], [ref[...] for ref in refs[:n_ins]])


def stack(segments, after=()):
    whole = pl.BlockSpec(memory_space=VMEM)
    shape = (len(segments),) + segments[0].shape
    return pl.pallas_call(
        functools.partial(stack_kernel, len(segments)),
        out_shape=jax.ShapeDtypeStruct(shape, jnp.float32),
        in_specs=[whole] * len(segments) + [pl.BlockSpec(memory_space=pl.ANY)] * len(after),
        out_specs=whole,
        compiler_params=pltpu.CompilerParams(vmem_limit_bytes=8 * MIB),
        name="stack",
    )(*segments, *after)


def far_exchange(segment, axis):
    size = lax.axis_size(axis)
    return lax.ppermute(segment, axis, [(i, i ^ (size // 2)) for i in range(size)])


def mirrored(number, size):
    bits = size.bit_length() - 1
    return sum(((number >> bit) & 1) << (bits - 1 - bit) for bit in range(bits))


def near_exchange(messages):
    n_row, n_col = lax.axis_size("row"), lax.axis_size("col")
    half = n_row // 2
    received = {0: messages[0]}
    for d in reversed(range(1, half)):
        pairs = []
        for row in range(n_row):
            for col in range(n_col):
                partner = row ^ (mirrored(d, half) if col % 2 else d)
                pairs.append((row * n_col + col, partner * n_col + col))
        received[d] = lax.ppermute(messages[d], ("row", "col"), pairs)
    return [received[d] for d in range(half)]


def gather_row(segment, after):
    half = lax.axis_size("row") // 2
    received = far_exchange(segment, "row")
    (both,) = combine([[[(segment, None)], [(received, None)]]], after)
    messages = near_exchange([both] * half)
    return [(message, side) for message in messages for side in range(2)]


def deliver_row(messages):
    received = near_exchange(messages)
    mine, other = combine(
        [
            [[(message, side) for message in [received[0], *reversed(received[1:])]]]
            for side in range(2)
        ]
    )
    return [(mine, None), (far_exchange(other, "row"), None)]


def exchange_each(messages, axis):
    size = lax.axis_size(axis)
    received = {0: messages[0]}
    for d in reversed(range(1, len(messages))):
        received[d] = lax.ppermute(messages[d], axis, [(i, i ^ d) for i in range(size)])
    return [received[d] for d in range(len(messages))]


def direct_shards(rhs, diag_inv, blocks, blk_target, blk_source, blk_count):
    levels = rhs.shape[0]
    n_row, n_col = lax.axis_size("row"), lax.axis_size("col")
    right = rhs.reshape((levels,) + rhs.shape[-2:])
    inverse = diag_inv.reshape((levels,) + diag_inv.shape[-2:])
    weights = blocks.reshape((levels - 1,) + blocks.shape[-3:])
    here = [lax.axis_index(axis).astype(jnp.int32) for axis in ("row", "col")]
    slots = jnp.concatenate(
        [blk_target.reshape(levels - 1, -1), blk_source.reshape(levels - 1, -1)]
        + [blk_count.reshape(levels - 1, 1)]
        + [jnp.full((levels - 1, 1), index) for index in here],
        axis=1,
    )
    gather = lambda level, after: gather_blocks(level, slots, weights, n_row, n_col, after)
    tidy = lambda level, flipped, after: split(totals[level], n_row, n_col, flipped, after)
    forward = [first_solve(right, inverse)]
    totals = [gather(0, ())]
    up, down = [], []
    for level in range(1, levels):
        solved = forward[-1:]
        up.append(tidy(level - 1, False, solved if level > 1 else ()))
        if level > 1:
            down.append(tidy(level - 2, True, solved))
        pieces = gather_row(forward[-1], [pair[0] for pair in up[-1:] + down[-1:]])
        base = couple(pieces, [0, 1, *range(4, n_row)], *up[-1], (0, n_col), 0)
        far = couple(pieces, [2, 3], *up[-1], (n_col // 2, n_col), 1, base)
        near = couple(pieces, [2, 3], *up[-1], (0, n_col // 2), 1, base)
        if level < levels - 1:
            totals.append(gather(level, near[:1]))
            after = totals[-1:]
        else:
            down.append(tidy(level - 1, True, near[:1]))
            after = down[-1][:1]
        pieces = plain(reversed(exchange_each(near + far, "col")))
        forward.append(solve(right, inverse, level, pieces, False, after))
    backward = [None] * levels
    backward[-1] = solve(forward[-1], inverse, levels - 1, [], True)
    for level in range(levels - 2, -1, -1):
        pieces = plain(exchange_each([backward[level + 1]] * n_col, "col"))
        late = list(range(n_col - 2, 0, -1))
        base = couple(pieces, [0, n_col - 1], *down[level], (0, n_row), 0)
        sent = couple(pieces, late, *down[level], (2, n_row), 2, base)
        kept = couple(pieces, late, *down[level], (0, 2), 2, base)
        if level == levels - 2:
            forward_out = stack(forward, kept[:1])
        pieces = deliver_row(kept + sent)
        after = (forward_out,) if level == levels - 2 else ()
        backward[level] = solve(forward[level], inverse, level, pieces, True, after)
    return forward_out.reshape(rhs.shape), stack(backward).reshape(rhs.shape)


def plain(messages):
    return [(message, None) for message in messages]


def fold_for(index, piece):
    entry_count = piece.shape[0]
    onehot = (index[:, None] == jnp.arange(entry_count, dtype=jnp.int32)[None, :]).astype(
        jnp.float32
    )
    return jnp.dot(
        onehot,
        piece.reshape(entry_count, -1),
        precision=HIGH_PRECISION,
        preferred_element_type=jnp.float32,
    )


def route_sum(index, entry_count, block_products, width):
    slot_count = block_products.shape[0]
    active_flags = jnp.arange(slot_count, dtype=jnp.int32) < entry_count
    routing_table = (
        (index[None, :] == jnp.arange(width, dtype=jnp.int32)[:, None]) & active_flags[None, :]
    ).astype(jnp.float32)
    return jnp.dot(
        routing_table,
        block_products.reshape(slot_count, -1),
        precision=HIGH_PRECISION,
        preferred_element_type=jnp.float32,
    )


def forward_level(previous, weight_matrix, target, source, entry_count):
    slot_count = weight_matrix.shape[0]
    slots, rhs_column_count, block_ordering = previous.shape
    selected_blocks = fold_for(source, lax.all_gather(previous, "row", axis=0, tiled=True))
    block_products = jnp.einsum(
        "ado,aon->adn",
        selected_blocks.reshape(slot_count, rhs_column_count, block_ordering),
        weight_matrix,
        precision=HIGH_PRECISION,
    )
    ncol = lax.axis_size("col")
    buckets = route_sum(target, entry_count, block_products, ncol * slots).reshape(
        ncol, slots, rhs_column_count, block_ordering
    )
    own = lax.psum_scatter(buckets, "col", scatter_dimension=0, tiled=True)[0]
    return own


def backward_level(upper, weight_matrix, target, source, entry_count):
    slot_count = weight_matrix.shape[0]
    slots, rhs_column_count, block_ordering = upper.shape
    selected_blocks = fold_for(target, lax.all_gather(upper, "col", axis=0, tiled=True))
    block_products = jnp.einsum(
        "mlv,mtv->mlt",
        selected_blocks.reshape(slot_count, rhs_column_count, block_ordering),
        weight_matrix,
        precision=HIGH_PRECISION,
    )
    nrow = lax.axis_size("row")
    buckets = route_sum(source, entry_count, block_products, nrow * slots).reshape(
        nrow, slots, rhs_column_count, block_ordering
    )
    own = lax.psum_scatter(buckets, "row", scatter_dimension=0, tiled=True)[0]
    return own


def shards(rhs, diag_inv, blocks, blk_target, blk_source, blk_count):
    levels = rhs.shape[0]
    right = rhs[:, 0, 0]
    inverse = diag_inv[:, 0, 0]
    weight_matrix = blocks[:, 0, 0]
    targets = blk_target[:, 0, 0]
    sources = blk_source[:, 0, 0]
    counts = blk_count[:, 0, 0]
    forward = [jnp.einsum("srb,sbc->src", right[0], inverse[0], precision=HIGH_PRECISION)]
    for level in range(1, levels):
        own = forward_level(
            forward[-1],
            weight_matrix[level - 1],
            targets[level - 1],
            sources[level - 1],
            counts[level - 1],
        )
        forward.append(
            jnp.einsum("srb,sbc->src", right[level] - own, inverse[level], precision=HIGH_PRECISION)
        )
    backward = [None] * levels
    backward[levels - 1] = jnp.einsum(
        "src,sbc->srb", forward[levels - 1], inverse[levels - 1], precision=HIGH_PRECISION
    )
    for level in range(levels - 2, -1, -1):
        own = backward_level(
            backward[level + 1], weight_matrix[level], targets[level], sources[level], counts[level]
        )
        backward[level] = jnp.einsum(
            "src,sbc->srb", forward[level] - own, inverse[level], precision=HIGH_PRECISION
        )
    forward_out = jnp.stack(forward)[:, None, None]
    backward_out = jnp.stack(backward)[:, None, None]
    return (forward_out, backward_out)


def solution(mesh):
    placed = (
        P(None, "row", "col", None, None, None),
        P(None, "row", "col", None, None, None),
        P(None, "row", "col", None, None, None),
        P(None, "row", "col", None),
        P(None, "row", "col", None),
        P(None, "row", "col"),
    )
    n_row, n_col = mesh.shape["row"], mesh.shape["col"]

    def local(rhs, diag_inv, blocks, blk_target, blk_source, blk_count):
        sizes = (n_row, n_col)
        dense = n_row * n_col <= blocks.shape[3] and rhs.shape[3] == 1
        even = n_row > 2 and n_col > 2 and all(size & (size - 1) == 0 for size in sizes)
        run = direct_shards if dense and even else shards
        return run(rhs, diag_inv, blocks, blk_target, blk_source, blk_count)

    return jax.shard_map(
        local,
        mesh=mesh,
        in_specs=placed,
        out_specs=(
            P(None, "row", "col", None, None, None),
            P(None, "row", "col", None, None, None),
        ),
        check_vma=False,
    )
```

```python
import functools

import jax
import jax.numpy as jnp
from jax import lax
from jax.experimental import pallas as pl
from jax.experimental.pallas import tpu as pltpu
from jax.sharding import PartitionSpec as P

HIGH_PRECISION = lax.Precision.HIGHEST
MIB = 1024 * 1024
VMEM = pltpu.MemorySpace.VMEM
SMEM = pltpu.MemorySpace.SMEM


def halves(value):
    high = value.astype(jnp.bfloat16)
    low = (value - high.astype(jnp.float32)).astype(jnp.bfloat16)
    return high, low


def product(left, right, transposed):
    contract = (((1,), (1 if transposed else 0,)), ((), ()))
    dot = functools.partial(
        lax.dot_general, dimension_numbers=contract, preferred_element_type=jnp.float32
    )
    return dot(left[0], right[0]) + (dot(left[0], right[1]) + dot(left[1], right[0]))


def gather_blocks_kernel(
    n_row, n_col, level, chunk, slots_ref, blocks_ref, *refs
):
    total, slots, arrived = refs[-3:]
    slot_count = slots.shape[0]
    count, row, col = (slots_ref[level, 2 * slot_count + place] for place in range(3))
    half = n_row // 2
    side = row // half

    def fetch(number):
        span = pl.ds(number * chunk, chunk)
        return pltpu.make_async_copy(
            blocks_ref.at[level, span], slots.at[span], arrived.at[number]
        )

    for number in range(arrived.shape[0]):
        pl.when(number * chunk < count)(fetch(number).start)
    total[...] = jnp.zeros_like(total)

    def add(slot, carry):
        pl.when(lax.rem(slot, chunk) == 0)(fetch(slot // chunk).wait)
        source = slots_ref[level, slot_count + slot]
        near = lax.rem(source, half) ^ lax.rem(row, half)
        near = jnp.where(lax.rem(col, 2) == 1, mirrored(near, half), near)
        below = near * 2 + ((source // half) ^ side)
        above = slots_ref[level, slot] ^ col
        total[below * n_col + above] += slots[slot]
        return carry

    lax.fori_loop(0, count, add, 0)


def gather_blocks(level, slots, blocks, n_row, n_col, after):
    slot_count, block = blocks.shape[1], blocks.shape[2]
    chunk = max(1, slot_count // 4)
    shape = (n_row * n_col, block, block)
    scalars = pl.BlockSpec(memory_space=SMEM)
    return pl.pallas_call(
        functools.partial(gather_blocks_kernel, n_row, n_col, level, chunk),
        out_shape=jax.ShapeDtypeStruct(shape, jnp.float32),
        in_specs=[scalars] + [pl.BlockSpec(memory_space=pl.ANY)] * (1 + len(after)),
        out_specs=pl.BlockSpec(memory_space=VMEM),
        scratch_shapes=[
            pltpu.VMEM((slot_count, block, block), jnp.float32),
            pltpu.SemaphoreType.DMA((slot_count // chunk,)),
        ],
        compiler_params=pltpu.CompilerParams(vmem_limit_bytes=(51 if level == 0 else 16) * MIB),
        cost_estimate=pl.CostEstimate(
            flops=slot_count * block * block,
            bytes_accessed=8 * slot_count * block * block,
            transcendentals=0,
        ),
        name=f"gather_blocks_{level}",
    )(slots, blocks, *after)


def split_kernel(n_col, flipped, total_ref, *refs):
    high_ref, low_ref = refs[-2:]
    block = total_ref.shape[-1]
    for pair in range(total_ref.shape[0]):
        at = (pair % n_col, pair // n_col) if flipped else (pair // n_col, pair % n_col)
        rows, lanes = (pl.ds(place * block, block) for place in at)
        high, low = halves(total_ref[pair].T if flipped else total_ref[pair])
        high_ref[rows, lanes] = high
        low_ref[rows, lanes] = low


def split(total, n_row, n_col, flipped, after):
    block = total.shape[-1]
    sizes = (n_col, n_row) if flipped else (n_row, n_col)
    shape = jax.ShapeDtypeStruct(tuple(size * block for size in sizes), jnp.bfloat16)
    whole = pl.BlockSpec(memory_space=VMEM)
    return pl.pallas_call(
        functools.partial(split_kernel, n_col, flipped),
        out_shape=[shape, shape],
        in_specs=[whole] + [pl.BlockSpec(memory_space=pl.ANY)] * len(after),
        out_specs=[whole, whole],
        compiler_params=pltpu.CompilerParams(vmem_limit_bytes=8 * MIB),
        cost_estimate=pl.CostEstimate(
            flops=3 * total.size, bytes_accessed=8 * total.size, transcendentals=0
        ),
        name="flip" if flipped else "split",
    )(total, *after)


def read(term, refs):
    number, place = term
    return refs[number][...] if place is None else refs[number][place]


def total_of(terms, refs):
    value = read(terms[0], refs)
    for term in terms[1:]:
        value += read(term, refs)
    return value


def write(ref, values):
    if len(ref.shape) == 2:
        ref[...] = values[0]
    else:
        for place, value in enumerate(values):
            ref[place] = value


class Operands:
    def __init__(self):
        self.arrays = []

    def term(self, piece):
        array, place = piece
        for number, known in enumerate(self.arrays):
            if known is array:
                return number, place
        self.arrays.append(array)
        return len(self.arrays) - 1, place


def couple_kernel(terms, span, high_ref, low_ref, *refs):
    n_in = 1 + max(number for number, _ in terms)
    ins, outs = refs[:n_in], refs[n_in:]
    block = ins[0].shape[-1]
    joined = jnp.concatenate([read(term, ins) for term in terms], axis=1)
    wanted = pl.ds(span[0] * block, (span[1] - span[0]) * block)
    result = product(halves(joined), (high_ref[:, wanted], low_ref[:, wanted]), False)
    pieces = [result[:, at : at + block] for at in range(0, result.shape[1], block)]
    each = len(pieces) // len(outs)
    for number, ref in enumerate(outs):
        write(ref, pieces[number * each : (number + 1) * each])


def couple(pieces, high, low, span, each):
    operands = Operands()
    terms = [operands.term(piece) for piece in pieces]
    rows, block = operands.arrays[0].shape[-2:]
    shape = (rows, block) if each == 1 else (each, rows, block)
    n_out = (span[1] - span[0]) // each
    whole = pl.BlockSpec(memory_space=VMEM)
    work = rows * block * block * len(terms) * (span[1] - span[0])
    return pl.pallas_call(
        functools.partial(couple_kernel, terms, span),
        out_shape=[jax.ShapeDtypeStruct(shape, jnp.float32)] * n_out,
        in_specs=[whole] * (2 + len(operands.arrays)),
        out_specs=[whole] * n_out,
        compiler_params=pltpu.CompilerParams(vmem_limit_bytes=16 * MIB),
        cost_estimate=pl.CostEstimate(
            flops=6 * work, bytes_accessed=4 * work // rows, transcendentals=0
        ),
        name="couple",
    )(high, low, *operands.arrays)


def first_solve_kernel(right_ref, inverse_ref, out_ref, right, inverse, arrived):
    fetches = [
        pltpu.make_async_copy(right_ref.at[0], right, arrived.at[0]),
        pltpu.make_async_copy(inverse_ref.at[0], inverse, arrived.at[1]),
    ]
    for fetch in fetches:
        fetch.start()
    for fetch in fetches:
        fetch.wait()
    out_ref[...] = product(halves(right[...]), halves(inverse[...]), False)


def first_solve(right, inverse):
    rows, block = right.shape[-2:]
    return pl.pallas_call(
        first_solve_kernel,
        out_shape=jax.ShapeDtypeStruct((rows, block), jnp.float32),
        in_specs=[pl.BlockSpec(memory_space=pl.ANY)] * 2,
        out_specs=pl.BlockSpec(memory_space=VMEM),
        scratch_shapes=[
            pltpu.VMEM((rows, block), jnp.float32),
            pltpu.VMEM((block, block), jnp.float32),
            pltpu.SemaphoreType.DMA((2,)),
        ],
        compiler_params=pltpu.CompilerParams(vmem_limit_bytes=60 * MIB),
        name="first_solve",
    )(right, inverse)


def solve_kernel(transposed, level, terms, n_ins, *refs):
    right_ref, inverse_ref = refs[:2]
    ins, out_ref = refs[2 : 2 + n_ins], refs[-1]
    value = right_ref[level] if len(right_ref.shape) == 3 else right_ref[...]
    if terms:
        value -= total_of(terms, ins)
    out_ref[...] = product(halves(value), halves(inverse_ref[level]), transposed)


def solve(right, inverse, level, pieces, transposed, after=()):
    rows, block = right.shape[-2:]
    operands = Operands()
    terms = [operands.term(piece) for piece in pieces]
    whole = pl.BlockSpec(memory_space=VMEM)
    return pl.pallas_call(
        functools.partial(solve_kernel, transposed, level, terms, len(operands.arrays)),
        out_shape=jax.ShapeDtypeStruct((rows, block), jnp.float32),
        in_specs=[whole] * (2 + len(operands.arrays))
        + [pl.BlockSpec(memory_space=pl.ANY)] * len(after),
        out_specs=whole,
        compiler_params=pltpu.CompilerParams(vmem_limit_bytes=8 * MIB),
        cost_estimate=pl.CostEstimate(
            flops=6 * rows * block * block, bytes_accessed=4 * block * block, transcendentals=0
        ),
        name="solve_up" if not transposed else "solve_down",
    )(right, inverse, *operands.arrays, *after)


def combine_kernel(sums, n_ins, *refs):
    ins, outs = refs[:n_ins], refs[-len(sums) :]
    for terms, ref in zip(sums, outs):
        write(ref, [total_of(entry, ins) for entry in terms])


def combine(sums, after=()):
    operands = Operands()
    sums = [[[operands.term(piece) for piece in entry] for entry in entries] for entries in sums]
    rows, block = operands.arrays[0].shape[-2:]
    whole = pl.BlockSpec(memory_space=VMEM)
    shapes = [(rows, block) if len(e) == 1 else (len(e), rows, block) for e in sums]
    return pl.pallas_call(
        functools.partial(combine_kernel, sums, len(operands.arrays)),
        out_shape=[jax.ShapeDtypeStruct(shape, jnp.float32) for shape in shapes],
        in_specs=[whole] * len(operands.arrays)
        + [pl.BlockSpec(memory_space=pl.ANY)] * len(after),
        out_specs=[whole] * len(sums),
        compiler_params=pltpu.CompilerParams(vmem_limit_bytes=8 * MIB),
        cost_estimate=pl.CostEstimate(
            flops=rows * block, bytes_accessed=4 * rows * block, transcendentals=0
        ),
        name="combine",
    )(*operands.arrays, *after)


def stack_kernel(n_ins, *refs):
    write(refs[-1], [ref[...] for ref in refs[:n_ins]])


def stack(segments, after=()):
    whole = pl.BlockSpec(memory_space=VMEM)
    shape = (len(segments),) + segments[0].shape
    return pl.pallas_call(
        functools.partial(stack_kernel, len(segments)),
        out_shape=jax.ShapeDtypeStruct(shape, jnp.float32),
        in_specs=[whole] * len(segments) + [pl.BlockSpec(memory_space=pl.ANY)] * len(after),
        out_specs=whole,
        compiler_params=pltpu.CompilerParams(vmem_limit_bytes=8 * MIB),
        name="stack",
    )(*segments, *after)


def far_exchange(segment, axis):
    size = lax.axis_size(axis)
    return lax.ppermute(segment, axis, [(i, i ^ (size // 2)) for i in range(size)])


def mirrored(number, size):
    bits = size.bit_length() - 1
    return sum(((number >> bit) & 1) << (bits - 1 - bit) for bit in range(bits))


def near_exchange(message, d):
    n_row, n_col = lax.axis_size("row"), lax.axis_size("col")
    half = n_row // 2
    pairs = []
    for row in range(n_row):
        for col in range(n_col):
            partner = row ^ (mirrored(d, half) if col % 2 else d)
            pairs.append((row * n_col + col, partner * n_col + col))
    return lax.ppermute(message, ("row", "col"), pairs)


def gather_row(segment, after):
    half = lax.axis_size("row") // 2
    last = half - 1
    received = far_exchange(segment, "row")
    (again,) = combine([[[(segment, None)]]], after)
    early = near_exchange(again, last)
    late = near_exchange(received, last)
    (both,) = combine([[[(segment, None)], [(received, None)]]], after)
    held = {d: near_exchange(both, d) for d in reversed(range(1, last))}
    held[0] = both
    pieces = [(held[d], side) for d in range(last) for side in range(2)]
    return pieces + [(early, None), (late, None)]


def deliver_row(messages):
    received = {d: near_exchange(messages[d], d) for d in reversed(range(1, len(messages)))}
    received = [messages[0]] + [received[d] for d in range(1, len(messages))]
    mine, other = combine(
        [
            [[(message, side) for message in [received[0], *reversed(received[1:])]]]
            for side in range(2)
        ]
    )
    return [(mine, None), (far_exchange(other, "row"), None)]


def exchange_each(messages, axis):
    size = lax.axis_size(axis)
    received = {0: messages[0]}
    for d in reversed(range(1, len(messages))):
        received[d] = lax.ppermute(messages[d], axis, [(i, i ^ d) for i in range(size)])
    return [received[d] for d in range(len(messages))]


def direct_shards(rhs, diag_inv, blocks, blk_target, blk_source, blk_count):
    levels = rhs.shape[0]
    n_row, n_col = lax.axis_size("row"), lax.axis_size("col")
    right = rhs.reshape((levels,) + rhs.shape[-2:])
    inverse = diag_inv.reshape((levels,) + diag_inv.shape[-2:])
    weights = blocks.reshape((levels - 1,) + blocks.shape[-3:])
    here = [lax.axis_index(axis).astype(jnp.int32) for axis in ("row", "col")]
    slots = jnp.concatenate(
        [blk_target.reshape(levels - 1, -1), blk_source.reshape(levels - 1, -1)]
        + [blk_count.reshape(levels - 1, 1)]
        + [jnp.full((levels - 1, 1), index) for index in here],
        axis=1,
    )
    gather = lambda level, after: gather_blocks(level, slots, weights, n_row, n_col, after)
    tidy = lambda level, flipped, after: split(totals[level], n_row, n_col, flipped, after)
    forward = [first_solve(right, inverse)]
    totals = [gather(0, ())]
    up, down = [], []
    for level in range(1, levels):
        solved = forward[-1:]
        up.append(tidy(level - 1, False, solved if level > 1 else ()))
        if level > 1:
            down.append(tidy(level - 2, True, solved))
        pieces = gather_row(forward[-1], [pair[0] for pair in up[-1:] + down[-1:]])
        far = couple(pieces, *up[-1], (n_col // 2, n_col), 1)
        near = couple(pieces, *up[-1], (0, n_col // 2), 1)
        if level < levels - 1:
            totals.append(gather(level, near[:1]))
            after = totals[-1:]
        else:
            down.append(tidy(level - 1, True, near[:1]))
            after = down[-1][:1]
        pieces = plain(reversed(exchange_each(near + far, "col")))
        forward.append(solve(right, inverse, level, pieces, False, after))
    backward = [None] * levels
    backward[-1] = solve(forward[-1], inverse, levels - 1, [], True)
    for level in range(levels - 2, -1, -1):
        pieces = plain(exchange_each([backward[level + 1]] * n_col, "col"))
        sent = couple(pieces, *down[level], (2, n_row), 2)
        kept = couple(pieces, *down[level], (0, 2), 2)
        if level == levels - 2:
            forward_out = stack(forward, kept[:1])
        pieces = deliver_row(kept + sent)
        after = (forward_out,) if level == levels - 2 else ()
        backward[level] = solve(forward[level], inverse, level, pieces, True, after)
    return forward_out.reshape(rhs.shape), stack(backward).reshape(rhs.shape)


def plain(messages):
    return [(message, None) for message in messages]


def fold_for(index, piece):
    entry_count = piece.shape[0]
    onehot = (index[:, None] == jnp.arange(entry_count, dtype=jnp.int32)[None, :]).astype(
        jnp.float32
    )
    return jnp.dot(
        onehot,
        piece.reshape(entry_count, -1),
        precision=HIGH_PRECISION,
        preferred_element_type=jnp.float32,
    )


def route_sum(index, entry_count, block_products, width):
    slot_count = block_products.shape[0]
    active_flags = jnp.arange(slot_count, dtype=jnp.int32) < entry_count
    routing_table = (
        (index[None, :] == jnp.arange(width, dtype=jnp.int32)[:, None]) & active_flags[None, :]
    ).astype(jnp.float32)
    return jnp.dot(
        routing_table,
        block_products.reshape(slot_count, -1),
        precision=HIGH_PRECISION,
        preferred_element_type=jnp.float32,
    )


def forward_level(previous, weight_matrix, target, source, entry_count):
    slot_count = weight_matrix.shape[0]
    slots, rhs_column_count, block_ordering = previous.shape
    selected_blocks = fold_for(source, lax.all_gather(previous, "row", axis=0, tiled=True))
    block_products = jnp.einsum(
        "ado,aon->adn",
        selected_blocks.reshape(slot_count, rhs_column_count, block_ordering),
        weight_matrix,
        precision=HIGH_PRECISION,
    )
    ncol = lax.axis_size("col")
    buckets = route_sum(target, entry_count, block_products, ncol * slots).reshape(
        ncol, slots, rhs_column_count, block_ordering
    )
    own = lax.psum_scatter(buckets, "col", scatter_dimension=0, tiled=True)[0]
    return own


def backward_level(upper, weight_matrix, target, source, entry_count):
    slot_count = weight_matrix.shape[0]
    slots, rhs_column_count, block_ordering = upper.shape
    selected_blocks = fold_for(target, lax.all_gather(upper, "col", axis=0, tiled=True))
    block_products = jnp.einsum(
        "mlv,mtv->mlt",
        selected_blocks.reshape(slot_count, rhs_column_count, block_ordering),
        weight_matrix,
        precision=HIGH_PRECISION,
    )
    nrow = lax.axis_size("row")
    buckets = route_sum(source, entry_count, block_products, nrow * slots).reshape(
        nrow, slots, rhs_column_count, block_ordering
    )
    own = lax.psum_scatter(buckets, "row", scatter_dimension=0, tiled=True)[0]
    return own


def shards(rhs, diag_inv, blocks, blk_target, blk_source, blk_count):
    levels = rhs.shape[0]
    right = rhs[:, 0, 0]
    inverse = diag_inv[:, 0, 0]
    weight_matrix = blocks[:, 0, 0]
    targets = blk_target[:, 0, 0]
    sources = blk_source[:, 0, 0]
    counts = blk_count[:, 0, 0]
    forward = [jnp.einsum("srb,sbc->src", right[0], inverse[0], precision=HIGH_PRECISION)]
    for level in range(1, levels):
        own = forward_level(
            forward[-1],
            weight_matrix[level - 1],
            targets[level - 1],
            sources[level - 1],
            counts[level - 1],
        )
        forward.append(
            jnp.einsum("srb,sbc->src", right[level] - own, inverse[level], precision=HIGH_PRECISION)
        )
    backward = [None] * levels
    backward[levels - 1] = jnp.einsum(
        "src,sbc->srb", forward[levels - 1], inverse[levels - 1], precision=HIGH_PRECISION
    )
    for level in range(levels - 2, -1, -1):
        own = backward_level(
            backward[level + 1], weight_matrix[level], targets[level], sources[level], counts[level]
        )
        backward[level] = jnp.einsum(
            "src,sbc->srb", forward[level] - own, inverse[level], precision=HIGH_PRECISION
        )
    forward_out = jnp.stack(forward)[:, None, None]
    backward_out = jnp.stack(backward)[:, None, None]
    return (forward_out, backward_out)


def solution(mesh):
    placed = (
        P(None, "row", "col", None, None, None),
        P(None, "row", "col", None, None, None),
        P(None, "row", "col", None, None, None),
        P(None, "row", "col", None),
        P(None, "row", "col", None),
        P(None, "row", "col"),
    )
    n_row, n_col = mesh.shape["row"], mesh.shape["col"]

    def local(rhs, diag_inv, blocks, blk_target, blk_source, blk_count):
        sizes = (n_row, n_col)
        dense = n_row * n_col <= blocks.shape[3] and rhs.shape[3] == 1
        even = n_row > 2 and n_col > 1 and all(size & (size - 1) == 0 for size in sizes)
        run = direct_shards if dense and even else shards
        return run(rhs, diag_inv, blocks, blk_target, blk_source, blk_count)

    return jax.shard_map(
        local,
        mesh=mesh,
        in_specs=placed,
        out_specs=(
            P(None, "row", "col", None, None, None),
            P(None, "row", "col", None, None, None),
        ),
        check_vma=False,
    )
```

```python
import functools

import jax
import jax.numpy as jnp
from jax import lax
from jax.experimental import pallas as pl
from jax.experimental.pallas import tpu as pltpu
from jax.sharding import PartitionSpec as P

HIGH_PRECISION = lax.Precision.HIGHEST
MIB = 1024 * 1024
VMEM = pltpu.MemorySpace.VMEM
SMEM = pltpu.MemorySpace.SMEM


def halves(value):
    high = value.astype(jnp.bfloat16)
    low = (value - high.astype(jnp.float32)).astype(jnp.bfloat16)
    return high, low


def product(left, right, transposed):
    contract = (((1,), (1 if transposed else 0,)), ((), ()))
    dot = functools.partial(
        lax.dot_general, dimension_numbers=contract, preferred_element_type=jnp.float32
    )
    return dot(left[0], right[0]) + (dot(left[0], right[1]) + dot(left[1], right[0]))


def gather_blocks_kernel(
    n_row, n_col, level, chunk, slots_ref, blocks_ref, *refs
):
    total, slots, arrived = refs[-3:]
    slot_count = slots.shape[0]
    count, row, col = (slots_ref[level, 2 * slot_count + place] for place in range(3))
    half = n_row // 2
    side = row // half

    def fetch(number):
        span = pl.ds(number * chunk, chunk)
        return pltpu.make_async_copy(
            blocks_ref.at[level, span], slots.at[span], arrived.at[number]
        )

    for number in range(arrived.shape[0]):
        pl.when(number * chunk < count)(fetch(number).start)
    total[...] = jnp.zeros_like(total)

    def add(slot, carry):
        pl.when(lax.rem(slot, chunk) == 0)(fetch(slot // chunk).wait)
        source = slots_ref[level, slot_count + slot]
        near = lax.rem(source, half) ^ lax.rem(row, half)
        near = jnp.where(lax.rem(col, 2) == 1, mirrored(near, half), near)
        below = near * 2 + ((source // half) ^ side)
        above = slots_ref[level, slot] ^ col
        total[below * n_col + above] += slots[slot]
        return carry

    lax.fori_loop(0, count, add, 0)


def gather_blocks(level, slots, blocks, n_row, n_col, after):
    slot_count, block = blocks.shape[1], blocks.shape[2]
    chunk = max(1, slot_count // 4)
    shape = (n_row * n_col, block, block)
    scalars = pl.BlockSpec(memory_space=SMEM)
    return pl.pallas_call(
        functools.partial(gather_blocks_kernel, n_row, n_col, level, chunk),
        out_shape=jax.ShapeDtypeStruct(shape, jnp.float32),
        in_specs=[scalars] + [pl.BlockSpec(memory_space=pl.ANY)] * (1 + len(after)),
        out_specs=pl.BlockSpec(memory_space=VMEM),
        scratch_shapes=[
            pltpu.VMEM((slot_count, block, block), jnp.float32),
            pltpu.SemaphoreType.DMA((slot_count // chunk,)),
        ],
        compiler_params=pltpu.CompilerParams(vmem_limit_bytes=(51 if level == 0 else 16) * MIB),
        cost_estimate=pl.CostEstimate(
            flops=slot_count * block * block,
            bytes_accessed=8 * slot_count * block * block,
            transcendentals=0,
        ),
        name=f"gather_blocks_{level}",
    )(slots, blocks, *after)


def split_kernel(n_col, flipped, total_ref, *refs):
    high_ref, low_ref = refs[-2:]
    block = total_ref.shape[-1]
    for pair in range(total_ref.shape[0]):
        at = (pair % n_col, pair // n_col) if flipped else (pair // n_col, pair % n_col)
        rows, lanes = (pl.ds(place * block, block) for place in at)
        high, low = halves(total_ref[pair].T if flipped else total_ref[pair])
        high_ref[rows, lanes] = high
        low_ref[rows, lanes] = low


def split(total, n_row, n_col, flipped, after):
    block = total.shape[-1]
    sizes = (n_col, n_row) if flipped else (n_row, n_col)
    shape = jax.ShapeDtypeStruct(tuple(size * block for size in sizes), jnp.bfloat16)
    whole = pl.BlockSpec(memory_space=VMEM)
    return pl.pallas_call(
        functools.partial(split_kernel, n_col, flipped),
        out_shape=[shape, shape],
        in_specs=[whole] + [pl.BlockSpec(memory_space=pl.ANY)] * len(after),
        out_specs=[whole, whole],
        compiler_params=pltpu.CompilerParams(vmem_limit_bytes=8 * MIB),
        cost_estimate=pl.CostEstimate(
            flops=3 * total.size, bytes_accessed=8 * total.size, transcendentals=0
        ),
        name="flip" if flipped else "split",
    )(total, *after)


def read(term, refs):
    number, place = term
    return refs[number][...] if place is None else refs[number][place]


def total_of(terms, refs):
    value = read(terms[0], refs)
    for term in terms[1:]:
        value += read(term, refs)
    return value


def write(ref, values):
    if len(ref.shape) == 2:
        ref[...] = values[0]
    else:
        for place, value in enumerate(values):
            ref[place] = value


class Operands:
    def __init__(self):
        self.arrays = []

    def term(self, piece):
        array, place = piece
        for number, known in enumerate(self.arrays):
            if known is array:
                return number, place
        self.arrays.append(array)
        return len(self.arrays) - 1, place


def couple_kernel(terms, span, high_ref, low_ref, *refs):
    n_in = 1 + max(number for number, _ in terms)
    ins, outs = refs[:n_in], refs[n_in:]
    block = ins[0].shape[-1]
    joined = jnp.concatenate([read(term, ins) for term in terms], axis=1)
    wanted = pl.ds(span[0] * block, (span[1] - span[0]) * block)
    result = product(halves(joined), (high_ref[:, wanted], low_ref[:, wanted]), False)
    pieces = [result[:, at : at + block] for at in range(0, result.shape[1], block)]
    each = len(pieces) // len(outs)
    for number, ref in enumerate(outs):
        write(ref, pieces[number * each : (number + 1) * each])


def couple(pieces, high, low, span, each):
    operands = Operands()
    terms = [operands.term(piece) for piece in pieces]
    rows, block = operands.arrays[0].shape[-2:]
    shape = (rows, block) if each == 1 else (each, rows, block)
    n_out = (span[1] - span[0]) // each
    whole = pl.BlockSpec(memory_space=VMEM)
    work = rows * block * block * len(terms) * (span[1] - span[0])
    return pl.pallas_call(
        functools.partial(couple_kernel, terms, span),
        out_shape=[jax.ShapeDtypeStruct(shape, jnp.float32)] * n_out,
        in_specs=[whole] * (2 + len(operands.arrays)),
        out_specs=[whole] * n_out,
        compiler_params=pltpu.CompilerParams(vmem_limit_bytes=16 * MIB),
        cost_estimate=pl.CostEstimate(
            flops=6 * work, bytes_accessed=4 * work // rows, transcendentals=0
        ),
        name="couple",
    )(high, low, *operands.arrays)


def first_solve_kernel(right_ref, inverse_ref, out_ref, right, inverse, arrived):
    fetches = [
        pltpu.make_async_copy(right_ref.at[0], right, arrived.at[0]),
        pltpu.make_async_copy(inverse_ref.at[0], inverse, arrived.at[1]),
    ]
    for fetch in fetches:
        fetch.start()
    for fetch in fetches:
        fetch.wait()
    out_ref[...] = product(halves(right[...]), halves(inverse[...]), False)


def first_solve(right, inverse):
    rows, block = right.shape[-2:]
    return pl.pallas_call(
        first_solve_kernel,
        out_shape=jax.ShapeDtypeStruct((rows, block), jnp.float32),
        in_specs=[pl.BlockSpec(memory_space=pl.ANY)] * 2,
        out_specs=pl.BlockSpec(memory_space=VMEM),
        scratch_shapes=[
            pltpu.VMEM((rows, block), jnp.float32),
            pltpu.VMEM((block, block), jnp.float32),
            pltpu.SemaphoreType.DMA((2,)),
        ],
        compiler_params=pltpu.CompilerParams(vmem_limit_bytes=60 * MIB),
        name="first_solve",
    )(right, inverse)


def solve_kernel(transposed, level, terms, n_ins, *refs):
    right_ref, inverse_ref = refs[:2]
    ins, out_ref = refs[2 : 2 + n_ins], refs[-1]
    value = right_ref[level] if len(right_ref.shape) == 3 else right_ref[...]
    if terms:
        value -= total_of(terms, ins)
    out_ref[...] = product(halves(value), halves(inverse_ref[level]), transposed)


def solve(right, inverse, level, pieces, transposed, after=()):
    rows, block = right.shape[-2:]
    operands = Operands()
    terms = [operands.term(piece) for piece in pieces]
    whole = pl.BlockSpec(memory_space=VMEM)
    return pl.pallas_call(
        functools.partial(solve_kernel, transposed, level, terms, len(operands.arrays)),
        out_shape=jax.ShapeDtypeStruct((rows, block), jnp.float32),
        in_specs=[whole] * (2 + len(operands.arrays))
        + [pl.BlockSpec(memory_space=pl.ANY)] * len(after),
        out_specs=whole,
        compiler_params=pltpu.CompilerParams(vmem_limit_bytes=8 * MIB),
        cost_estimate=pl.CostEstimate(
            flops=6 * rows * block * block, bytes_accessed=4 * block * block, transcendentals=0
        ),
        name="solve_up" if not transposed else "solve_down",
    )(right, inverse, *operands.arrays, *after)


def combine_kernel(sums, n_ins, *refs):
    ins, outs = refs[:n_ins], refs[-len(sums) :]
    for terms, ref in zip(sums, outs):
        write(ref, [total_of(entry, ins) for entry in terms])


def combine(sums, after=()):
    operands = Operands()
    sums = [[[operands.term(piece) for piece in entry] for entry in entries] for entries in sums]
    rows, block = operands.arrays[0].shape[-2:]
    whole = pl.BlockSpec(memory_space=VMEM)
    shapes = [(rows, block) if len(e) == 1 else (len(e), rows, block) for e in sums]
    return pl.pallas_call(
        functools.partial(combine_kernel, sums, len(operands.arrays)),
        out_shape=[jax.ShapeDtypeStruct(shape, jnp.float32) for shape in shapes],
        in_specs=[whole] * len(operands.arrays)
        + [pl.BlockSpec(memory_space=pl.ANY)] * len(after),
        out_specs=[whole] * len(sums),
        compiler_params=pltpu.CompilerParams(vmem_limit_bytes=8 * MIB),
        cost_estimate=pl.CostEstimate(
            flops=rows * block, bytes_accessed=4 * rows * block, transcendentals=0
        ),
        name="combine",
    )(*operands.arrays, *after)


def last_solve_kernel(terms, n_ins, right_ref, inverse_ref, *refs):
    ins, others, out_ref = refs[:n_ins], refs[n_ins:-1], refs[-1]
    for level, other_ref in enumerate(others):
        out_ref[level + 1] = other_ref[...]
    value = right_ref[...] - total_of(terms, ins)
    out_ref[0] = product(halves(value), halves(inverse_ref[0]), True)


def last_solve(right, inverse, pieces, others):
    operands = Operands()
    terms = [operands.term(piece) for piece in pieces]
    whole = pl.BlockSpec(memory_space=VMEM)
    shape = (len(others) + 1,) + right.shape
    return pl.pallas_call(
        functools.partial(last_solve_kernel, terms, len(operands.arrays)),
        out_shape=jax.ShapeDtypeStruct(shape, jnp.float32),
        in_specs=[whole] * (2 + len(operands.arrays) + len(others)),
        out_specs=whole,
        compiler_params=pltpu.CompilerParams(vmem_limit_bytes=8 * MIB),
        name="last_solve",
    )(right, inverse, *operands.arrays, *others)


def stack_kernel(n_ins, *refs):
    write(refs[-1], [ref[...] for ref in refs[:n_ins]])


def stack(segments, after=()):
    whole = pl.BlockSpec(memory_space=VMEM)
    shape = (len(segments),) + segments[0].shape
    return pl.pallas_call(
        functools.partial(stack_kernel, len(segments)),
        out_shape=jax.ShapeDtypeStruct(shape, jnp.float32),
        in_specs=[whole] * len(segments) + [pl.BlockSpec(memory_space=pl.ANY)] * len(after),
        out_specs=whole,
        compiler_params=pltpu.CompilerParams(vmem_limit_bytes=8 * MIB),
        name="stack",
    )(*segments, *after)


def far_exchange(segment, axis):
    size = lax.axis_size(axis)
    return lax.ppermute(segment, axis, [(i, i ^ (size // 2)) for i in range(size)])


def mirrored(number, size):
    bits = size.bit_length() - 1
    return sum(((number >> bit) & 1) << (bits - 1 - bit) for bit in range(bits))


def near_exchange(messages):
    n_row, n_col = lax.axis_size("row"), lax.axis_size("col")
    half = n_row // 2
    received = {0: messages[0]}
    for d in reversed(range(1, half)):
        pairs = []
        for row in range(n_row):
            for col in range(n_col):
                partner = row ^ (mirrored(d, half) if col % 2 else d)
                pairs.append((row * n_col + col, partner * n_col + col))
        received[d] = lax.ppermute(messages[d], ("row", "col"), pairs)
    return [received[d] for d in range(half)]


def gather_row(segment, after):
    half = lax.axis_size("row") // 2
    received = far_exchange(segment, "row")
    (both,) = combine([[[(segment, None)], [(received, None)]]], after)
    messages = near_exchange([both] * half)
    return [(message, side) for message in messages for side in range(2)]


def deliver_row(messages):
    received = near_exchange(messages)
    mine, other = combine(
        [
            [[(message, side) for message in [received[0], *reversed(received[1:])]]]
            for side in range(2)
        ]
    )
    return [(mine, None), (far_exchange(other, "row"), None)]


def exchange_each(messages, axis):
    size = lax.axis_size(axis)
    received = {0: messages[0]}
    for d in reversed(range(1, len(messages))):
        received[d] = lax.ppermute(messages[d], axis, [(i, i ^ d) for i in range(size)])
    return [received[d] for d in range(len(messages))]


def direct_shards(rhs, diag_inv, blocks, blk_target, blk_source, blk_count):
    levels = rhs.shape[0]
    n_row, n_col = lax.axis_size("row"), lax.axis_size("col")
    right = rhs.reshape((levels,) + rhs.shape[-2:])
    inverse = diag_inv.reshape((levels,) + diag_inv.shape[-2:])
    weights = blocks.reshape((levels - 1,) + blocks.shape[-3:])
    here = [lax.axis_index(axis).astype(jnp.int32) for axis in ("row", "col")]
    slots = jnp.concatenate(
        [blk_target.reshape(levels - 1, -1), blk_source.reshape(levels - 1, -1)]
        + [blk_count.reshape(levels - 1, 1)]
        + [jnp.full((levels - 1, 1), index) for index in here],
        axis=1,
    )
    gather = lambda level, after: gather_blocks(level, slots, weights, n_row, n_col, after)
    tidy = lambda level, flipped, after: split(totals[level], n_row, n_col, flipped, after)
    forward = [first_solve(right, inverse)]
    totals = [gather(0, ())]
    up, down = [], []
    for level in range(1, levels):
        solved = forward[-1:]
        up.append(tidy(level - 1, False, solved if level > 1 else ()))
        if level > 1:
            down.append(tidy(level - 2, True, solved))
        pieces = gather_row(forward[-1], [pair[0] for pair in up[-1:] + down[-1:]])
        far = couple(pieces, *up[-1], (n_col // 2, n_col), 1)
        near = couple(pieces, *up[-1], (0, n_col // 2), 1)
        if level < levels - 1:
            totals.append(gather(level, near[:1]))
            after = totals[-1:]
        else:
            down.append(tidy(level - 1, True, near[:1]))
            after = down[-1][:1]
        pieces = plain(reversed(exchange_each(near + far, "col")))
        forward.append(solve(right, inverse, level, pieces, False, after))
    backward = [None] * levels
    backward[-1] = solve(forward[-1], inverse, levels - 1, [], True)
    for level in range(levels - 2, -1, -1):
        pieces = plain(exchange_each([backward[level + 1]] * n_col, "col"))
        sent = couple(pieces, *down[level], (2, n_row), 2)
        kept = couple(pieces, *down[level], (0, 2), 2)
        if level == levels - 2:
            forward_out = stack(forward, kept[:1])
        pieces = deliver_row(kept + sent)
        after = (forward_out,) if level == levels - 2 else ()
        if level == 0:
            backward_out = last_solve(forward[0], inverse, pieces, backward[1:])
            break
        backward[level] = solve(forward[level], inverse, level, pieces, True, after)
    return forward_out.reshape(rhs.shape), backward_out.reshape(rhs.shape)


def plain(messages):
    return [(message, None) for message in messages]


def fold_for(index, piece):
    entry_count = piece.shape[0]
    onehot = (index[:, None] == jnp.arange(entry_count, dtype=jnp.int32)[None, :]).astype(
        jnp.float32
    )
    return jnp.dot(
        onehot,
        piece.reshape(entry_count, -1),
        precision=HIGH_PRECISION,
        preferred_element_type=jnp.float32,
    )


def route_sum(index, entry_count, block_products, width):
    slot_count = block_products.shape[0]
    active_flags = jnp.arange(slot_count, dtype=jnp.int32) < entry_count
    routing_table = (
        (index[None, :] == jnp.arange(width, dtype=jnp.int32)[:, None]) & active_flags[None, :]
    ).astype(jnp.float32)
    return jnp.dot(
        routing_table,
        block_products.reshape(slot_count, -1),
        precision=HIGH_PRECISION,
        preferred_element_type=jnp.float32,
    )


def forward_level(previous, weight_matrix, target, source, entry_count):
    slot_count = weight_matrix.shape[0]
    slots, rhs_column_count, block_ordering = previous.shape
    selected_blocks = fold_for(source, lax.all_gather(previous, "row", axis=0, tiled=True))
    block_products = jnp.einsum(
        "ado,aon->adn",
        selected_blocks.reshape(slot_count, rhs_column_count, block_ordering),
        weight_matrix,
        precision=HIGH_PRECISION,
    )
    ncol = lax.axis_size("col")
    buckets = route_sum(target, entry_count, block_products, ncol * slots).reshape(
        ncol, slots, rhs_column_count, block_ordering
    )
    own = lax.psum_scatter(buckets, "col", scatter_dimension=0, tiled=True)[0]
    return own


def backward_level(upper, weight_matrix, target, source, entry_count):
    slot_count = weight_matrix.shape[0]
    slots, rhs_column_count, block_ordering = upper.shape
    selected_blocks = fold_for(target, lax.all_gather(upper, "col", axis=0, tiled=True))
    block_products = jnp.einsum(
        "mlv,mtv->mlt",
        selected_blocks.reshape(slot_count, rhs_column_count, block_ordering),
        weight_matrix,
        precision=HIGH_PRECISION,
    )
    nrow = lax.axis_size("row")
    buckets = route_sum(source, entry_count, block_products, nrow * slots).reshape(
        nrow, slots, rhs_column_count, block_ordering
    )
    own = lax.psum_scatter(buckets, "row", scatter_dimension=0, tiled=True)[0]
    return own


def shards(rhs, diag_inv, blocks, blk_target, blk_source, blk_count):
    levels = rhs.shape[0]
    right = rhs[:, 0, 0]
    inverse = diag_inv[:, 0, 0]
    weight_matrix = blocks[:, 0, 0]
    targets = blk_target[:, 0, 0]
    sources = blk_source[:, 0, 0]
    counts = blk_count[:, 0, 0]
    forward = [jnp.einsum("srb,sbc->src", right[0], inverse[0], precision=HIGH_PRECISION)]
    for level in range(1, levels):
        own = forward_level(
            forward[-1],
            weight_matrix[level - 1],
            targets[level - 1],
            sources[level - 1],
            counts[level - 1],
        )
        forward.append(
            jnp.einsum("srb,sbc->src", right[level] - own, inverse[level], precision=HIGH_PRECISION)
        )
    backward = [None] * levels
    backward[levels - 1] = jnp.einsum(
        "src,sbc->srb", forward[levels - 1], inverse[levels - 1], precision=HIGH_PRECISION
    )
    for level in range(levels - 2, -1, -1):
        own = backward_level(
            backward[level + 1], weight_matrix[level], targets[level], sources[level], counts[level]
        )
        backward[level] = jnp.einsum(
            "src,sbc->srb", forward[level] - own, inverse[level], precision=HIGH_PRECISION
        )
    forward_out = jnp.stack(forward)[:, None, None]
    backward_out = jnp.stack(backward)[:, None, None]
    return (forward_out, backward_out)


def solution(mesh):
    placed = (
        P(None, "row", "col", None, None, None),
        P(None, "row", "col", None, None, None),
        P(None, "row", "col", None, None, None),
        P(None, "row", "col", None),
        P(None, "row", "col", None),
        P(None, "row", "col"),
    )
    n_row, n_col = mesh.shape["row"], mesh.shape["col"]

    def local(rhs, diag_inv, blocks, blk_target, blk_source, blk_count):
        sizes = (n_row, n_col)
        dense = n_row * n_col <= blocks.shape[3] and rhs.shape[3] == 1
        even = all(size > 1 and size & (size - 1) == 0 for size in sizes)
        run = direct_shards if dense and even else shards
        return run(rhs, diag_inv, blocks, blk_target, blk_source, blk_count)

    return jax.shard_map(
        local,
        mesh=mesh,
        in_specs=placed,
        out_specs=(
            P(None, "row", "col", None, None, None),
            P(None, "row", "col", None, None, None),
        ),
        check_vma=False,
    )
```
